128 devices in a mesh: row: 16 (over x, z), col: 8 (over y, core).
Axes of the slice: x: 4, y: 4, z: 4, core: 2. Of those that a mesh axis runs over, the one named last changes fastest.
Arguments:
- fine_input: bfloat16 [1024, 1024, 128], P('row', 'col'), may hold values from -6 to 6
- interp_weights: bfloat16 [1024, 1024, 128], P('row', 'col'), may hold values from -0.5 to 0.5
- intersection_ids: int32 [16, 8, 16], P('row', 'col'), may hold values from 0 to 4095, as said below
- live_counts: int32 [16, 8], P('row', 'col'), may hold values from 10 to 16
- coarse_state: bfloat16 [32768, 100], P('row'), may hold values from -6 to 6
- cond_weight: bfloat16 [100, 128], replicated, may hold values from -0.625 to 0.625
- conv_one: bfloat16 [3, 3, 128, 128], replicated, may hold values from -0.1875 to 0.1875
- conv_two: bfloat16 [3, 3, 128, 128], replicated, may hold values from -0.1875 to 0.1875
- cot_one: bfloat16 [1024, 1024, 128], P('row', 'col'), may hold values from -6 to 6
- cot_two: bfloat16 [512, 512, 128], P('row', 'col'), may hold values from -6 to 6
Outputs:
- skip_two: bfloat16 [512, 512, 128], P('row', 'col')
- grad_input: bfloat16 [1024, 1024, 128], P('row', 'col')
- grad_conv_one: float32 [3, 3, 128, 128], replicated
- grad_conv_two: float32 [3, 3, 128, 128], replicated
- grad_cond: float32 [100, 128], replicated
- grad_coarse: float32 [32768, 100], P('row')
The draws below stay inside these ranges and needn't reach their ends.
Inputs may be any that keep to these rules, and one draw needn't show every extreme that they name: `intersection_ids`: block ids; block b lies on coarse shard b // 256. At most 2 of the 16 entries of one tile name blocks of one shard, and some shard is named 2 times by every tile; a block may be listed more than once.
All inputs are finite; a program needn't handle non-finite values.
Results may differ from the reference program's by a relative error of at most 0.015.
Values may be sent and summed in bfloat16 or wider, within the bound.
A program may use at most 128 MiB of HBM per device.

```python
import jax
import jax.numpy as jnp
from jax import lax

C = 128
CCH = 100
CB = 8
NOV = 16
CAP = 2
TH = 64
TW = 128
BPD = 256
GR = 16
GC = 8
NH = 1024
NW = 1024
J = 128
NBLK = 4096
COARSE = 32768


def single_tile(tile_key):
    first_key, second_key, third_key, fourth_key = jax.random.split(tile_key, 4)
    owner_order = jax.random.permutation(first_key, GR)
    others = jax.random.permutation(second_key, (GR - 1) * CAP)[:NOV - CAP] + CAP
    positions = jnp.concatenate([jnp.arange(CAP), others])
    slot_order = jax.random.permutation(third_key, NOV)
    positions = positions[slot_order]
    owner_shard = owner_order[positions // CAP]
    local_block = jax.random.randint(fourth_key, (NOV,), 0, BPD)
    return (owner_shard * BPD + local_block).astype(jnp.int32)


def draw_intersection_ids(key, part):
    key = jax.random.fold_in(key, 11)
    tile_keys = jax.random.split(key, GR * GC)
    return jax.vmap(single_tile)(tile_keys).reshape(GR, GC, NOV)


def draw_live_counts(key, part):
    key = jax.random.fold_in(key, 23)
    counts = jax.random.randint(key, (GR, GC), NOV * 5 // 8, NOV + 1)
    return counts.at[0, 0].set(NOV).astype(jnp.int32)


def shard_levels(key, shape, pieces, smallest, high):
    def one(axis_at, parts):
        steps = jax.random.uniform(jax.random.fold_in(jax.random.fold_in(key, 6), axis_at), (parts,), jnp.float32, smallest / len(pieces), high / len(pieces))
        return jnp.repeat(jnp.exp(steps), shape[axis_at] // parts).reshape((-1,) + (1,) * (len(shape) - axis_at - 1))

    level = one(*pieces[0])
    for cut in pieces[1:]:
        level = level * one(*cut)
    return level


def centred(stream_key, dims, spread, limit, shards=(), dtype=jnp.bfloat16):
    loudness = shard_levels(stream_key, dims, shards, -0.22, 0.18) if shards else 1.0
    array = jax.random.normal(stream_key, dims, jnp.float32) * spread * loudness
    return jnp.minimum(jnp.maximum(array, -limit), limit).astype(dtype)


def setup_inputs(seed: int = 0) -> dict:
    key_list = jax.random.split(jax.random.key(seed), 11)
    fine_input = centred(key_list[0], (NH, NW, C), 1.0, 6.0, ((0, 16), (1, 8)))
    interp_weights = centred(key_list[1], (NH, NW, J), J ** -0.5, 0.5, ((0, 16), (1, 8)))
    intersection_ids = draw_intersection_ids(jax.random.fold_in(key_list[10], 71), 0)
    live_counts = draw_live_counts(jax.random.fold_in(key_list[10], 71), 0)
    coarse_state = centred(key_list[4], (COARSE, CCH), 1.0, 6.0, ((0, 16),))
    cond_weight = centred(key_list[5], (CCH, C), CCH ** -0.5, 0.625)
    conv_one = centred(key_list[6], (3, 3, C, C), (9 * C) ** -0.5, 0.1875)
    conv_two = centred(key_list[7], (3, 3, C, C), (9 * C) ** -0.5, 0.1875)
    cot_one = centred(key_list[8], (NH, NW, C), 1.0, 6.0, ((0, 16), (1, 8)))
    cot_two = centred(key_list[9], (NH // 2, NW // 2, C), 1.0, 6.0, ((0, 16), (1, 8)))
    return dict(fine_input=fine_input, interp_weights=interp_weights, intersection_ids=intersection_ids, live_counts=live_counts, coarse_state=coarse_state, cond_weight=cond_weight, conv_one=conv_one, conv_two=conv_two, cot_one=cot_one, cot_two=cot_two)


def silu_slope(field):
    sig = jax.nn.sigmoid(field)
    return sig * (1.0 + field * (1.0 - sig))

def tap_conv(field, weight):
    height, breadth, channels = field.shape
    padded = jnp.pad(field, ((1, 1), (1, 1), (0, 0)))
    running = jnp.zeros((height * breadth, weight.shape[3]), jnp.float32)
    for row_tap in range(3):
        for col_tap in range(3):
            window = padded[row_tap:row_tap + height, col_tap:col_tap + breadth].reshape(-1, channels)
            running = running + jnp.dot(window, weight[row_tap, col_tap], preferred_element_type=jnp.float32)
    return (running.reshape(height, breadth, -1), padded)

def tap_transposed(delta, weight):
    height, breadth, channels = delta.shape
    padded = jnp.pad(delta, ((1, 1), (1, 1), (0, 0)))
    running = jnp.zeros((height * breadth, weight.shape[2]), jnp.float32)
    for row_tap in range(3):
        for col_tap in range(3):
            window = padded[2 - row_tap:2 - row_tap + height, 2 - col_tap:2 - col_tap + breadth].reshape(-1, channels)
            running = running + jnp.dot(window, weight[row_tap, col_tap].T, preferred_element_type=jnp.float32)
    return running.reshape(height, breadth, -1)

def tap_grad(padded, delta):
    height, breadth, channels = delta.shape
    flat_delta = delta.reshape(-1, channels)
    tap_rows = []
    for row_tap in range(3):
        tap_line = []
        for col_tap in range(3):
            window = padded[row_tap:row_tap + height, col_tap:col_tap + breadth].reshape(-1, padded.shape[2])
            tap_line.append(jnp.dot(window.T, flat_delta, preferred_element_type=jnp.float32))
        tap_rows.append(jnp.stack(tap_line))
    return jnp.stack(tap_rows)

def pool_pairs(field):
    height, breadth, channels = field.shape
    grouped = field.astype(jnp.float32).reshape(height // 2, 2, breadth // 2, 2, channels)
    return (lax.optimization_barrier(jnp.sum(grouped, axis=(1, 3))) * 0.25).astype(jnp.bfloat16)

def spread_pairs(field):
    return jnp.repeat(jnp.repeat(field, 2, axis=0), 2, axis=1) * 0.25

def reference(fine_input, interp_weights, intersection_ids, live_counts, coarse_state, cond_weight, conv_one, conv_two, cot_one, cot_two):
    highest = lax.Precision.HIGHEST
    tiles = GR * GC
    stored = coarse_state.reshape(NBLK, CB, CCH)
    listed_ids = intersection_ids.reshape(tiles, NOV).astype(jnp.int32)
    live_slot = jnp.arange(NOV)[None, :] < live_counts.reshape(tiles)[:, None]
    patches = jnp.where(live_slot[:, :, None, None], stored[listed_ids], jnp.zeros((), jnp.bfloat16))
    patches = patches.reshape(tiles, J, CCH)
    projected = jnp.einsum('tjd,de->tje', patches.astype(jnp.float32), cond_weight.astype(jnp.float32), precision=highest).astype(jnp.bfloat16)
    interp_tiles = interp_weights.reshape(GR, TH, GC, TW, J).transpose(0, 2, 1, 3, 4).reshape(tiles, TH * TW, J)
    condition = jnp.einsum('tnj,tjc->tnc', interp_tiles.astype(jnp.float32), projected.astype(jnp.float32), precision=highest)
    condition = condition.reshape(GR, GC, TH, TW, C).transpose(0, 2, 1, 3, 4).reshape(NH, NW, C)
    level_one_in = (fine_input.astype(jnp.float32) + condition).astype(jnp.bfloat16)
    z_one, pad_one = tap_conv(level_one_in, conv_one)
    y_one = jax.nn.silu(z_one).astype(jnp.bfloat16)
    level_two_in = pool_pairs(y_one)
    z_two, pad_two = tap_conv(level_two_in, conv_two)
    skip_two = jax.nn.silu(z_two).astype(jnp.bfloat16)
    delta_two = (cot_two.astype(jnp.float32) * silu_slope(z_two)).astype(jnp.bfloat16)
    grad_conv_two = tap_grad(pad_two, delta_two)
    back_two = tap_transposed(delta_two, conv_two)
    delta_one = ((cot_one.astype(jnp.float32) + spread_pairs(back_two)) * silu_slope(z_one)).astype(jnp.bfloat16)
    grad_conv_one = tap_grad(pad_one, delta_one)
    grad_input = tap_transposed(delta_one, conv_one).astype(jnp.bfloat16)
    grad_tiles = grad_input.reshape(GR, TH, GC, TW, C).transpose(0, 2, 1, 3, 4).reshape(tiles, TH * TW, C)
    grad_projected = jnp.einsum('tnj,tnc->tjc', interp_tiles.astype(jnp.float32), grad_tiles.astype(jnp.float32), precision=highest).astype(jnp.bfloat16)
    row_live = jnp.repeat(live_slot, CB, axis=1)
    grad_projected = jnp.where(row_live[:, :, None], grad_projected, jnp.zeros((), jnp.bfloat16))
    grad_cond = jnp.einsum('tjd,tjc->dc', patches.astype(jnp.float32), grad_projected.astype(jnp.float32), precision=highest)
    grad_patch = jnp.einsum('tjc,dc->tjd', grad_projected.astype(jnp.float32), cond_weight.astype(jnp.float32), precision=highest)
    grad_coarse = jnp.zeros((NBLK, CB, CCH), jnp.float32).at[listed_ids.reshape(-1)].add(grad_patch.reshape(tiles * NOV, CB, CCH))
    grad_coarse = grad_coarse.reshape(COARSE, CCH)
    return (skip_two, grad_input, grad_conv_one, grad_conv_two, grad_cond, grad_coarse)
```

```python
import functools

import jax
import jax.numpy as jnp
from jax import lax
from jax.experimental import pallas as pl
from jax.experimental.pallas import tpu as pltpu
from jax.sharding import PartitionSpec as P

MESH = pl.DeviceIdType.MESH
BF = jnp.bfloat16
F32 = jnp.float32
CB = 8
CAP = 2
SLOT = CAP * CB
CONTRACT0 = (((0,), (0,)), ((), ()))
CONTRACT1 = (((1,), (1,)), ((), ()))


def dot(left, right):
    return jnp.dot(left, right, preferred_element_type=F32)


def iota(shape, dim):
    return lax.broadcasted_iota(jnp.int32, shape, dim)


class Push:
    def __init__(self, coords, axis, count, source, target, send, recv):
        self.coords, self.axis, self.count = coords, axis, count
        self.source, self.target, self.send, self.recv = source, target, send, recv
        self.me = coords[axis]

    def device(self, index):
        return (index, self.coords[1]) if self.axis == 0 else (self.coords[0], index)

    def copy(self, step, slot):
        peer = lax.rem(self.me + step, self.count)
        return pltpu.make_async_remote_copy(
            src_ref=self.source(peer),
            dst_ref=self.target.at[slot],
            send_sem=self.send.at[step],
            recv_sem=self.recv.at[step],
            device_id=self.device(peer),
            device_id_type=MESH,
        )

    def each(self, act):
        def body(step, carry):
            act(step)
            return carry

        lax.fori_loop(1, self.count, body, 0)

    def start(self):
        self.each(lambda step: self.copy(step, self.me).start())

    def wait_recv(self):
        self.each(
            lambda step: self.copy(step, lax.rem(self.me + self.count - step, self.count)).wait_recv()
        )

    def wait_send(self):
        self.each(lambda step: self.copy(step, self.me).wait_send())


class Halo:
    def __init__(self, coords, counts, rows, cols, hrow, hcol, hcor, send, recv):
        (r, c), (nr, nc) = coords, counts
        north, south = lax.rem(r + nr - 1, nr), lax.rem(r + 1, nr)
        west, east = lax.rem(c + nc - 1, nc), lax.rem(c + 1, nc)
        width = rows.shape[1]
        low, high = pl.ds(0, 16), pl.ds(width - 16, 16)
        plan = (
            (rows.at[0], hrow.at[1], (north, c)),
            (rows.at[1], hrow.at[0], (south, c)),
            (cols.at[0], hcol.at[1], (r, west)),
            (cols.at[1], hcol.at[0], (r, east)),
            (rows.at[0, low], hcor.at[3], (north, west)),
            (rows.at[0, high], hcor.at[2], (north, east)),
            (rows.at[1, low], hcor.at[1], (south, west)),
            (rows.at[1, high], hcor.at[0], (south, east)),
        )
        self.copies = [
            pltpu.make_async_remote_copy(
                src_ref=source,
                dst_ref=target,
                send_sem=send.at[k],
                recv_sem=recv.at[k],
                device_id=device,
                device_id_type=MESH,
            )
            for k, (source, target, device) in enumerate(plan)
        ]

    def start(self):
        for copy in self.copies:
            copy.start()

    def wait_recv(self):
        for copy in self.copies:
            copy.wait_recv()

    def wait_send(self):
        for copy in self.copies:
            copy.wait_send()


def put_row(field, pair, side, value, scratch):
    width = value.shape[0]
    base = side * 384
    scratch[8 : 8 + width] = value
    field[pair, :, base : base + 128] = scratch[7 : 7 + width].astype(BF)
    field[pair, :, base + 128 : base + 256] = value.astype(BF)
    field[pair, :, base + 256 : base + 384] = scratch[9 : 9 + width].astype(BF)


def set_halo(field, hrow, hcol, hcor, hcolf, masks, scratch):
    north, south, west, east = masks
    pairs, width = field.shape[0] - 1, field.shape[1]
    for pair, side, k, up in ((0, 0, 0, north), (pairs, 1, 1, south)):
        scratch[7:8] = hcor[2 * k].astype(F32)[15:16] * (up * west)
        scratch[8 + width : 9 + width] = hcor[2 * k + 1].astype(F32)[0:1] * (up * east)
        put_row(field, pair, side, hrow[k].astype(F32) * up, scratch)
    hcolf[0] = hcol[0].astype(F32) * west
    hcolf[1] = hcol[1].astype(F32) * east
    place = iota((16, 128), 0)

    def body(pair, carry):
        for half, spot, sub, lane in ((0, 0, 0, 0), (1, width - 16, 15, 256)):
            for side in (1, 0):
                at = (
                    pair + 1 - side,
                    pl.ds(spot, 16),
                    pl.ds(side * 384 + lane, 128),
                )
                cell = hcolf[half, pl.ds(2 * pair + 1 - side, 1), :]
                field[at] = jnp.where(place == sub, cell, field[at].astype(F32)).astype(BF)
        return carry

    lax.fori_loop(0, pairs, body, 0)


def take_edges(field, rows, cols, colf):
    pairs = field.shape[0] - 1
    rows[0] = field[0, :, 512:640]
    rows[1] = field[pairs, :, 128:256]
    cols[0] = colf[0].astype(BF)
    cols[1] = colf[1].astype(BF)


def windows(field, at, count):
    width = field.shape[1]
    low = field[pl.ds(at, count)].reshape(count * width, 768)
    high = field[pl.ds(at + 1, count)].reshape(count * width, 768)
    return low, high


def centres(field, at, count):
    width = field.shape[1]
    even = field[pl.ds(at, count), :, 512:640].reshape(count * width, 128)
    odd = field[pl.ds(at + 1, count), :, 128:256].reshape(count * width, 128)
    return even, odd


def pair_weights(kernel, out, flipped):
    out[...] = jnp.zeros_like(out)
    for a in range(3):
        for b in range(3):
            if flipped:
                block = kernel[(2 - a) * 3 + 2 - b].astype(F32).T.astype(BF)
            else:
                block = kernel[a * 3 + b]
            for half in range(2):
                base = (a + half) * 384 + b * 128
                out[base : base + 128, half * 128 : half * 128 + 128] = block


def tap_sums(acc, out):
    for a in range(3):
        for b in range(3):
            total = None
            for half in range(2):
                i = a + half
                lane = (i % 2) * 384 + b * 128
                part = acc[i // 2, half * 128 : half * 128 + 128, lane : lane + 128]
                total = part if total is None else total + part
            t = a * 3 + b
            out[t * 8 : t * 8 + 8] = total.T.astype(BF).reshape(8, 16, 128)


def activate(z):
    sig = 0.5 + 0.5 * jnp.tanh(0.5 * z)
    y = z * sig
    return y, sig + y * (1.0 - sig)


def kernel(counts, *refs):
    nr, nc = counts
    (ids, live, fine_h, interp_h, coarse_h, cw_h, k1_h, k2_h, c1_h, c2_h) = refs[:10]
    (skip_h, gin_h, g1_h, g2_h, gcond_h, gcoarse_h) = refs[10:16]
    (
        fine, interp, coarse, cw, k1, k2, cot1, cot2,
        skip, gin, g1, g2, gcond, gcoarse,
        field1, field2, delta1, delta2, slope, back, flip,
        w1, w2, v1, v2, cwp, cpad, table, hot, spread, perm, proj, patch,
        acc1, acc2, gpacc, shift, pool, colf, hcolf,
        ask, asked, askrow, askedrow, reply, arrived, placed, gotten, gathered,
        rows1, cols1, hrow1, hcol1, hcor1,
        rows2, cols2, hrow2, hcol2, hcor2,
        rows3, cols3, hrow3, hcol3, hcor3,
        rows4, cols4, hrow4, hcol4, hcor4,
        p1, p1in, p1mid, p1all, p1out, p2, p2in, p2mid, p2all, p2out,
        q, qin, qmid, qall, qout,
        local_sem, row_send, row_recv, col_send, col_recv, halo_send, halo_recv,
    ) = refs[16:]
    r, c = lax.axis_index("row"), lax.axis_index("col")
    here = (r, c)
    pairs1, width1 = fine.shape[0], fine.shape[2]
    pairs2, width2 = pairs1 // 2, width1 // 2
    listed = ids.shape[1]
    places = nr * SLOT
    ncoarse = coarse.shape[0]
    nblocks = ncoarse // CB

    loads = [
        pltpu.make_async_copy(source, target, local_sem.at[k])
        for k, (source, target) in enumerate(
            (
                (cw_h, cw), (coarse_h, coarse), (k1_h, k1), (interp_h, interp),
                (fine_h, fine), (k2_h, k2), (c2_h, cot2), (c1_h, cot1),
            )
        )
    ]
    for load in loads:
        load.start()

    barrier = pltpu.get_barrier_semaphore()

    def greet_row(step, carry):
        pl.semaphore_signal(barrier, inc=1, device_id=(lax.rem(r + step, nr), c), device_id_type=MESH)
        return carry

    def greet_col(step, carry):
        pl.semaphore_signal(barrier, inc=1, device_id=(r, lax.rem(c + step, nc)), device_id_type=MESH)
        return carry

    lax.fori_loop(1, nr, greet_row, 0)
    lax.fori_loop(1, nc, greet_col, 0)
    for dr in (1, nr - 1):
        for dc in (1, nc - 1):
            pl.semaphore_signal(
                barrier,
                inc=1,
                device_id=(lax.rem(r + dr, nr), lax.rem(c + dc, nc)),
                device_id_type=MESH,
            )

    live_total = live[0, 0]
    owner = [lax.shift_right_logical(ids[0, k], jnp.int32(nblocks.bit_length() - 1)) for k in range(listed)]
    local = [ids[0, k] - owner[k] * nblocks for k in range(listed)]
    place = []
    for k in range(listed):
        rank = jnp.int32(0)
        for j in range(k):
            rank = rank + jnp.where(owner[j] == owner[k], 1, 0)
        place.append(jnp.where(k < live_total, owner[k] * CAP + rank, -1))
    row_at = iota((places, 128), 0)
    row_place = lax.shift_right_logical(row_at, 3)
    row_sub = row_at - row_place * CB
    wanted = jnp.full((places, 128), -1, jnp.int32)
    for k in range(listed):
        wanted = jnp.where(row_place == place[k], local[k] * CB + row_sub, wanted)
    ask[...] = wanted.astype(F32).reshape(ask.shape)
    list_at = iota((listed * CB, 128), 0)
    list_slot = lax.shift_right_logical(list_at, 3)
    list_sub = list_at - list_slot * CB
    target = jnp.full((listed * CB, 128), -1, jnp.int32)
    for k in range(listed):
        found = jnp.where(place[k] >= 0, place[k] * CB, -CB)
        target = jnp.where(list_slot == k, found + list_sub, target)
    lanes = iota((listed * CB, 128), 1)
    for j in range(places // 128):
        perm[:, j * 128 : j * 128 + 128] = jnp.where(target == lanes + j * 128, 1.0, 0.0).astype(BF)

    pl.semaphore_wait(barrier, nr - 1 + nc - 1 + 4)

    row = lambda k, source, dest: Push(here, 0, nr, source, dest, row_send.at[k], row_recv.at[k])
    col = lambda k, source, dest: Push(here, 1, nc, source, dest, col_send.at[k], col_recv.at[k])
    halo = lambda k, *bufs: Halo(here, counts, *bufs, halo_send.at[k], halo_recv.at[k])
    masks = (
        jnp.where(r > 0, 1.0, 0.0),
        jnp.where(r < nr - 1, 1.0, 0.0),
        jnp.where(c > 0, 1.0, 0.0),
        jnp.where(c < nc - 1, 1.0, 0.0),
    )

    push_ask = row(0, lambda peer: ask.at[peer], asked)
    push_ask.start()
    asked[r] = ask[r]

    loads[0].wait()
    loads[1].wait()
    cwp[...] = jnp.zeros_like(cwp)
    cwp[0 : cw.shape[0], :] = cw[...].astype(F32)
    cpad[...] = jnp.zeros_like(cpad)
    cpad[:, 0 : coarse.shape[1]] = coarse[...]
    weight = cwp[...].astype(BF)

    def project(k, carry):
        at = pl.ds(pl.multiple_of(k * 512, 512), 512)
        part = cpad[at, :]
        table[at, 0:128] = dot(part, weight).astype(BF)
        table[at, 128:256] = part
        return carry

    lax.fori_loop(0, ncoarse // 512, project, 0)
    loads[2].wait()
    pair_weights(k1, w1, False)

    push_ask.wait_recv()
    every = asked[...].reshape(places, 128)
    lane_f = iota((places, 128), 1).astype(F32)

    def heat(k, carry):
        base = (k * 128).astype(F32)
        hot[k] = jnp.where(every == lane_f + base, 1.0, 0.0).astype(BF)
        return carry

    lax.fori_loop(0, ncoarse // 128, heat, 0)
    gathered_rows = jnp.zeros((places, 256), F32)

    def gather(k, carry):
        pieces = [hot[k * 4 + j] for j in range(4)]
        return carry + dot(
            jnp.concatenate(pieces, axis=1), table[pl.ds(pl.multiple_of(k * 512, 512), 512), :]
        )

    gathered_rows = lax.fori_loop(0, ncoarse // 512, gather, gathered_rows)
    reply[...] = gathered_rows.astype(BF).reshape(reply.shape)
    push_reply = row(1, lambda peer: reply.at[peer], arrived)
    push_reply.start()
    arrived[r] = reply[r]
    askrow[...] = every.T[0:8, :]
    push_row = col(0, lambda peer: askrow, askedrow)
    push_row.start()
    askedrow[c] = askrow[...]

    loads[5].wait()
    pair_weights(k1, v1, True)
    pair_weights(k2, w2, False)
    pair_weights(k2, v2, True)
    loads[3].wait()

    def turn(pair, carry):
        at = pl.ds(pl.multiple_of(pair * width1, width1), width1)
        for side in range(2):
            flip[side, :, at] = interp[pair, side].astype(F32).T.astype(BF)
        return carry

    lax.fori_loop(0, pairs1, turn, 0)
    shift[...] = jnp.zeros_like(shift)

    push_reply.wait_recv()
    both = dot(perm[...], arrived[...].reshape(places, 256)).astype(BF)
    proj[...] = both[:, 0:128]
    patch[...] = both[:, 128:256]
    loads[4].wait()

    def condition(k, carry):
        for j in range(4):
            pair = k * 4 + j
            value = dot(interp[pair].reshape(2 * width1, 128), proj[...])
            value = value + fine[pair].reshape(2 * width1, 128).astype(F32)
            for side in range(2):
                line = value[side * width1 : (side + 1) * width1]
                at = pl.ds(2 * pair + side, 1)
                colf[0, at, :] = line[0:1]
                colf[1, at, :] = line[width1 - 1 : width1]
                put_row(field1, pair + side, 1 - side, line, shift.at[2 * j + side])
        return carry

    lax.fori_loop(0, pairs1 // 4, condition, 0)
    take_edges(field1, rows1, cols1, colf)
    halo1 = halo(0, rows1, cols1, hrow1, hcol1, hcor1)
    halo1.start()

    push_row.wait_recv()

    def spot(k, carry):
        at = pl.ds(pl.multiple_of(k * 256, 256), 256)
        number = iota((256, places), 0).astype(F32) + (k * 256).astype(F32)
        for j in range(nc):
            match = number == askedrow[j, 0:1, :]
            spread[at, j * places : (j + 1) * places] = jnp.where(match, 1.0, 0.0).astype(BF)
        return carry

    lax.fori_loop(0, ncoarse // 256, spot, 0)

    halo1.wait_recv()
    set_halo(field1, hrow1, hcol1, hcor1, hcolf, masks, shift.at[0])

    def level_one(k, carry):
        pair = k * 4
        z = dot(jnp.concatenate(windows(field1, pair, 4), axis=1), w1[...])
        y, grade = activate(z)
        slope[pl.ds(pair, 4)] = grade.reshape(4, width1, 256)
        pool[...] = y[:, 0:128] + y[:, 128:256]
        total = pool[pl.ds(0, 4 * width2, stride=2), :] + pool[pl.ds(1, 4 * width2, stride=2), :]
        total = total * 0.25
        for j in range(4):
            line = total[j * width2 : (j + 1) * width2]
            at = pl.ds(pair + j, 1)
            colf[0, at, :] = line[0:1]
            colf[1, at, :] = line[width2 - 1 : width2]
            put_row(field2, k * 2 + (j + 1) // 2, (j + 1) % 2, line, shift.at[j])
        return carry

    lax.fori_loop(0, pairs1 // 4, level_one, 0)
    half = pl.ds(0, 2 * pairs2)
    take_edges(field2, rows2, cols2, colf.at[:, half])
    halo2 = halo(1, rows2, cols2, hrow2, hcol2, hcor2)
    halo2.start()
    loads[6].wait()
    halo2.wait_recv()
    set_halo(field2, hrow2, hcol2, hcor2, hcolf.at[:, half], masks, shift.at[0])

    def level_two(k, carry):
        pair = k * 8
        z = dot(jnp.concatenate(windows(field2, pair, 8), axis=1), w2[...])
        y, grade = activate(z)
        for side in range(2):
            lane = slice(side * 128, side * 128 + 128)
            skip[pl.ds(pair, 8), side] = y[:, lane].astype(BF).reshape(8, width2, 128)
            value = cot2[pl.ds(pair, 8), side].astype(F32) * grade[:, lane].reshape(8, width2, 128)
            for j in range(8):
                at = pl.ds(2 * (pair + j) + side, 1)
                colf[0, at, :] = value[j, 0:1]
                colf[1, at, :] = value[j, width2 - 1 : width2]
                put_row(delta2, pair + j + side, 1 - side, value[j], shift.at[j])
        return carry

    lax.fori_loop(0, pairs2 // 8, level_two, 0)
    skip_out = pltpu.make_async_copy(skip, skip_h, local_sem.at[8])
    skip_out.start()
    take_edges(delta2, rows3, cols3, colf.at[:, half])
    halo3 = halo(2, rows3, cols3, hrow3, hcol3, hcor3)
    halo3.start()

    def tap_grad(field, delta, acc, step):
        count = step // field.shape[1]

        def body(k, carry):
            outer = jnp.concatenate(centres(delta, k * count, count), axis=1)
            for i, window in enumerate(windows(field, k * count, count)):
                acc[i] += lax.dot_general(outer, window, CONTRACT0, preferred_element_type=F32)
            return carry

        acc[...] = jnp.zeros_like(acc)
        lax.fori_loop(0, (field.shape[0] - 1) // count, body, 0)

    tap_grad(field2, delta2, acc2, 1024)
    tap_sums(acc2, p2)

    class Total:
        def __init__(self, k, parts, held, middle, full):
            self.parts, self.held, self.middle, self.full = parts, held, middle, full
            self.size = parts.shape[0] // nr
            block = lambda peer: parts.at[pl.ds(peer * self.size, self.size)]
            self.first = row(k, block, held)
            self.second = col(k - 1, lambda peer: middle.at[c], middle)
            self.third = row(k + 1, lambda peer: full.at[r], full)

        def scatter(self):
            self.first.start()
            self.held[r] = self.parts[pl.ds(r * self.size, self.size)]

        def exchange(self):
            self.first.wait_recv()
            total = self.held[0].astype(F32)
            for k in range(1, nr):
                total = total + self.held[k].astype(F32)
            self.middle[c] = total.astype(self.middle.dtype)
            self.second.start()

        def gather(self):
            self.second.wait_recv()
            total = self.middle[0].astype(F32)
            for k in range(1, nc):
                total = total + self.middle[k].astype(F32)
            self.full[r] = total.astype(self.full.dtype)
            self.third.start()

        def finish(self):
            self.third.wait_recv()

        def wait_send(self):
            self.first.wait_send()
            self.second.wait_send()
            self.third.wait_send()

    sum2 = Total(2, p2, p2in, p2mid, p2all)
    sum1 = Total(4, p1, p1in, p1mid, p1all)
    sumq = Total(6, q, qin, qmid, qall)
    sum2.scatter()

    halo3.wait_recv()
    set_halo(delta2, hrow3, hcol3, hcor3, hcolf.at[:, half], masks, shift.at[0])

    def back_two(k, carry):
        z = dot(jnp.concatenate(windows(delta2, k * 8, 8), axis=1), v2[...]) * 0.25
        back[pl.ds(k * 8, 8)] = z.reshape(8, width2, 256)
        return carry

    lax.fori_loop(0, pairs2 // 8, back_two, 0)
    loads[7].wait()

    def delta_one(k, carry):
        for j in range(2):
            pair = k * 2 + j
            line = back[k, :, j * 128 : j * 128 + 128]
            base = j * width1
            pool[pl.ds(base, width2, stride=2), :] = line
            pool[pl.ds(base + 1, width2, stride=2), :] = line
            wide = pool[base : base + width1]
            for side in range(2):
                grade = slope[pair, :, side * 128 : side * 128 + 128]
                value = (cot1[pair, side].astype(F32) + wide) * grade
                at = pl.ds(2 * pair + side, 1)
                colf[0, at, :] = value[0:1]
                colf[1, at, :] = value[width1 - 1 : width1]
                put_row(delta1, pair + side, 1 - side, value, shift.at[2 * j + side])
        return carry

    lax.fori_loop(0, pairs1 // 2, delta_one, 0)
    take_edges(delta1, rows4, cols4, colf)
    halo4 = halo(3, rows4, cols4, hrow4, hcol4, hcor4)
    halo4.start()
    sum2.exchange()
    tap_grad(field1, delta1, acc1, 1024)
    tap_sums(acc1, p1)
    sum1.scatter()
    sum2.gather()
    halo4.wait_recv()
    set_halo(delta1, hrow4, hcol4, hcor4, hcolf, masks, shift.at[0])

    gpacc[...] = jnp.zeros_like(gpacc)

    def input_grad(k, carry):
        z = dot(jnp.concatenate(windows(delta1, k * 4, 4), axis=1), v1[...]).astype(BF)
        at = pl.ds(pl.multiple_of(k * 4 * width1, 4 * width1), 4 * width1)
        total = gpacc[...]
        for side in range(2):
            half_z = z[:, side * 128 : side * 128 + 128]
            gin[pl.ds(k * 4, 4), side] = half_z.reshape(4, width1, 128)
            total = total + dot(flip[side, :, at], half_z)
        gpacc[...] = total
        return carry

    lax.fori_loop(0, pairs1 // 4, input_grad, 0)
    gin_out = pltpu.make_async_copy(gin, gin_h, local_sem.at[9])
    gin_out.start()

    gproj = gpacc[...].astype(BF)
    gpatch = lax.dot_general(gproj, weight, CONTRACT1, preferred_element_type=F32).astype(BF)
    moved = lax.dot_general(perm[...], gpatch, CONTRACT0, preferred_element_type=F32)
    placed[...] = moved.astype(BF).reshape(placed.shape)
    push_back = row(8, lambda peer: placed.at[peer], gotten)
    push_back.start()
    gotten[r] = placed[r]
    q[...] = lax.dot_general(patch[...], gproj, CONTRACT0, preferred_element_type=F32).reshape(q.shape)
    sumq.scatter()
    sum1.exchange()

    push_back.wait_recv()
    gathered[c] = gotten[...]
    push_spread = col(7, lambda peer: gathered.at[c], gathered)
    push_spread.start()
    sumq.exchange()
    sum1.gather()
    sum2.finish()
    g2[...] = p2all[...].reshape(p2.shape)[0 : g2.shape[0]].astype(F32)
    g2_out = pltpu.make_async_copy(g2, g2_h, local_sem.at[10])
    g2_out.start()
    sumq.gather()
    push_spread.wait_recv()
    merged = gathered[...].reshape(nc * places, 128)

    def scatter(k, carry):
        at = pl.ds(pl.multiple_of(k * 512, 512), 512)
        gcoarse[at, :] = dot(spread[at, :], merged)[:, 0 : gcoarse.shape[1]]
        return carry

    lax.fori_loop(0, ncoarse // 512, scatter, 0)
    gcoarse_out = pltpu.make_async_copy(gcoarse, gcoarse_h, local_sem.at[11])
    gcoarse_out.start()
    sum1.finish()
    g1[...] = p1all[...].reshape(p1.shape)[0 : g1.shape[0]].astype(F32)
    g1_out = pltpu.make_async_copy(g1, g1_h, local_sem.at[12])
    g1_out.start()
    sumq.finish()
    gcond[...] = qall[...].reshape(128, 128)
    gcond_out = pltpu.make_async_copy(gcond, gcond_h, local_sem.at[13])
    gcond_out.start()

    for sent in (
        push_ask, push_reply, push_row, halo1, halo2, halo3, halo4, sum2, sum1, push_back,
        push_spread, sumq,
    ):
        sent.wait_send()
    for out in (skip_out, gin_out, g2_out, gcoarse_out, g1_out, gcond_out):
        out.wait()


def per_device(counts, fine, interp, ids, live, coarse, cw, conv_one, conv_two, cot_one, cot_two):
    nr, nc = counts
    height, width, channels = fine.shape
    pairs1, pairs2, width2 = height // 2, height // 4, width // 2
    ncoarse, cch = coarse.shape
    listed = ids.shape[-1]
    places = nr * SLOT
    blocks = -(-72 // nr) * nr
    any_space = pl.BlockSpec(memory_space=pl.ANY)
    smem = pl.BlockSpec(memory_space=pltpu.SMEM)
    vm = pltpu.VMEM
    chunk = blocks // nr

    def halo_bufs(rows, cols):
        return [
            vm((2, cols, 128), BF), vm((2, rows, 128), BF),
            vm((2, cols, 128), BF), vm((2, rows, 128), BF), vm((4, 16, 128), BF),
        ]

    def sum_bufs():
        return [
            vm((blocks, 16, 128), BF), vm((nr, chunk, 16, 128), BF), vm((nc, chunk, 16, 128), BF),
            vm((nr, chunk, 16, 128), BF),
        ]

    scratch = [
        vm((pairs1, 2, width, 128), BF), vm((pairs1, 2, width, 128), BF), vm((ncoarse, cch), BF),
        vm(cw.shape, BF), vm((9, 128, 128), BF), vm((9, 128, 128), BF),
        vm((pairs1, 2, width, 128), BF), vm((pairs2, 2, width2, 128), BF),
        vm((pairs2, 2, width2, 128), BF), vm((pairs1, 2, width, 128), BF),
        vm((72, 16, 128), F32), vm((72, 16, 128), F32), vm((128, 128), F32), vm((ncoarse, cch), F32),
        vm((pairs1 + 1, width, 768), BF), vm((pairs2 + 1, width2, 768), BF),
        vm((pairs1 + 1, width, 768), BF), vm((pairs2 + 1, width2, 768), BF),
        vm((pairs1, width, 256), F32), vm((pairs2, width2, 256), F32), vm((2, 128, pairs1 * width), BF),
        vm((1536, 256), BF), vm((1536, 256), BF), vm((1536, 256), BF), vm((1536, 256), BF),
        vm((128, 128), F32), vm((ncoarse, 128), BF), vm((ncoarse, 256), BF),
        vm((ncoarse // 128, places, 128), BF), vm((ncoarse, nc * places), BF),
        vm((listed * CB, places), BF), vm((listed * CB, 128), BF), vm((listed * CB, 128), BF),
        vm((2, 256, 768), F32), vm((2, 256, 768), F32), vm((128, 128), F32),
        vm((8, width + 16, 128), F32), vm((4 * width, 128), F32),
        vm((2, height, 128), F32), vm((2, height, 128), F32),
        vm((nr, SLOT, 128), F32), vm((nr, SLOT, 128), F32), vm((8, places), F32), vm((nc, 8, places), F32),
        vm((nr, SLOT, 256), BF), vm((nr, SLOT, 256), BF),
        vm((nr, SLOT, 128), BF), vm((nr, SLOT, 128), BF), vm((nc, nr, SLOT, 128), BF),
        *halo_bufs(height, width), *halo_bufs(height // 2, width2),
        *halo_bufs(height // 2, width2), *halo_bufs(height, width),
        *sum_bufs(), vm((8, 128), F32), *sum_bufs(), vm((8, 128), F32),
        vm((nr, 128 // nr, 128), F32), vm((nr, 1, 128 // nr, 128), F32), vm((nc, 1, 128 // nr, 128), F32),
        vm((nr, 1, 128 // nr, 128), F32), vm((8, 128), F32),
        pltpu.SemaphoreType.DMA((16,)),
        pltpu.SemaphoreType.DMA((9, nr)), pltpu.SemaphoreType.DMA((9, nr)),
        pltpu.SemaphoreType.DMA((8, nc)), pltpu.SemaphoreType.DMA((8, nc)),
        pltpu.SemaphoreType.DMA((4, 8)), pltpu.SemaphoreType.DMA((4, 8)),
    ]
    shape = jax.ShapeDtypeStruct
    skip, gin, g1, g2, gcond, gcoarse = pl.pallas_call(
        functools.partial(kernel, counts),
        out_shape=(
            shape((pairs2, 2, width2, 128), BF),
            shape((pairs1, 2, width, 128), BF),
            shape((72, 16, 128), F32),
            shape((72, 16, 128), F32),
            shape((128, 128), F32),
            shape((ncoarse, cch), F32),
        ),
        in_specs=[smem, smem] + [any_space] * 8,
        out_specs=(any_space,) * 6,
        scratch_shapes=scratch,
        compiler_params=pltpu.CompilerParams(
            collective_id=0, has_side_effects=True, vmem_limit_bytes=63 * 2**20
        ),
        cost_estimate=pl.CostEstimate(
            flops=10 * 10**9, bytes_accessed=13 * 10**6, transcendentals=2 * 10**6
        ),
    )(
        ids.reshape(1, listed),
        live.reshape(1, 1),
        fine.reshape(pairs1, 2, width, channels),
        interp.reshape(pairs1, 2, width, interp.shape[2]),
        coarse,
        cw,
        conv_one.reshape(9, 128, 128),
        conv_two.reshape(9, 128, 128),
        cot_one.reshape(pairs1, 2, width, channels),
        cot_two.reshape(pairs2, 2, width2, channels),
    )
    return (
        skip.reshape(height // 2, width2, 128),
        gin.reshape(height, width, 128),
        g1.reshape(3, 3, 128, 128),
        g2.reshape(3, 3, 128, 128),
        gcond[0:cch],
        gcoarse,
    )


def solution(mesh):
    counts = (mesh.shape["row"], mesh.shape["col"])
    tiles = P("row", "col", None)
    return jax.shard_map(
        functools.partial(per_device, counts),
        mesh=mesh,
        in_specs=(tiles, tiles, tiles, P("row", "col"), P("row", None), P(), P(), P(), tiles, tiles),
        out_specs=(tiles, tiles, P(), P(), P(), P("row", None)),
        check_vma=False,
    )
```

```python
import functools

import jax
import jax.numpy as jnp
from jax import lax
from jax.experimental import pallas as pl
from jax.experimental.pallas import tpu as pltpu
from jax.sharding import PartitionSpec as P

MESH = pl.DeviceIdType.MESH
BF = jnp.bfloat16
F32 = jnp.float32
CB = 8
CAP = 2
SLOT = CAP * CB
CONTRACT0 = (((0,), (0,)), ((), ()))
CONTRACT1 = (((1,), (1,)), ((), ()))


def dot(left, right):
    return jnp.dot(left, right, preferred_element_type=F32)


def iota(shape, dim):
    return lax.broadcasted_iota(jnp.int32, shape, dim)


class Push:
    def __init__(self, coords, axis, count, source, target, send, recv):
        self.coords, self.axis, self.count = coords, axis, count
        self.source, self.target, self.send, self.recv = source, target, send, recv
        self.me = coords[axis]

    def device(self, index):
        return (index, self.coords[1]) if self.axis == 0 else (self.coords[0], index)

    def copy(self, step, slot):
        peer = lax.rem(self.me + step, self.count)
        return pltpu.make_async_remote_copy(
            src_ref=self.source(peer),
            dst_ref=self.target.at[slot],
            send_sem=self.send.at[step],
            recv_sem=self.recv.at[step],
            device_id=self.device(peer),
            device_id_type=MESH,
        )

    def each(self, act):
        def body(step, carry):
            act(step)
            return carry

        lax.fori_loop(1, self.count, body, 0)

    def start(self):
        self.each(lambda step: self.copy(step, self.me).start())

    def wait_recv(self):
        self.each(
            lambda step: self.copy(step, lax.rem(self.me + self.count - step, self.count)).wait_recv()
        )

    def wait_send(self):
        self.each(lambda step: self.copy(step, self.me).wait_send())


class Spread:
    def __init__(self, coords, count, field, send, recv):
        self.row, self.c = coords
        self.field, self.send, self.recv = field, send, recv
        self.core = lax.rem(self.c, 2)
        self.chip = lax.div(self.c, 2)
        self.chips = count // 2

    def slot(self, step, core):
        return lax.rem(self.chip + self.chips - step, self.chips) * 2 + core

    def along(self, step):
        peer = lax.rem(self.chip + step, self.chips) * 2 + self.core
        return pltpu.make_async_remote_copy(
            src_ref=self.field.at[self.c],
            dst_ref=self.field.at[self.c],
            send_sem=self.send.at[step],
            recv_sem=self.recv.at[step],
            device_id=(self.row, peer),
            device_id_type=MESH,
        )

    def across(self, step):
        at = self.slot(step, self.core)
        return pltpu.make_async_remote_copy(
            src_ref=self.field.at[at],
            dst_ref=self.field.at[at],
            send_sem=self.send.at[self.chips + step],
            recv_sem=self.recv.at[self.chips + step],
            device_id=(self.row, self.chip * 2 + 1 - self.core),
            device_id_type=MESH,
        )

    def start(self):
        for step in range(1, self.chips):
            self.along(step).start()
        self.across(0).start()

    def drain(self, use):
        steps = range(1, self.chips)
        self.across(0).wait_recv()
        use([self.c, self.slot(0, 1 - self.core)])
        for step in steps:
            self.along(step).wait_recv()
            self.across(step).start()
        use([self.slot(step, self.core) for step in steps])
        for step in steps:
            self.across(step).wait_recv()
        use([self.slot(step, 1 - self.core) for step in steps])

    def wait_send(self):
        for step in range(1, self.chips):
            self.along(step).wait_send()
        for step in range(self.chips):
            self.across(step).wait_send()


class Halo:
    def __init__(self, coords, counts, rows, cols, hrow, hcol, hcor, send, recv):
        (r, c), (nr, nc) = coords, counts
        north, south = lax.rem(r + nr - 1, nr), lax.rem(r + 1, nr)
        west, east = lax.rem(c + nc - 1, nc), lax.rem(c + 1, nc)
        width = rows.shape[1]
        low, high = pl.ds(0, 16), pl.ds(width - 16, 16)
        plan = (
            (rows.at[0], hrow.at[1], (north, c)),
            (rows.at[1], hrow.at[0], (south, c)),
            (cols.at[0], hcol.at[1], (r, west)),
            (cols.at[1], hcol.at[0], (r, east)),
            (rows.at[0, low], hcor.at[3], (north, west)),
            (rows.at[0, high], hcor.at[2], (north, east)),
            (rows.at[1, low], hcor.at[1], (south, west)),
            (rows.at[1, high], hcor.at[0], (south, east)),
        )
        self.copies = [
            pltpu.make_async_remote_copy(
                src_ref=source,
                dst_ref=target,
                send_sem=send.at[k],
                recv_sem=recv.at[k],
                device_id=device,
                device_id_type=MESH,
            )
            for k, (source, target, device) in enumerate(plan)
        ]

    def start(self):
        for copy in self.copies:
            copy.start()

    def wait_recv(self):
        for copy in self.copies:
            copy.wait_recv()

    def wait_send(self):
        for copy in self.copies:
            copy.wait_send()


def put_row(field, pair, side, value, scratch):
    width = value.shape[0]
    base = side * 384
    scratch[8 : 8 + width] = value
    field[pair, :, base : base + 128] = scratch[7 : 7 + width].astype(BF)
    field[pair, :, base + 128 : base + 256] = value.astype(BF)
    field[pair, :, base + 256 : base + 384] = scratch[9 : 9 + width].astype(BF)


def set_halo(field, hrow, hcol, hcor, hcolf, masks, scratch):
    north, south, west, east = masks
    pairs, width = field.shape[0] - 1, field.shape[1]
    for pair, side, k, up in ((0, 0, 0, north), (pairs, 1, 1, south)):
        scratch[7:8] = hcor[2 * k].astype(F32)[15:16] * (up * west)
        scratch[8 + width : 9 + width] = hcor[2 * k + 1].astype(F32)[0:1] * (up * east)
        put_row(field, pair, side, hrow[k].astype(F32) * up, scratch)
    hcolf[0] = hcol[0].astype(F32) * west
    hcolf[1] = hcol[1].astype(F32) * east
    place = iota((16, 128), 0)

    def body(pair, carry):
        for half, spot, sub, lane in ((0, 0, 0, 0), (1, width - 16, 15, 256)):
            for side in (1, 0):
                at = (
                    pair + 1 - side,
                    pl.ds(spot, 16),
                    pl.ds(side * 384 + lane, 128),
                )
                cell = hcolf[half, pl.ds(2 * pair + 1 - side, 1), :]
                field[at] = jnp.where(place == sub, cell, field[at].astype(F32)).astype(BF)
        return carry

    lax.fori_loop(0, pairs, body, 0)


def take_edges(field, rows, cols, colf):
    pairs = field.shape[0] - 1
    rows[0] = field[0, :, 512:640]
    rows[1] = field[pairs, :, 128:256]
    cols[0] = colf[0].astype(BF)
    cols[1] = colf[1].astype(BF)


def windows(field, at, count):
    width = field.shape[1]
    low = field[pl.ds(at, count)].reshape(count * width, 768)
    high = field[pl.ds(at + 1, count)].reshape(count * width, 768)
    return low, high


def centres(field, at, count):
    width = field.shape[1]
    even = field[pl.ds(at, count), :, 512:640].reshape(count * width, 128)
    odd = field[pl.ds(at + 1, count), :, 128:256].reshape(count * width, 128)
    return even, odd


def pair_weights(kernel, out, flipped):
    out[...] = jnp.zeros_like(out)
    for a in range(3):
        for b in range(3):
            if flipped:
                block = kernel[(2 - a) * 3 + 2 - b].astype(F32).T.astype(BF)
            else:
                block = kernel[a * 3 + b]
            for half in range(2):
                base = (a + half) * 384 + b * 128
                out[base : base + 128, half * 128 : half * 128 + 128] = block


def tap_sums(acc, out):
    for a in range(3):
        for b in range(3):
            total = None
            for half in range(2):
                i = a + half
                lane = (i % 2) * 384 + b * 128
                part = acc[i // 2, half * 128 : half * 128 + 128, lane : lane + 128]
                total = part if total is None else total + part
            t = a * 3 + b
            out[t * 8 : t * 8 + 8] = total.T.astype(BF).reshape(8, 16, 128)


def activate(z):
    sig = 0.5 + 0.5 * jnp.tanh(0.5 * z)
    y = z * sig
    return y, sig + y * (1.0 - sig)


def kernel(counts, *refs):
    nr, nc = counts
    (ids, live, fine_h, interp_h, coarse_h, cw_h, k1_h, k2_h, c1_h, c2_h) = refs[:10]
    (skip_h, gin_h, p1_h, p2_h, gcond_h, gcoarse_h) = refs[10:16]
    (
        fine, interp, coarse, cw, k1, k2, cot1, cot2,
        skip, gin, gcoarse,
        field1, field2, delta1, delta2, slope, back, flip,
        w1, w2, v1, v2, cwp, coarse_t, table, hot, spread, perm, proj, patch,
        acc1, acc2, shift, pool, colf, hcolf,
        ask, asked, askrow, askedrow, reply, arrived, placed, gotten, gathered,
        rows1, cols1, hrow1, hcol1, hcor1,
        rows2, cols2, hrow2, hcol2, hcor2,
        rows3, cols3, hrow3, hcol3, hcor3,
        rows4, cols4, hrow4, hcol4, hcor4,
        p1, p1in, p1mid, p1all, p2, p2in, p2mid, p2all,
        q, qin, qmid, qall,
        local_sem, row_send, row_recv, col_send, col_recv, halo_send, halo_recv,
    ) = refs[16:]
    r, c = lax.axis_index("row"), lax.axis_index("col")
    here = (r, c)
    pairs1, width1 = fine.shape[0], fine.shape[2]
    pairs2, width2 = pairs1 // 2, width1 // 2
    listed = ids.shape[1]
    places = nr * SLOT
    ncoarse = coarse.shape[1]
    nblocks = ncoarse // CB

    loads = [
        pltpu.make_async_copy(source, target, local_sem.at[k])
        for k, (source, target) in enumerate(
            (
                (cw_h, cw), (coarse_h, coarse), (k1_h, k1), (interp_h, interp),
                (fine_h, fine), (k2_h, k2), (c2_h, cot2), (c1_h, cot1),
            )
        )
    ]
    for load in loads:
        load.start()

    barrier = pltpu.get_barrier_semaphore()

    def greet_row(step, carry):
        pl.semaphore_signal(barrier, inc=1, device_id=(lax.rem(r + step, nr), c), device_id_type=MESH)
        return carry

    def greet_col(step, carry):
        pl.semaphore_signal(barrier, inc=1, device_id=(r, lax.rem(c + step, nc)), device_id_type=MESH)
        return carry

    lax.fori_loop(1, nr, greet_row, 0)
    lax.fori_loop(1, nc, greet_col, 0)
    for dr in (1, nr - 1):
        for dc in (1, nc - 1):
            pl.semaphore_signal(
                barrier,
                inc=1,
                device_id=(lax.rem(r + dr, nr), lax.rem(c + dc, nc)),
                device_id_type=MESH,
            )

    live_total = live[0, 0]
    owner = [lax.shift_right_logical(ids[0, k], jnp.int32(nblocks.bit_length() - 1)) for k in range(listed)]
    local = [ids[0, k] - owner[k] * nblocks for k in range(listed)]
    place = []
    for k in range(listed):
        rank = jnp.int32(0)
        for j in range(k):
            rank = rank + jnp.where(owner[j] == owner[k], 1, 0)
        place.append(jnp.where(k < live_total, owner[k] * CAP + rank, -1))
    row_at = iota((places, 128), 0)
    row_place = lax.shift_right_logical(row_at, 3)
    row_sub = row_at - row_place * CB
    wanted = jnp.full((places, 128), -1, jnp.int32)
    for k in range(listed):
        wanted = jnp.where(row_place == place[k], local[k] * CB + row_sub, wanted)
    ask[...] = wanted.astype(F32).reshape(ask.shape)
    list_at = iota((listed * CB, 128), 0)
    list_slot = lax.shift_right_logical(list_at, 3)
    list_sub = list_at - list_slot * CB
    target = jnp.full((listed * CB, 128), -1, jnp.int32)
    for k in range(listed):
        found = jnp.where(place[k] >= 0, place[k] * CB, -CB)
        target = jnp.where(list_slot == k, found + list_sub, target)
    lanes = iota((listed * CB, 128), 1)
    for j in range(places // 128):
        perm[:, j * 128 : j * 128 + 128] = jnp.where(target == lanes + j * 128, 1.0, 0.0).astype(BF)

    loads[0].wait()
    loads[1].wait()
    cwp[...] = jnp.zeros_like(cwp)
    cwp[0 : cw.shape[0], :] = cw[...].astype(F32)
    coarse_t[...] = jnp.zeros_like(coarse_t)
    weight = cwp[...].astype(BF)

    def project(k, carry):
        at = pl.ds(pl.multiple_of(k * 512, 512), 512)
        coarse_t[0 : coarse.shape[0], :] = coarse[:, at].astype(F32)
        part = coarse_t[...].T.astype(BF)
        table[at, 0:128] = dot(part, weight).astype(BF)
        table[at, 128:256] = part
        return carry

    lax.fori_loop(0, ncoarse // 512, project, 0)
    loads[2].wait()
    pair_weights(k1, w1, False)

    loads[5].wait()
    pair_weights(k1, v1, True)
    pair_weights(k2, w2, False)
    pair_weights(k2, v2, True)
    loads[3].wait()

    def turn(pair, carry):
        at = pl.ds(pl.multiple_of(pair * width1, width1), width1)
        for side in range(2):
            flip[side, :, at] = interp[pair, side].astype(F32).T.astype(BF)
        return carry

    lax.fori_loop(0, pairs1, turn, 0)
    shift[...] = jnp.zeros_like(shift)


    pl.semaphore_wait(barrier, nr - 1 + nc - 1 + 4)

    row = lambda k, source, dest: Push(here, 0, nr, source, dest, row_send.at[k], row_recv.at[k])
    col = lambda k, source, dest: Push(here, 1, nc, source, dest, col_send.at[k], col_recv.at[k])
    halo = lambda k, *bufs: Halo(here, counts, *bufs, halo_send.at[k], halo_recv.at[k])
    masks = (
        jnp.where(r > 0, 1.0, 0.0),
        jnp.where(r < nr - 1, 1.0, 0.0),
        jnp.where(c > 0, 1.0, 0.0),
        jnp.where(c < nc - 1, 1.0, 0.0),
    )

    push_ask = row(0, lambda peer: ask.at[peer], asked)
    push_ask.start()
    asked[r] = ask[r]

    push_ask.wait_recv()
    every = asked[...].reshape(places, 128)
    lane_f = iota((places, 128), 1).astype(F32)

    def heat(k, carry):
        base = (k * 128).astype(F32)
        hot[k] = jnp.where(every == lane_f + base, 1.0, 0.0).astype(BF)
        return carry

    lax.fori_loop(0, ncoarse // 128, heat, 0)
    gathered_rows = jnp.zeros((places, 256), F32)

    def gather(k, carry):
        pieces = [hot[k * 4 + j] for j in range(4)]
        return carry + dot(
            jnp.concatenate(pieces, axis=1), table[pl.ds(pl.multiple_of(k * 512, 512), 512), :]
        )

    gathered_rows = lax.fori_loop(0, ncoarse // 512, gather, gathered_rows)
    reply[...] = gathered_rows.astype(BF).reshape(reply.shape)
    push_reply = row(1, lambda peer: reply.at[peer], arrived)
    push_reply.start()
    arrived[r] = reply[r]
    askrow[...] = every.T[0:8, :]
    push_row = col(0, lambda peer: askrow, askedrow)
    push_row.start()
    askedrow[c] = askrow[...]

    push_reply.wait_recv()
    both = dot(perm[...], arrived[...].reshape(places, 256)).astype(BF)
    proj[...] = both[:, 0:128]
    patch[...] = both[:, 128:256]
    loads[4].wait()

    def condition(k, carry):
        for j in range(4):
            pair = k * 4 + j
            value = dot(interp[pair].reshape(2 * width1, 128), proj[...])
            value = value + fine[pair].reshape(2 * width1, 128).astype(F32)
            for side in range(2):
                line = value[side * width1 : (side + 1) * width1]
                at = pl.ds(2 * pair + side, 1)
                colf[0, at, :] = line[0:1]
                colf[1, at, :] = line[width1 - 1 : width1]
                put_row(field1, pair + side, 1 - side, line, shift.at[2 * j + side])
        return carry

    lax.fori_loop(0, pairs1 // 4, condition, 0)
    take_edges(field1, rows1, cols1, colf)
    halo1 = halo(0, rows1, cols1, hrow1, hcol1, hcor1)
    halo1.start()

    push_row.wait_recv()

    def spot(k, carry):
        at = pl.ds(pl.multiple_of(k * 256, 256), 256)
        number = iota((256, places), 0).astype(F32) + (k * 256).astype(F32)
        for j in range(nc):
            match = number == askedrow[j, 0:1, :]
            spread[j, at, :] = jnp.where(match, 1.0, 0.0).astype(BF)
        return carry

    lax.fori_loop(0, ncoarse // 256, spot, 0)

    halo1.wait_recv()
    set_halo(field1, hrow1, hcol1, hcor1, hcolf, masks, shift.at[0])

    def level_one(k, carry):
        pair = k * 8
        z = dot(jnp.concatenate(windows(field1, pair, 8), axis=1), w1[...])
        y, grade = activate(z)
        slope[pl.ds(pair, 8)] = grade.reshape(8, width1, 256)
        pool[...] = y[:, 0:128] + y[:, 128:256]
        total = pool[pl.ds(0, 8 * width2, stride=2), :] + pool[pl.ds(1, 8 * width2, stride=2), :]
        total = total * 0.25
        for j in range(8):
            line = total[j * width2 : (j + 1) * width2]
            at = pl.ds(pair + j, 1)
            colf[0, at, :] = line[0:1]
            colf[1, at, :] = line[width2 - 1 : width2]
            put_row(field2, k * 4 + (j + 1) // 2, (j + 1) % 2, line, shift.at[j])
        return carry

    lax.fori_loop(0, pairs1 // 8, level_one, 0)
    half = pl.ds(0, 2 * pairs2)
    take_edges(field2, rows2, cols2, colf.at[:, half])
    halo2 = halo(1, rows2, cols2, hrow2, hcol2, hcor2)
    halo2.start()
    loads[6].wait()
    halo2.wait_recv()
    set_halo(field2, hrow2, hcol2, hcor2, hcolf.at[:, half], masks, shift.at[0])

    def level_two(k, carry):
        pair = k * 8
        z = dot(jnp.concatenate(windows(field2, pair, 8), axis=1), w2[...])
        y, grade = activate(z)
        for side in range(2):
            lane = slice(side * 128, side * 128 + 128)
            skip[pl.ds(pair, 8), side] = y[:, lane].astype(BF).reshape(8, width2, 128)
            value = cot2[pl.ds(pair, 8), side].astype(F32) * grade[:, lane].reshape(8, width2, 128)
            for j in range(8):
                at = pl.ds(2 * (pair + j) + side, 1)
                colf[0, at, :] = value[j, 0:1]
                colf[1, at, :] = value[j, width2 - 1 : width2]
                put_row(delta2, pair + j + side, 1 - side, value[j], shift.at[j])
        return carry

    lax.fori_loop(0, pairs2 // 8, level_two, 0)
    skip_out = pltpu.make_async_copy(skip, skip_h, local_sem.at[8])
    skip_out.start()
    take_edges(delta2, rows3, cols3, colf.at[:, half])
    halo3 = halo(2, rows3, cols3, hrow3, hcol3, hcor3)
    halo3.start()

    def tap_grad(field, delta, acc, step):
        count = step // field.shape[1]

        def body(k, carry):
            outer = jnp.concatenate(centres(delta, k * count, count), axis=1)
            for i, window in enumerate(windows(field, k * count, count)):
                acc[i] += lax.dot_general(outer, window, CONTRACT0, preferred_element_type=F32)
            return carry

        acc[...] = jnp.zeros_like(acc)
        lax.fori_loop(0, (field.shape[0] - 1) // count, body, 0)

    tap_grad(field2, delta2, acc2, 1024)
    tap_sums(acc2, p2)

    class Total:
        def __init__(self, k, parts, held, middle, full):
            self.parts, self.held, self.middle, self.full = parts, held, middle, full
            self.size = parts.shape[0] // nr
            block = lambda peer: parts.at[pl.ds(peer * self.size, self.size)]
            self.first = row(k, block, held)
            self.second = col(k - 1, lambda peer: middle.at[c], middle)
            self.third = row(k + 1, lambda peer: full.at[r], full)

        def scatter(self):
            self.first.start()
            self.held[r] = self.parts[pl.ds(r * self.size, self.size)]

        def exchange(self):
            self.first.wait_recv()
            total = self.held[0].astype(F32)
            for k in range(1, nr):
                total = total + self.held[k].astype(F32)
            self.middle[c] = total.astype(self.middle.dtype)
            self.second.start()

        def gather(self):
            self.second.wait_recv()
            total = self.middle[0].astype(F32)
            for k in range(1, nc):
                total = total + self.middle[k].astype(F32)
            self.full[r] = total.astype(self.full.dtype)
            self.third.start()

        def finish(self):
            self.third.wait_recv()

        def wait_send(self):
            self.first.wait_send()
            self.second.wait_send()
            self.third.wait_send()

    sum2 = Total(2, p2, p2in, p2mid, p2all)
    sum1 = Total(4, p1, p1in, p1mid, p1all)
    sumq = Total(6, q, qin, qmid, qall)
    sum2.scatter()

    halo3.wait_recv()
    set_halo(delta2, hrow3, hcol3, hcor3, hcolf.at[:, half], masks, shift.at[0])

    def back_two(k, carry):
        z = dot(jnp.concatenate(windows(delta2, k * 8, 8), axis=1), v2[...]) * 0.25
        back[pl.ds(k * 8, 8)] = z.reshape(8, width2, 256)
        return carry

    lax.fori_loop(0, pairs2 // 8, back_two, 0)
    loads[7].wait()

    def delta_one(k, carry):
        for j in range(2):
            pair = k * 2 + j
            line = back[k, :, j * 128 : j * 128 + 128]
            base = j * width1
            pool[pl.ds(base, width2, stride=2), :] = line
            pool[pl.ds(base + 1, width2, stride=2), :] = line
            wide = pool[base : base + width1]
            for side in range(2):
                grade = slope[pair, :, side * 128 : side * 128 + 128]
                value = (cot1[pair, side].astype(F32) + wide) * grade
                at = pl.ds(2 * pair + side, 1)
                colf[0, at, :] = value[0:1]
                colf[1, at, :] = value[width1 - 1 : width1]
                put_row(delta1, pair + side, 1 - side, value, shift.at[2 * j + side])
        return carry

    lax.fori_loop(0, pairs1 // 2, delta_one, 0)
    take_edges(delta1, rows4, cols4, colf)
    halo4 = halo(3, rows4, cols4, hrow4, hcol4, hcor4)
    halo4.start()
    sum2.exchange()
    tap_grad(field1, delta1, acc1, 2048)
    tap_sums(acc1, p1)
    sum1.scatter()
    sum2.gather()
    halo4.wait_recv()
    set_halo(delta1, hrow4, hcol4, hcor4, hcolf, masks, shift.at[0])

    def input_grad(k, carry):
        z = dot(jnp.concatenate(windows(delta1, k * 16, 16), axis=1), v1[...]).astype(BF)
        for side in range(2):
            gin[pl.ds(k * 16, 16), side] = z[:, side * 128 : side * 128 + 128].reshape(16, width1, 128)
        return carry

    lax.fori_loop(0, pairs1 // 16, input_grad, 0)

    def list_grad(k, carry):
        at = pl.ds(pl.multiple_of(k * 8 * width1, 8 * width1), 8 * width1)
        for side in range(2):
            part = gin[pl.ds(k * 8, 8), side].reshape(8 * width1, 128)
            carry = carry + dot(flip[side, :, at], part)
        return carry

    gpacc = lax.fori_loop(0, pairs1 // 8, list_grad, jnp.zeros((128, 128), F32))
    gin_out = pltpu.make_async_copy(gin, gin_h, local_sem.at[9])
    gin_out.start()

    gproj = gpacc.astype(BF)
    gpatch = lax.dot_general(gproj, weight, CONTRACT1, preferred_element_type=F32).astype(BF)
    moved = lax.dot_general(perm[...], gpatch, CONTRACT0, preferred_element_type=F32)
    placed[...] = moved.astype(BF).reshape(placed.shape)
    push_back = row(8, lambda peer: placed.at[peer], gotten)
    push_back.start()
    gotten[r] = placed[r]
    q[...] = lax.dot_general(patch[...], gproj, CONTRACT0, preferred_element_type=F32).reshape(q.shape)
    sumq.scatter()
    sum1.exchange()

    push_back.wait_recv()
    gathered[c] = gotten[...]
    push_spread = Spread(here, nc, gathered, col_send.at[7], col_recv.at[7])
    push_spread.start()
    sumq.exchange()
    sum1.gather()
    sum2.finish()
    p2_out = pltpu.make_async_copy(p2all, p2_h, local_sem.at[10])
    p2_out.start()
    sumq.gather()
    started = []

    def scatter(slots):
        if not slots:
            return
        parts = jnp.concatenate([gathered[slot].reshape(places, 128) for slot in slots], axis=0)
        first = not started
        started.append(slots)

        def body(k, carry):
            at = pl.ds(pl.multiple_of(k * 512, 512), 512)
            value = dot(jnp.concatenate([spread[slot, at, :] for slot in slots], axis=1), parts)
            gcoarse[at, :] = value if first else gcoarse[at, :] + value
            return carry

        lax.fori_loop(0, ncoarse // 512, body, 0)

    push_spread.drain(scatter)
    gcoarse_out = pltpu.make_async_copy(gcoarse, gcoarse_h, local_sem.at[11])
    gcoarse_out.start()
    sum1.finish()
    p1_out = pltpu.make_async_copy(p1all, p1_h, local_sem.at[12])
    p1_out.start()
    sumq.finish()
    gcond_out = pltpu.make_async_copy(qall, gcond_h, local_sem.at[13])
    gcond_out.start()

    for sent in (
        push_ask, push_reply, push_row, halo1, halo2, halo3, halo4, sum2, sum1, push_back,
        push_spread, sumq,
    ):
        sent.wait_send()
    for out in (skip_out, gin_out, p2_out, gcoarse_out, p1_out, gcond_out):
        out.wait()


def finish_kernel(skip_k, gin_k, p1_k, p2_k, gcond_k, gcoarse_k, *refs):
    skip_h, gin_h, g1_h, g2_h, gcond_h, gcoarse_h = refs[:6]
    skip, gin, p1, p2, qs, held, g1, g2, gcond, gcoarse, sem = refs[6:]
    quarter = gin.shape[0] // 4
    parts = [pl.ds(k * quarter, quarter) for k in range(4)]
    loads = [
        pltpu.make_async_copy(source, target, sem.at[k])
        for k, (source, target) in enumerate(
            (
                (gcoarse_k, held), (skip_k, skip), (p2_k, p2), (p1_k, p1), (gcond_k, qs),
                *((gin_k.at[part], gin.at[part]) for part in parts),
            )
        )
    ]
    for load in loads:
        load.start()
    outs = []

    def store(source, target):
        copy = pltpu.make_async_copy(source, target, sem.at[16 + len(outs)])
        copy.start()
        outs.append(copy)

    loads[0].wait()
    for k in range(held.shape[0] // 128):
        at = slice(k * 128, k * 128 + 128)
        gcoarse[:, at] = held[at, :].T[0 : gcoarse.shape[0], :]
    store(gcoarse, gcoarse_h)
    loads[1].wait()
    store(skip, skip_h)
    for load, part in zip(loads[5:], parts):
        load.wait()
        store(gin.at[part], gin_h.at[part])
    loads[2].wait()
    g2[...] = p2[0 : g2.shape[0]].astype(F32)
    store(g2, g2_h)
    loads[3].wait()
    g1[...] = p1[0 : g1.shape[0]].astype(F32)
    store(g1, g1_h)
    loads[4].wait()
    gcond[...] = qs[0 : gcond.shape[0], :]
    store(gcond, gcond_h)
    for out in outs:
        out.wait()


def per_device(counts, fine, interp, ids, live, coarse, cw, conv_one, conv_two, cot_one, cot_two):
    nr, nc = counts
    height, width, channels = fine.shape
    pairs1, pairs2, width2 = height // 2, height // 4, width // 2
    cch, ncoarse = coarse.shape[1], coarse.shape[0]
    listed = ids.shape[-1]
    places = nr * SLOT
    blocks = -(-72 // nr) * nr
    any_space = pl.BlockSpec(memory_space=pl.ANY)
    smem = pl.BlockSpec(memory_space=pltpu.SMEM)
    vm = pltpu.VMEM
    chunk = blocks // nr

    def halo_bufs(rows, cols):
        return [
            vm((2, cols, 128), BF), vm((2, rows, 128), BF),
            vm((2, cols, 128), BF), vm((2, rows, 128), BF), vm((4, 16, 128), BF),
        ]

    def sum_bufs():
        return [
            vm((blocks, 16, 128), BF), vm((nr, chunk, 16, 128), BF), vm((nc, chunk, 16, 128), BF),
            vm((nr, chunk, 16, 128), BF),
        ]

    scratch = [
        vm((pairs1, 2, width, 128), BF), vm((pairs1, 2, width, 128), BF), vm((cch, ncoarse), BF),
        vm(cw.shape, BF), vm((9, 128, 128), BF), vm((9, 128, 128), BF),
        vm((pairs1, 2, width, 128), BF), vm((pairs2, 2, width2, 128), BF),
        vm((pairs2, 2, width2, 128), BF), vm((pairs1, 2, width, 128), BF),
        vm((ncoarse, 128), F32),
        vm((pairs1 + 1, width, 768), BF), vm((pairs2 + 1, width2, 768), BF),
        vm((pairs1 + 1, width, 768), BF), vm((pairs2 + 1, width2, 768), BF),
        vm((pairs1, width, 256), F32), vm((pairs2, width2, 256), F32), vm((2, 128, pairs1 * width), BF),
        vm((1536, 256), BF), vm((1536, 256), BF), vm((1536, 256), BF), vm((1536, 256), BF),
        vm((128, 128), F32), vm((128, 512), F32), vm((ncoarse, 256), BF),
        vm((ncoarse // 128, places, 128), BF), vm((nc, ncoarse, places), BF),
        vm((listed * CB, places), BF), vm((listed * CB, 128), BF), vm((listed * CB, 128), BF),
        vm((2, 256, 768), F32), vm((2, 256, 768), F32),
        vm((8, width + 16, 128), F32), vm((8 * width, 128), F32),
        vm((2, height, 128), F32), vm((2, height, 128), F32),
        vm((nr, SLOT, 128), F32), vm((nr, SLOT, 128), F32), vm((8, places), F32), vm((nc, 8, places), F32),
        vm((nr, SLOT, 256), BF), vm((nr, SLOT, 256), BF),
        vm((nr, SLOT, 128), BF), vm((nr, SLOT, 128), BF), vm((nc, nr, SLOT, 128), BF),
        *halo_bufs(height, width), *halo_bufs(height // 2, width2),
        *halo_bufs(height // 2, width2), *halo_bufs(height, width),
        *sum_bufs(), *sum_bufs(),
        vm((nr, 128 // nr, 128), F32), vm((nr, 1, 128 // nr, 128), F32), vm((nc, 1, 128 // nr, 128), F32),
        vm((nr, 1, 128 // nr, 128), F32),
        pltpu.SemaphoreType.DMA((16,)),
        pltpu.SemaphoreType.DMA((9, nr)), pltpu.SemaphoreType.DMA((9, nr)),
        pltpu.SemaphoreType.DMA((8, nc)), pltpu.SemaphoreType.DMA((8, nc)),
        pltpu.SemaphoreType.DMA((4, 8)), pltpu.SemaphoreType.DMA((4, 8)),
    ]
    shape = jax.ShapeDtypeStruct
    results = pl.pallas_call(
        functools.partial(kernel, counts),
        out_shape=(
            shape((pairs2, 2, width2, 128), BF),
            shape((pairs1, 2, width, 128), BF),
            shape((nr, chunk, 16, 128), BF),
            shape((nr, chunk, 16, 128), BF),
            shape((nr, 1, 128 // nr, 128), F32),
            shape((ncoarse, 128), F32),
        ),
        in_specs=[smem, smem] + [any_space] * 8,
        out_specs=(any_space,) * 6,
        scratch_shapes=scratch,
        compiler_params=pltpu.CompilerParams(
            collective_id=0, has_side_effects=True, vmem_limit_bytes=63 * 2**20
        ),
        cost_estimate=pl.CostEstimate(
            flops=10 * 10**9, bytes_accessed=13 * 10**6, transcendentals=2 * 10**6
        ),
    )(
        ids.reshape(1, listed),
        live.reshape(1, 1),
        fine.reshape(pairs1, 2, width, channels),
        interp.reshape(pairs1, 2, width, interp.shape[2]),
        coarse.T,
        cw,
        conv_one.reshape(9, 128, 128),
        conv_two.reshape(9, 128, 128),
        cot_one.reshape(pairs1, 2, width, channels),
        cot_two.reshape(pairs2, 2, width2, channels),
    )
    skip, gin, g1, g2, gcond, gcoarse = pl.pallas_call(
        finish_kernel,
        out_shape=(
            shape((pairs2, 2, width2, 128), BF),
            shape((pairs1, 2, width, 128), BF),
            shape((72, 16, 128), F32),
            shape((72, 16, 128), F32),
            shape((cch, 128), F32),
            shape((cch, ncoarse), F32),
        ),
        in_specs=[any_space] * 6,
        out_specs=(any_space,) * 6,
        scratch_shapes=[
            vm((pairs2, 2, width2, 128), BF), vm((pairs1, 2, width, 128), BF),
            vm((blocks, 16, 128), BF), vm((blocks, 16, 128), BF), vm((128, 128), F32), vm((ncoarse, 128), F32),
            vm((72, 16, 128), F32), vm((72, 16, 128), F32), vm((cch, 128), F32), vm((cch, ncoarse), F32),
            pltpu.SemaphoreType.DMA((32,)),
        ],
        compiler_params=pltpu.CompilerParams(vmem_limit_bytes=63 * 2**20),
        cost_estimate=pl.CostEstimate(flops=0, bytes_accessed=12 * 10**6, transcendentals=0),
    )(
        results[0],
        results[1],
        results[2].reshape(blocks, 16, 128),
        results[3].reshape(blocks, 16, 128),
        results[4].reshape(128, 128),
        results[5],
    )
    return (
        skip.reshape(height // 2, width2, 128),
        gin.reshape(height, width, 128),
        g1.reshape(3, 3, 128, 128),
        g2.reshape(3, 3, 128, 128),
        gcond,
        gcoarse.T,
    )


def solution(mesh):
    counts = (mesh.shape["row"], mesh.shape["col"])
    tiles = P("row", "col", None)
    return jax.shard_map(
        functools.partial(per_device, counts),
        mesh=mesh,
        in_specs=(tiles, tiles, tiles, P("row", "col"), P("row", None), P(), P(), P(), tiles, tiles),
        out_specs=(tiles, tiles, P(), P(), P(), P("row", None)),
        check_vma=False,
    )
```

```python
import functools

import jax
import jax.numpy as jnp
from jax import lax
from jax.experimental import pallas as pl
from jax.experimental.pallas import tpu as pltpu
from jax.sharding import PartitionSpec as P

MESH = pl.DeviceIdType.MESH
BF = jnp.bfloat16
F32 = jnp.float32
CB = 8
CAP = 2
SLOT = CAP * CB
CONTRACT0 = (((0,), (0,)), ((), ()))
CONTRACT1 = (((1,), (1,)), ((), ()))


def dot(left, right):
    return jnp.dot(left, right, preferred_element_type=F32)


def iota(shape, dim):
    return lax.broadcasted_iota(jnp.int32, shape, dim)


class Push:
    def __init__(self, coords, axis, count, source, target, send, recv):
        self.coords, self.axis, self.count = coords, axis, count
        self.source, self.target, self.send, self.recv = source, target, send, recv
        self.me = coords[axis]

    def device(self, index):
        return (index, self.coords[1]) if self.axis == 0 else (self.coords[0], index)

    def copy(self, step, slot):
        peer = lax.rem(self.me + step, self.count)
        return pltpu.make_async_remote_copy(
            src_ref=self.source(peer),
            dst_ref=self.target.at[slot],
            send_sem=self.send.at[step],
            recv_sem=self.recv.at[step],
            device_id=self.device(peer),
            device_id_type=MESH,
        )

    def each(self, act):
        def body(step, carry):
            act(step)
            return carry

        lax.fori_loop(1, self.count, body, 0)

    def start(self):
        self.each(lambda step: self.copy(step, self.me).start())

    def wait_recv(self):
        self.each(
            lambda step: self.copy(step, lax.rem(self.me + self.count - step, self.count)).wait_recv()
        )

    def wait_send(self):
        self.each(lambda step: self.copy(step, self.me).wait_send())


class Back:
    def __init__(self, coords, counts, placed, gathered, send, recv, core_send, core_recv):
        self.row, self.c = coords
        self.rows, self.chips = counts[0], counts[1] // 2
        self.placed, self.gathered = placed, gathered
        self.send, self.recv, self.core_send, self.core_recv = send, recv, core_send, core_recv
        self.core = lax.rem(self.c, 2)
        self.chip = lax.div(self.c, 2)

    def slot(self, step, core):
        return lax.rem(self.chip + self.chips - step, self.chips) * 2 + core

    def along(self, step, place, chip_slot, row_slot):
        row = lax.rem(self.row + place, self.rows)
        col = lax.rem(self.chip + step, self.chips) * 2 + self.core
        return pltpu.make_async_remote_copy(
            src_ref=self.placed.at[row],
            dst_ref=self.gathered.at[chip_slot, row_slot],
            send_sem=self.send.at[step, place],
            recv_sem=self.recv.at[step, place],
            device_id=(row, col),
            device_id_type=MESH,
        )

    def across(self, step):
        at = self.slot(step, self.core)
        return pltpu.make_async_remote_copy(
            src_ref=self.gathered.at[at],
            dst_ref=self.gathered.at[at],
            send_sem=self.core_send.at[step],
            recv_sem=self.core_recv.at[step],
            device_id=(self.row, self.chip * 2 + 1 - self.core),
            device_id_type=MESH,
        )

    def each(self, step, act):
        def body(place, carry):
            act(place)
            return carry

        lax.fori_loop(1 if step == 0 else 0, self.rows, body, 0)

    def start(self):
        for step in reversed(range(self.chips)):
            self.each(step, lambda place: self.along(step, place, self.c, self.row).start())

    def forward(self):
        for step in range(self.chips):
            at = self.slot(step, self.core)
            self.each(
                step,
                lambda place: self.along(
                    step, place, at, lax.rem(self.row + self.rows - place, self.rows)
                ).wait_recv(),
            )
            self.across(step).start()

    def slots(self, core):
        return [self.slot(step, core) for step in range(self.chips)]

    def wait_across(self):
        for step in range(self.chips):
            self.across(step).wait_recv()

    def wait_send(self):
        for step in range(self.chips):
            self.each(step, lambda place: self.along(step, place, self.c, self.row).wait_send())
            self.across(step).wait_send()


class Halo:
    def __init__(self, coords, counts, rows, cols, hrow, hcol, hcor, send, recv):
        (r, c), (nr, nc) = coords, counts
        north, south = lax.rem(r + nr - 1, nr), lax.rem(r + 1, nr)
        west, east = lax.rem(c + nc - 1, nc), lax.rem(c + 1, nc)
        width = rows.shape[1]
        low, high = pl.ds(0, 16), pl.ds(width - 16, 16)
        plan = (
            (rows.at[0], hrow.at[1], (north, c)),
            (rows.at[1], hrow.at[0], (south, c)),
            (cols.at[0], hcol.at[1], (r, west)),
            (cols.at[1], hcol.at[0], (r, east)),
            (rows.at[0, low], hcor.at[3], (north, west)),
            (rows.at[0, high], hcor.at[2], (north, east)),
            (rows.at[1, low], hcor.at[1], (south, west)),
            (rows.at[1, high], hcor.at[0], (south, east)),
        )
        self.copies = [
            pltpu.make_async_remote_copy(
                src_ref=source,
                dst_ref=target,
                send_sem=send.at[k],
                recv_sem=recv.at[k],
                device_id=device,
                device_id_type=MESH,
            )
            for k, (source, target, device) in enumerate(plan)
        ]

    def start(self):
        for copy in self.copies:
            copy.start()

    def wait_recv(self):
        for copy in self.copies:
            copy.wait_recv()

    def wait_send(self):
        for copy in self.copies:
            copy.wait_send()


def put_row(field, pair, side, value, scratch):
    width = value.shape[0]
    base = side * 384
    scratch[8 : 8 + width] = value
    field[pair, :, base : base + 128] = scratch[7 : 7 + width].astype(BF)
    field[pair, :, base + 128 : base + 256] = value.astype(BF)
    field[pair, :, base + 256 : base + 384] = scratch[9 : 9 + width].astype(BF)


def set_halo(field, hrow, hcol, hcor, hcolf, masks, scratch):
    north, south, west, east = masks
    pairs, width = field.shape[0] - 1, field.shape[1]
    for pair, side, k, up in ((0, 0, 0, north), (pairs, 1, 1, south)):
        scratch[7:8] = hcor[2 * k].astype(F32)[15:16] * (up * west)
        scratch[8 + width : 9 + width] = hcor[2 * k + 1].astype(F32)[0:1] * (up * east)
        put_row(field, pair, side, hrow[k].astype(F32) * up, scratch)
    hcolf[0] = hcol[0].astype(F32) * west
    hcolf[1] = hcol[1].astype(F32) * east
    place = iota((16, 128), 0)

    def body(pair, carry):
        for half, spot, sub, lane in ((0, 0, 0, 0), (1, width - 16, 15, 256)):
            for side in (1, 0):
                at = (
                    pair + 1 - side,
                    pl.ds(spot, 16),
                    pl.ds(side * 384 + lane, 128),
                )
                cell = hcolf[half, pl.ds(2 * pair + 1 - side, 1), :]
                field[at] = jnp.where(place == sub, cell, field[at].astype(F32)).astype(BF)
        return carry

    lax.fori_loop(0, pairs, body, 0)


def take_edges(field, rows, cols, colf):
    pairs = field.shape[0] - 1
    rows[0] = field[0, :, 512:640]
    rows[1] = field[pairs, :, 128:256]
    cols[0] = colf[0].astype(BF)
    cols[1] = colf[1].astype(BF)


def windows(field, at, count):
    width = field.shape[1]
    low = field[pl.ds(at, count)].reshape(count * width, 768)
    high = field[pl.ds(at + 1, count)].reshape(count * width, 768)
    return low, high


def centres(field, at, count):
    width = field.shape[1]
    even = field[pl.ds(at, count), :, 512:640].reshape(count * width, 128)
    odd = field[pl.ds(at + 1, count), :, 128:256].reshape(count * width, 128)
    return even, odd


def pair_weights(kernel, out, flipped):
    out[...] = jnp.zeros_like(out)
    for a in range(3):
        for b in range(3):
            if flipped:
                block = kernel[(2 - a) * 3 + 2 - b].astype(F32).T.astype(BF)
            else:
                block = kernel[a * 3 + b]
            for half in range(2):
                base = (a + half) * 384 + b * 128
                out[base : base + 128, half * 128 : half * 128 + 128] = block


def tap_sums(acc, out):
    for a in range(3):
        for b in range(3):
            total = None
            for half in range(2):
                i = a + half
                lane = (i % 2) * 384 + b * 128
                part = acc[i // 2, half * 128 : half * 128 + 128, lane : lane + 128]
                total = part if total is None else total + part
            t = a * 3 + b
            out[t * 8 : t * 8 + 8] = total.T.astype(BF).reshape(8, 16, 128)


def activate(z):
    sig = 0.5 + 0.5 * jnp.tanh(0.5 * z)
    y = z * sig
    return y, sig + y * (1.0 - sig)


def kernel(counts, *refs):
    nr, nc = counts
    (ids, live, fine_h, interp_h, coarse_h, cw_h, k1_h, k2_h, c1_h, c2_h) = refs[:10]
    (skip_h, gin_h, p1_h, p2_h, gcond_h, gcoarse_h) = refs[10:16]
    (
        fine, interp, coarse, cw, k1, k2, cot1, cot2,
        skip, gin, gcoarse,
        field1, field2, delta1, delta2, slope, back, flip,
        w1, w2, v1, v2, cwp, coarse_t, table, hot, spread, perm, proj, patch,
        acc1, acc2, shift, pool, stage, colf, hcolf,
        ask, asked, askrow, askedrow, reply, arrived, placed, gathered,
        rows1, cols1, hrow1, hcol1, hcor1,
        rows2, cols2, hrow2, hcol2, hcor2,
        rows3, cols3, hrow3, hcol3, hcor3,
        rows4, cols4, hrow4, hcol4, hcor4,
        p1, p1in, p1mid, p1all, p2, p2in, p2mid, p2all,
        q, qin, qmid, qall,
        local_sem, row_send, row_recv, col_send, col_recv, halo_send, halo_recv, back_send, back_recv,
    ) = refs[16:]
    r, c = lax.axis_index("row"), lax.axis_index("col")
    here = (r, c)
    pairs1, width1 = fine.shape[0], fine.shape[2]
    pairs2, width2 = pairs1 // 2, width1 // 2
    listed = ids.shape[1]
    places = nr * SLOT
    ncoarse = coarse.shape[1]
    nblocks = ncoarse // CB

    loads = [
        pltpu.make_async_copy(source, target, local_sem.at[k])
        for k, (source, target) in enumerate(
            (
                (cw_h, cw), (coarse_h, coarse), (k1_h, k1), (interp_h, interp),
                (fine_h, fine), (k2_h, k2), (c2_h, cot2), (c1_h, cot1),
            )
        )
    ]
    for load in loads:
        load.start()

    barrier = pltpu.get_barrier_semaphore()

    def greet(row, col):
        pl.semaphore_signal(barrier, inc=1, device_id=(row, col), device_id_type=MESH)

    for step in range(1, nc):
        greet(r, lax.rem(c + step, nc))
    for step in range(1, nr):
        greet(lax.rem(r + step, nr), c)

    live_total = live[0, 0]
    owner = [lax.shift_right_logical(ids[0, k], jnp.int32(nblocks.bit_length() - 1)) for k in range(listed)]
    local = [ids[0, k] - owner[k] * nblocks for k in range(listed)]
    place = []
    for k in range(listed):
        rank = jnp.int32(0)
        for j in range(k):
            rank = rank + jnp.where(owner[j] == owner[k], 1, 0)
        place.append(jnp.where(k < live_total, owner[k] * CAP + rank, -1))
    row_at = iota((places, 128), 0)
    row_place = lax.shift_right_logical(row_at, 3)
    row_sub = row_at - row_place * CB
    wanted = jnp.full((places, 128), -1, jnp.int32)
    for k in range(listed):
        wanted = jnp.where(row_place == place[k], local[k] * CB + row_sub, wanted)
    ask[...] = wanted.astype(F32).reshape(ask.shape)
    list_at = iota((listed * CB, 128), 0)
    list_slot = lax.shift_right_logical(list_at, 3)
    list_sub = list_at - list_slot * CB
    target = jnp.full((listed * CB, 128), -1, jnp.int32)
    for k in range(listed):
        found = jnp.where(place[k] >= 0, place[k] * CB, -CB)
        target = jnp.where(list_slot == k, found + list_sub, target)
    lanes = iota((listed * CB, 128), 1)
    for j in range(places // 128):
        perm[:, j * 128 : j * 128 + 128] = jnp.where(target == lanes + j * 128, 1.0, 0.0).astype(BF)

    loads[0].wait()
    loads[1].wait()
    cwp[...] = jnp.zeros_like(cwp)
    cwp[0 : cw.shape[0], :] = cw[...].astype(F32)
    coarse_t[...] = jnp.zeros_like(coarse_t)
    weight = cwp[...].astype(BF)

    def project(k, carry):
        at = pl.ds(pl.multiple_of(k * 512, 512), 512)
        coarse_t[0 : coarse.shape[0], :] = coarse[:, at].astype(F32)
        part = coarse_t[...].T.astype(BF)
        table[at, 0:128] = dot(part, weight).astype(BF)
        table[at, 128:256] = part
        return carry

    lax.fori_loop(0, ncoarse // 512, project, 0)
    loads[2].wait()
    pair_weights(k1, w1, False)

    loads[5].wait()
    pair_weights(k1, v1, True)
    pair_weights(k2, w2, False)
    pair_weights(k2, v2, True)
    loads[3].wait()

    def turn(pair, carry):
        at = pl.ds(pl.multiple_of(pair * width1, width1), width1)
        for side in range(2):
            flip[side, :, at] = interp[pair, side].astype(F32).T.astype(BF)
        return carry

    lax.fori_loop(0, pairs1, turn, 0)
    shift[...] = jnp.zeros_like(shift)


    pl.semaphore_wait(barrier, nr - 1 + nc - 1)

    row = lambda k, source, dest: Push(here, 0, nr, source, dest, row_send.at[k], row_recv.at[k])
    col = lambda k, source, dest: Push(here, 1, nc, source, dest, col_send.at[k], col_recv.at[k])
    halo = lambda k, *bufs: Halo(here, counts, *bufs, halo_send.at[k], halo_recv.at[k])
    masks = (
        jnp.where(r > 0, 1.0, 0.0),
        jnp.where(r < nr - 1, 1.0, 0.0),
        jnp.where(c > 0, 1.0, 0.0),
        jnp.where(c < nc - 1, 1.0, 0.0),
    )

    push_ask = row(0, lambda peer: ask.at[peer], asked)
    push_ask.start()
    asked[r] = ask[r]

    push_ask.wait_recv()
    every = asked[...].reshape(places, 128)
    lane_f = iota((places, 128), 1).astype(F32)

    def heat(k, carry):
        base = (k * 128).astype(F32)
        hot[k] = jnp.where(every == lane_f + base, 1.0, 0.0).astype(BF)
        return carry

    lax.fori_loop(0, ncoarse // 128, heat, 0)
    gathered_rows = jnp.zeros((places, 256), F32)

    def gather(k, carry):
        pieces = [hot[k * 4 + j] for j in range(4)]
        return carry + dot(
            jnp.concatenate(pieces, axis=1), table[pl.ds(pl.multiple_of(k * 512, 512), 512), :]
        )

    gathered_rows = lax.fori_loop(0, ncoarse // 512, gather, gathered_rows)
    reply[...] = gathered_rows.astype(BF).reshape(reply.shape)
    push_reply = row(1, lambda peer: reply.at[peer], arrived)
    push_reply.start()
    arrived[r] = reply[r]
    askrow[...] = every.T[0:8, :]
    push_row = col(0, lambda peer: askrow, askedrow)
    push_row.start()
    askedrow[c] = askrow[...]

    push_reply.wait_recv()
    both = dot(perm[...], arrived[...].reshape(places, 256)).astype(BF)
    proj[...] = both[:, 0:128]
    patch[...] = both[:, 128:256]
    loads[4].wait()

    for half in range(2):
        at = pl.ds(half * (width1 - 16), 16)
        value = dot(interp[:, :, at, :].reshape(pairs1 * 32, 128), proj[...])
        pool[...] = value + fine[:, :, at, :].reshape(pairs1 * 32, 128).astype(F32)
        cols1[half] = pool[pl.ds(15 * half, 2 * pairs1, stride=16), :].astype(BF)
        at = (half * (pairs1 - 1), half)
        rows1[half] = (dot(interp[at], proj[...]) + fine[at].astype(F32)).astype(BF)
    halo1 = halo(0, rows1, cols1, hrow1, hcol1, hcor1)
    halo1.start()

    def condition(k, carry):
        for j in range(4):
            pair = k * 4 + j
            value = dot(interp[pair].reshape(2 * width1, 128), proj[...])
            value = value + fine[pair].reshape(2 * width1, 128).astype(F32)
            for side in range(2):
                line = value[side * width1 : (side + 1) * width1]
                put_row(field1, pair + side, 1 - side, line, shift.at[2 * j + side])
        return carry

    lax.fori_loop(0, pairs1 // 4, condition, 0)
    halo1.wait_recv()
    set_halo(field1, hrow1, hcol1, hcor1, hcolf, masks, shift.at[0])

    middle = width1 - 32
    inner = middle // 2

    def level_one(pair, count, cols):
        lane_rows = [field1[pl.ds(pair + j, count), cols, :].reshape(-1, 768) for j in range(2)]
        y, grade = activate(dot(jnp.concatenate(lane_rows, axis=1), w1[...]))
        cells = y.shape[0]
        slope[pl.ds(pair, count), cols, :] = grade.reshape(count, cells // count, 256)
        pool[0:cells] = y[:, 0:128] + y[:, 128:256]
        total = pool[pl.ds(0, cells // 2, stride=2), :] + pool[pl.ds(1, cells // 2, stride=2), :]
        return total * 0.25

    for half in range(2):
        total = level_one(0, pairs1, pl.ds(half * (width1 - 16), 16))
        pool[0 : pairs1 * 8] = total
        cols2[half] = pool[pl.ds(7 * half, pairs1, stride=8), :].astype(BF)
        stage[1 : pairs1 + 1, 8 + half * (width2 - 8) : 16 + half * (width2 - 8), :] = total.reshape(
            pairs1, 8, 128
        )
    for half in range(2):
        at = half * (pairs1 - 1)
        stage[at + 1, 16 : 16 + inner, :] = level_one(at, 1, pl.ds(16, middle))
        rows2[half] = stage[at + 1, 8 : 8 + width2, :].astype(BF)
    halo2 = halo(1, rows2, cols2, hrow2, hcol2, hcor2)
    halo2.start()
    step1 = (pairs1 - 2) // 3

    def level_one_inner(k, carry):
        pair = 1 + k * step1
        total = level_one(pair, step1, pl.ds(16, middle))
        stage[pl.ds(pair + 1, step1), 16 : 16 + inner, :] = total.reshape(step1, inner, 128)
        return carry

    lax.fori_loop(0, 3, level_one_inner, 0)
    half = pl.ds(0, 2 * pairs2)
    loads[6].wait()
    halo2.wait_recv()
    north, south, west, east = masks
    for k, up in ((0, north), (1, south)):
        at = k * (pairs1 + 1)
        stage[at, 8 : 8 + width2, :] = hrow2[k].astype(F32) * up
        stage[at, 7:8, :] = hcor2[2 * k].astype(F32)[15:16] * (up * west)
        stage[at, 8 + width2 : 9 + width2, :] = hcor2[2 * k + 1].astype(F32)[0:1] * (up * east)
    hcolf[0, half] = hcol2[0].astype(F32) * west
    hcolf[1, half] = hcol2[1].astype(F32) * east

    def edge_cells(k, carry):
        stage[k + 1, 7:8, :] = hcolf[0, pl.ds(k, 1), :]
        stage[k + 1, 8 + width2 : 9 + width2, :] = hcolf[1, pl.ds(k, 1), :]
        return carry

    lax.fori_loop(0, pairs1, edge_cells, 0)

    def lay_out(pair, carry):
        for side in range(2):
            for j in range(3):
                lane = side * 384 + j * 128
                line = stage[2 * pair + side, 7 + j : 7 + j + width2, :]
                field2[pair, :, lane : lane + 128] = line.astype(BF)
        return carry

    lax.fori_loop(0, pairs2 + 1, lay_out, 0)

    def level_two(k, carry):
        pair = k * 8
        z = dot(jnp.concatenate(windows(field2, pair, 8), axis=1), w2[...])
        y, grade = activate(z)
        for side in range(2):
            lane = slice(side * 128, side * 128 + 128)
            skip[pl.ds(pair, 8), side] = y[:, lane].astype(BF).reshape(8, width2, 128)
            value = cot2[pl.ds(pair, 8), side].astype(F32) * grade[:, lane].reshape(8, width2, 128)
            for j in range(8):
                at = pl.ds(2 * (pair + j) + side, 1)
                colf[0, at, :] = value[j, 0:1]
                colf[1, at, :] = value[j, width2 - 1 : width2]
                put_row(delta2, pair + j + side, 1 - side, value[j], shift.at[j])
        return carry

    lax.fori_loop(0, pairs2 // 8, level_two, 0)
    skip_out = pltpu.make_async_copy(skip, skip_h, local_sem.at[8])
    skip_out.start()
    take_edges(delta2, rows3, cols3, colf.at[:, half])
    halo3 = halo(2, rows3, cols3, hrow3, hcol3, hcor3)
    halo3.start()

    def tap_grad(field, delta, acc, step):
        count = step // field.shape[1]

        def body(k, carry):
            outer = jnp.concatenate(centres(delta, k * count, count), axis=1)
            for i, window in enumerate(windows(field, k * count, count)):
                acc[i] += lax.dot_general(outer, window, CONTRACT0, preferred_element_type=F32)
            return carry

        acc[...] = jnp.zeros_like(acc)
        lax.fori_loop(0, (field.shape[0] - 1) // count, body, 0)

    push_row.wait_recv()

    def spot(k, carry):
        at = pl.ds(pl.multiple_of(k * 256, 256), 256)
        number = iota((256, places), 0).astype(F32) + (k * 256).astype(F32)
        for j in range(nc):
            match = number == askedrow[j, 0:1, :]
            spread[j, at, :] = jnp.where(match, 1.0, 0.0).astype(BF)
        return carry

    lax.fori_loop(0, ncoarse // 256, spot, 0)

    tap_grad(field2, delta2, acc2, 1024)
    tap_sums(acc2, p2)

    class Total:
        def __init__(self, k, parts, held, middle, full):
            self.parts, self.held, self.middle, self.full = parts, held, middle, full
            self.size = parts.shape[0] // nr
            block = lambda peer: parts.at[pl.ds(peer * self.size, self.size)]
            self.first = row(k, block, held)
            self.second = col(k - 1, lambda peer: middle.at[c], middle)
            self.third = row(k + 1, lambda peer: full.at[r], full)

        def scatter(self):
            self.first.start()
            self.held[r] = self.parts[pl.ds(r * self.size, self.size)]

        def exchange(self):
            self.first.wait_recv()
            total = self.held[0].astype(F32)
            for k in range(1, nr):
                total = total + self.held[k].astype(F32)
            self.middle[c] = total.astype(self.middle.dtype)
            self.second.start()

        def gather(self):
            self.second.wait_recv()
            total = self.middle[0].astype(F32)
            for k in range(1, nc):
                total = total + self.middle[k].astype(F32)
            self.full[r] = total.astype(self.full.dtype)
            self.third.start()

        def finish(self):
            self.third.wait_recv()

        def wait_send(self):
            self.first.wait_send()
            self.second.wait_send()
            self.third.wait_send()

    sum2 = Total(2, p2, p2in, p2mid, p2all)
    sum1 = Total(4, p1, p1in, p1mid, p1all)
    sumq = Total(6, q, qin, qmid, qall)
    sum2.scatter()

    halo3.wait_recv()
    set_halo(delta2, hrow3, hcol3, hcor3, hcolf.at[:, half], masks, shift.at[0])

    def back_two(k, carry):
        z = dot(jnp.concatenate(windows(delta2, k * 8, 8), axis=1), v2[...]) * 0.25
        back[pl.ds(k * 8, 8)] = z.reshape(8, width2, 256)
        return carry

    lax.fori_loop(0, pairs2 // 8, back_two, 0)
    loads[7].wait()

    def delta_one(k, carry):
        for j in range(2):
            pair = k * 2 + j
            line = back[k, :, j * 128 : j * 128 + 128]
            base = j * width1
            pool[pl.ds(base, width2, stride=2), :] = line
            pool[pl.ds(base + 1, width2, stride=2), :] = line
            wide = pool[base : base + width1]
            for side in range(2):
                grade = slope[pair, :, side * 128 : side * 128 + 128]
                value = (cot1[pair, side].astype(F32) + wide) * grade
                at = pl.ds(2 * pair + side, 1)
                colf[0, at, :] = value[0:1]
                colf[1, at, :] = value[width1 - 1 : width1]
                put_row(delta1, pair + side, 1 - side, value, shift.at[2 * j + side])
        return carry

    lax.fori_loop(0, pairs1 // 2, delta_one, 0)
    take_edges(delta1, rows4, cols4, colf)
    halo4 = halo(3, rows4, cols4, hrow4, hcol4, hcor4)
    halo4.start()
    sum2.exchange()
    tap_grad(field1, delta1, acc1, 2048)
    tap_sums(acc1, p1)
    sum1.scatter()
    sum2.gather()
    halo4.wait_recv()
    set_halo(delta1, hrow4, hcol4, hcor4, hcolf, masks, shift.at[0])

    def input_grad(k, carry):
        z = dot(jnp.concatenate(windows(delta1, k * 16, 16), axis=1), v1[...]).astype(BF)
        for side in range(2):
            gin[pl.ds(k * 16, 16), side] = z[:, side * 128 : side * 128 + 128].reshape(16, width1, 128)
        return carry

    lax.fori_loop(0, pairs1 // 16, input_grad, 0)

    def list_grad(k, carry):
        at = pl.ds(pl.multiple_of(k * 8 * width1, 8 * width1), 8 * width1)
        for side in range(2):
            part = gin[pl.ds(k * 8, 8), side].reshape(8 * width1, 128)
            carry = carry + dot(flip[side, :, at], part)
        return carry

    gpacc = lax.fori_loop(0, pairs1 // 8, list_grad, jnp.zeros((128, 128), F32))
    gin_out = pltpu.make_async_copy(gin, gin_h, local_sem.at[9])
    gin_out.start()

    gproj = gpacc.astype(BF)
    q[...] = lax.dot_general(patch[...], gproj, CONTRACT0, preferred_element_type=F32).reshape(q.shape)
    sumq.scatter()
    gpatch = lax.dot_general(gproj, weight, CONTRACT1, preferred_element_type=F32).astype(BF)
    moved = lax.dot_general(perm[...], gpatch, CONTRACT0, preferred_element_type=F32)
    placed[...] = moved.astype(BF).reshape(placed.shape)
    push_back = Back(
        here, counts, placed, gathered, back_send, back_recv, col_send.at[7], col_recv.at[7]
    )
    push_back.start()
    gathered[c, r] = placed[r]
    sum1.exchange()
    sum2.finish()
    p2_out = pltpu.make_async_copy(p2all, p2_h, local_sem.at[10])
    p2_out.start()
    sumq.exchange()
    push_back.forward()
    sum1.gather()
    started = []

    def scatter(slots):
        if not slots:
            return
        parts = jnp.concatenate([gathered[slot].reshape(places, 128) for slot in slots], axis=0)
        first = not started
        started.append(slots)

        def body(k, carry):
            at = pl.ds(pl.multiple_of(k * 1024, 1024), 1024)
            value = dot(jnp.concatenate([spread[slot, at, :] for slot in slots], axis=1), parts)
            gcoarse[at, :] = value if first else gcoarse[at, :] + value
            return carry

        lax.fori_loop(0, ncoarse // 1024, body, 0)

    scatter(push_back.slots(push_back.core))
    sumq.gather()
    push_back.wait_across()
    scatter(push_back.slots(1 - push_back.core))
    gcoarse_out = pltpu.make_async_copy(gcoarse, gcoarse_h, local_sem.at[11])
    gcoarse_out.start()
    sum1.finish()
    p1_out = pltpu.make_async_copy(p1all, p1_h, local_sem.at[12])
    p1_out.start()
    sumq.finish()
    gcond_out = pltpu.make_async_copy(qall, gcond_h, local_sem.at[13])
    gcond_out.start()

    for sent in (
        push_ask, push_reply, push_row, halo1, halo2, halo3, halo4, sum2, sum1, push_back,
        sumq,
    ):
        sent.wait_send()
    for out in (skip_out, gin_out, p2_out, gcoarse_out, p1_out, gcond_out):
        out.wait()


def finish_kernel(skip_k, gin_k, p1_k, p2_k, gcond_k, gcoarse_k, *refs):
    skip_h, gin_h, g1_h, g2_h, gcond_h, gcoarse_h = refs[:6]
    skip, gin, p1, p2, qs, held, g1, g2, gcond, gcoarse, sem = refs[6:]
    quarter = gin.shape[0] // 4
    parts = [pl.ds(k * quarter, quarter) for k in range(4)]
    loads = [
        pltpu.make_async_copy(source, target, sem.at[k])
        for k, (source, target) in enumerate(
            (
                (gcoarse_k, held), (skip_k, skip), (p2_k, p2), (p1_k, p1), (gcond_k, qs),
                *((gin_k.at[part], gin.at[part]) for part in parts),
            )
        )
    ]
    for load in loads:
        load.start()
    outs = []

    def store(source, target):
        copy = pltpu.make_async_copy(source, target, sem.at[16 + len(outs)])
        copy.start()
        outs.append(copy)

    loads[0].wait()
    for k in range(held.shape[0] // 128):
        at = slice(k * 128, k * 128 + 128)
        gcoarse[:, at] = held[at, :].T[0 : gcoarse.shape[0], :]
    store(gcoarse, gcoarse_h)
    loads[1].wait()
    store(skip, skip_h)
    for load, part in zip(loads[5:], parts):
        load.wait()
        store(gin.at[part], gin_h.at[part])
    loads[2].wait()
    g2[...] = p2[0 : g2.shape[0]].astype(F32)
    store(g2, g2_h)
    loads[3].wait()
    g1[...] = p1[0 : g1.shape[0]].astype(F32)
    store(g1, g1_h)
    loads[4].wait()
    gcond[...] = qs[0 : gcond.shape[0], :]
    store(gcond, gcond_h)
    for out in outs:
        out.wait()


def per_device(counts, fine, interp, ids, live, coarse, cw, conv_one, conv_two, cot_one, cot_two):
    nr, nc = counts
    height, width, channels = fine.shape
    pairs1, pairs2, width2 = height // 2, height // 4, width // 2
    cch, ncoarse = coarse.shape[1], coarse.shape[0]
    listed = ids.shape[-1]
    places = nr * SLOT
    blocks = -(-72 // nr) * nr
    any_space = pl.BlockSpec(memory_space=pl.ANY)
    smem = pl.BlockSpec(memory_space=pltpu.SMEM)
    vm = pltpu.VMEM
    chunk = blocks // nr

    def halo_bufs(rows, cols):
        return [
            vm((2, cols, 128), BF), vm((2, rows, 128), BF),
            vm((2, cols, 128), BF), vm((2, rows, 128), BF), vm((4, 16, 128), BF),
        ]

    def sum_bufs():
        return [
            vm((blocks, 16, 128), BF), vm((nr, chunk, 16, 128), BF), vm((nc, chunk, 16, 128), BF),
            vm((nr, chunk, 16, 128), BF),
        ]

    scratch = [
        vm((pairs1, 2, width, 128), BF), vm((pairs1, 2, width, 128), BF), vm((cch, ncoarse), BF),
        vm(cw.shape, BF), vm((9, 128, 128), BF), vm((9, 128, 128), BF),
        vm((pairs1, 2, width, 128), BF), vm((pairs2, 2, width2, 128), BF),
        vm((pairs2, 2, width2, 128), BF), vm((pairs1, 2, width, 128), BF),
        vm((ncoarse, 128), F32),
        vm((pairs1 + 1, width, 768), BF), vm((pairs2 + 1, width2, 768), BF),
        vm((pairs1 + 1, width, 768), BF), vm((pairs2 + 1, width2, 768), BF),
        vm((pairs1, width, 256), F32), vm((pairs2, width2, 256), F32), vm((2, 128, pairs1 * width), BF),
        vm((1536, 256), BF), vm((1536, 256), BF), vm((1536, 256), BF), vm((1536, 256), BF),
        vm((128, 128), F32), vm((128, 512), F32), vm((ncoarse, 256), BF),
        vm((ncoarse // 128, places, 128), BF), vm((nc, ncoarse, places), BF),
        vm((listed * CB, places), BF), vm((listed * CB, 128), BF), vm((listed * CB, 128), BF),
        vm((2, 256, 768), F32), vm((2, 256, 768), F32),
        vm((8, width + 16, 128), F32), vm((8 * width, 128), F32), vm((pairs1 + 2, width2 + 16, 128), F32),
        vm((2, height, 128), F32), vm((2, height, 128), F32),
        vm((nr, SLOT, 128), F32), vm((nr, SLOT, 128), F32), vm((8, places), F32), vm((nc, 8, places), F32),
        vm((nr, SLOT, 256), BF), vm((nr, SLOT, 256), BF),
        vm((nr, SLOT, 128), BF), vm((nc, nr, SLOT, 128), BF),
        *halo_bufs(height, width), *halo_bufs(height // 2, width2),
        *halo_bufs(height // 2, width2), *halo_bufs(height, width),
        *sum_bufs(), *sum_bufs(),
        vm((nr, 128 // nr, 128), F32), vm((nr, 1, 128 // nr, 128), F32), vm((nc, 1, 128 // nr, 128), F32),
        vm((nr, 1, 128 // nr, 128), F32),
        pltpu.SemaphoreType.DMA((16,)),
        pltpu.SemaphoreType.DMA((9, nr)), pltpu.SemaphoreType.DMA((9, nr)),
        pltpu.SemaphoreType.DMA((8, nc)), pltpu.SemaphoreType.DMA((8, nc)),
        pltpu.SemaphoreType.DMA((4, 8)), pltpu.SemaphoreType.DMA((4, 8)),
        pltpu.SemaphoreType.DMA((nc // 2, nr)), pltpu.SemaphoreType.DMA((nc // 2, nr)),
    ]
    shape = jax.ShapeDtypeStruct
    results = pl.pallas_call(
        functools.partial(kernel, counts),
        out_shape=(
            shape((pairs2, 2, width2, 128), BF),
            shape((pairs1, 2, width, 128), BF),
            shape((nr, chunk, 16, 128), BF),
            shape((nr, chunk, 16, 128), BF),
            shape((nr, 1, 128 // nr, 128), F32),
            shape((ncoarse, 128), F32),
        ),
        in_specs=[smem, smem] + [any_space] * 8,
        out_specs=(any_space,) * 6,
        scratch_shapes=scratch,
        compiler_params=pltpu.CompilerParams(
            collective_id=0, has_side_effects=True, vmem_limit_bytes=63 * 2**20
        ),
        cost_estimate=pl.CostEstimate(
            flops=10 * 10**9, bytes_accessed=13 * 10**6, transcendentals=2 * 10**6
        ),
    )(
        ids.reshape(1, listed),
        live.reshape(1, 1),
        fine.reshape(pairs1, 2, width, channels),
        interp.reshape(pairs1, 2, width, interp.shape[2]),
        coarse.T,
        cw,
        conv_one.reshape(9, 128, 128),
        conv_two.reshape(9, 128, 128),
        cot_one.reshape(pairs1, 2, width, channels),
        cot_two.reshape(pairs2, 2, width2, channels),
    )
    skip, gin, g1, g2, gcond, gcoarse = pl.pallas_call(
        finish_kernel,
        out_shape=(
            shape((pairs2, 2, width2, 128), BF),
            shape((pairs1, 2, width, 128), BF),
            shape((72, 16, 128), F32),
            shape((72, 16, 128), F32),
            shape((cch, 128), F32),
            shape((cch, ncoarse), F32),
        ),
        in_specs=[any_space] * 6,
        out_specs=(any_space,) * 6,
        scratch_shapes=[
            vm((pairs2, 2, width2, 128), BF), vm((pairs1, 2, width, 128), BF),
            vm((blocks, 16, 128), BF), vm((blocks, 16, 128), BF), vm((128, 128), F32), vm((ncoarse, 128), F32),
            vm((72, 16, 128), F32), vm((72, 16, 128), F32), vm((cch, 128), F32), vm((cch, ncoarse), F32),
            pltpu.SemaphoreType.DMA((32,)),
        ],
        compiler_params=pltpu.CompilerParams(vmem_limit_bytes=63 * 2**20),
        cost_estimate=pl.CostEstimate(flops=0, bytes_accessed=12 * 10**6, transcendentals=0),
    )(
        results[0],
        results[1],
        results[2].reshape(blocks, 16, 128),
        results[3].reshape(blocks, 16, 128),
        results[4].reshape(128, 128),
        results[5],
    )
    return (
        skip.reshape(height // 2, width2, 128),
        gin.reshape(height, width, 128),
        g1.reshape(3, 3, 128, 128),
        g2.reshape(3, 3, 128, 128),
        gcond,
        gcoarse.T,
    )


def solution(mesh):
    counts = (mesh.shape["row"], mesh.shape["col"])
    tiles = P("row", "col", None)
    return jax.shard_map(
        functools.partial(per_device, counts),
        mesh=mesh,
        in_specs=(tiles, tiles, tiles, P("row", "col"), P("row", None), P(), P(), P(), tiles, tiles),
        out_specs=(tiles, tiles, P(), P(), P(), P("row", None)),
        check_vma=False,
    )
```

```python
import functools

import jax
import jax.numpy as jnp
from jax import lax
from jax.experimental import pallas as pl
from jax.experimental.pallas import tpu as pltpu
from jax.sharding import PartitionSpec as P

MESH = pl.DeviceIdType.MESH
BF = jnp.bfloat16
F32 = jnp.float32
CB = 8
CAP = 2
SLOT = CAP * CB
CONTRACT0 = (((0,), (0,)), ((), ()))
CONTRACT1 = (((1,), (1,)), ((), ()))


def dot(left, right):
    return jnp.dot(left, right, preferred_element_type=F32)


def iota(shape, dim):
    return lax.broadcasted_iota(jnp.int32, shape, dim)


class Push:
    def __init__(self, coords, axis, count, source, target, send, recv):
        self.coords, self.axis, self.count = coords, axis, count
        self.source, self.target, self.send, self.recv = source, target, send, recv
        self.me = coords[axis]

    def device(self, index):
        return (index, self.coords[1]) if self.axis == 0 else (self.coords[0], index)

    def copy(self, step):
        peer = lax.rem(self.me + step, self.count)
        return pltpu.make_async_remote_copy(
            src_ref=self.source(peer),
            dst_ref=self.target.at[self.me],
            send_sem=self.send,
            recv_sem=self.recv,
            device_id=self.device(peer),
            device_id_type=MESH,
        )

    def all(self):
        blocks = self.target.at[pl.ds(0, self.count - 1)]
        return pltpu.make_async_remote_copy(
            src_ref=blocks,
            dst_ref=blocks,
            send_sem=self.send,
            recv_sem=self.recv,
            device_id=self.device(lax.rem(self.me + 1, self.count)),
            device_id_type=MESH,
        )

    def each(self, act):
        def body(step, carry):
            act(step)
            return carry

        lax.fori_loop(1, self.count, body, 0)

    def start(self):
        self.each(lambda step: self.copy(step).start())

    def wait_recv(self):
        self.all().wait_recv()

    def wait_send(self):
        self.all().wait_send()


class Back:
    def __init__(self, coords, counts, placed, gathered, send, recv, core_send, core_recv):
        self.row, self.c = coords
        self.rows, self.chips = counts[0], counts[1] // 2
        self.placed, self.gathered = placed, gathered
        self.send, self.recv, self.core_send, self.core_recv = send, recv, core_send, core_recv
        self.core = lax.rem(self.c, 2)
        self.chip = lax.div(self.c, 2)

    def slot(self, step, core):
        return lax.rem(self.chip + self.chips - step, self.chips) * 2 + core

    def along(self, step, place):
        row = lax.rem(self.row + place, self.rows)
        col = lax.rem(self.chip + step, self.chips) * 2 + self.core
        return pltpu.make_async_remote_copy(
            src_ref=self.placed.at[row],
            dst_ref=self.gathered.at[self.c, self.row],
            send_sem=self.send.at[step],
            recv_sem=self.recv.at[step],
            device_id=(row, col),
            device_id_type=MESH,
        )

    def all(self, step):
        blocks = self.placed.at[pl.ds(0, self.rows - 1 if step == 0 else self.rows)]
        return pltpu.make_async_remote_copy(
            src_ref=blocks,
            dst_ref=blocks,
            send_sem=self.send.at[step],
            recv_sem=self.recv.at[step],
            device_id=(lax.rem(self.row + 1, self.rows), self.c),
            device_id_type=MESH,
        )

    def across(self, step):
        at = self.slot(step, self.core)
        return pltpu.make_async_remote_copy(
            src_ref=self.gathered.at[at],
            dst_ref=self.gathered.at[at],
            send_sem=self.core_send.at[step],
            recv_sem=self.core_recv.at[step],
            device_id=(self.row, self.chip * 2 + 1 - self.core),
            device_id_type=MESH,
        )

    def each(self, step, act):
        def body(place, carry):
            act(place)
            return carry

        lax.fori_loop(1 if step == 0 else 0, self.rows, body, 0)

    def start(self):
        for step in reversed(range(self.chips)):
            self.each(step, lambda place: self.along(step, place).start())

    def forward(self):
        for step in range(self.chips):
            self.all(step).wait_recv()
            self.across(step).start()

    def slots(self, core):
        return [self.slot(step, core) for step in range(self.chips)]

    def wait_across(self):
        for step in range(self.chips):
            self.across(step).wait_recv()

    def wait_send(self):
        for step in range(self.chips):
            self.all(step).wait_send()
            self.across(step).wait_send()


class Halo:
    def __init__(self, coords, counts, rows, cols, hrow, hcol, hcor, send, recv):
        (r, c), (nr, nc) = coords, counts
        north, south = lax.rem(r + nr - 1, nr), lax.rem(r + 1, nr)
        west, east = lax.rem(c + nc - 1, nc), lax.rem(c + 1, nc)
        width = rows.shape[1]
        low, high = pl.ds(0, 16), pl.ds(width - 16, 16)
        plan = (
            (rows.at[0], hrow.at[1], (north, c)),
            (rows.at[1], hrow.at[0], (south, c)),
            (cols.at[0], hcol.at[1], (r, west)),
            (cols.at[1], hcol.at[0], (r, east)),
            (rows.at[0, low], hcor.at[3], (north, west)),
            (rows.at[0, high], hcor.at[2], (north, east)),
            (rows.at[1, low], hcor.at[1], (south, west)),
            (rows.at[1, high], hcor.at[0], (south, east)),
        )
        self.copies = [
            pltpu.make_async_remote_copy(
                src_ref=source,
                dst_ref=target,
                send_sem=send.at[k],
                recv_sem=recv.at[k],
                device_id=device,
                device_id_type=MESH,
            )
            for k, (source, target, device) in enumerate(plan)
        ]

    def start(self):
        for copy in self.copies:
            copy.start()

    def wait_recv(self):
        for copy in self.copies:
            copy.wait_recv()

    def wait_send(self):
        for copy in self.copies:
            copy.wait_send()


def put_row(field, pair, side, value, scratch):
    width = value.shape[0]
    base = side * 384
    scratch[8 : 8 + width] = value
    field[pair, :, base : base + 128] = scratch[7 : 7 + width].astype(BF)
    field[pair, :, base + 128 : base + 256] = value.astype(BF)
    field[pair, :, base + 256 : base + 384] = scratch[9 : 9 + width].astype(BF)


def set_halo(field, hrow, hcol, hcor, hcolf, masks, scratch):
    north, south, west, east = masks
    pairs, width = field.shape[0] - 1, field.shape[1]
    for pair, side, k, up in ((0, 0, 0, north), (pairs, 1, 1, south)):
        scratch[7:8] = hcor[2 * k].astype(F32)[15:16] * (up * west)
        scratch[8 + width : 9 + width] = hcor[2 * k + 1].astype(F32)[0:1] * (up * east)
        put_row(field, pair, side, hrow[k].astype(F32) * up, scratch)
    hcolf[0] = hcol[0].astype(F32) * west
    hcolf[1] = hcol[1].astype(F32) * east
    place = iota((16, 128), 0)

    def body(pair, carry):
        for half, spot, sub, lane in ((0, 0, 0, 0), (1, width - 16, 15, 256)):
            for side in (1, 0):
                at = (
                    pair + 1 - side,
                    pl.ds(spot, 16),
                    pl.ds(side * 384 + lane, 128),
                )
                cell = hcolf[half, pl.ds(2 * pair + 1 - side, 1), :]
                field[at] = jnp.where(place == sub, cell, field[at].astype(F32)).astype(BF)
        return carry

    lax.fori_loop(0, pairs, body, 0)


def take_edges(field, rows, cols, colf):
    pairs = field.shape[0] - 1
    rows[0] = field[0, :, 512:640]
    rows[1] = field[pairs, :, 128:256]
    cols[0] = colf[0].astype(BF)
    cols[1] = colf[1].astype(BF)


def windows(field, at, count):
    width = field.shape[1]
    low = field[pl.ds(at, count)].reshape(count * width, 768)
    high = field[pl.ds(at + 1, count)].reshape(count * width, 768)
    return low, high


def centres(field, at, count):
    width = field.shape[1]
    even = field[pl.ds(at, count), :, 512:640].reshape(count * width, 128)
    odd = field[pl.ds(at + 1, count), :, 128:256].reshape(count * width, 128)
    return even, odd


def pair_weights(kernel, out, flipped):
    out[...] = jnp.zeros_like(out)
    for a in range(3):
        for b in range(3):
            if flipped:
                block = kernel[(2 - a) * 3 + 2 - b].astype(F32).T.astype(BF)
            else:
                block = kernel[a * 3 + b]
            for half in range(2):
                base = (a + half) * 384 + b * 128
                out[base : base + 128, half * 128 : half * 128 + 128] = block


def tap_sums(acc, out):
    for a in range(3):
        for b in range(3):
            total = None
            for half in range(2):
                i = a + half
                lane = (i % 2) * 384 + b * 128
                part = acc[i // 2, half * 128 : half * 128 + 128, lane : lane + 128]
                total = part if total is None else total + part
            t = a * 3 + b
            out[t * 8 : t * 8 + 8] = total.T.astype(BF).reshape(8, 16, 128)


def activate(z):
    sig = 0.5 + 0.5 * jnp.tanh(0.5 * z)
    y = z * sig
    return y, sig + y * (1.0 - sig)


def kernel(counts, *refs):
    nr, nc = counts
    (ids, live, fine_h, interp_h, coarse_h, cw_h, k1_h, k2_h, c1_h, c2_h) = refs[:10]
    (skip_h, gin_h, p1_h, p2_h, gcond_h, gcoarse_h) = refs[10:16]
    (
        fine, interp, coarse, cw, k1, k2, cot1, cot2,
        skip, gin, gcoarse,
        field1, field2, delta1, delta2, slope, back, flip,
        w1, w2, v1, v2, cwp, coarse_t, table, hot, spread, perm, proj, patch,
        acc1, acc2, shift, pool, stage, colf, hcolf,
        ask, asked, askrow, askedrow, reply, arrived, placed, gathered,
        rows1, cols1, hrow1, hcol1, hcor1,
        rows2, cols2, hrow2, hcol2, hcor2,
        rows3, cols3, hrow3, hcol3, hcor3,
        rows4, cols4, hrow4, hcol4, hcor4,
        p1, p1in, p1mid, p1all, p2, p2in, p2mid, p2all,
        q, qin, qmid, qall,
        local_sem, row_send, row_recv, col_send, col_recv, halo_send, halo_recv, back_send, back_recv, core_send, core_recv,
    ) = refs[16:]
    r, c = lax.axis_index("row"), lax.axis_index("col")
    here = (r, c)
    pairs1, width1 = fine.shape[0], fine.shape[2]
    pairs2, width2 = pairs1 // 2, width1 // 2
    listed = ids.shape[1]
    places = nr * SLOT
    ncoarse = coarse.shape[1]
    nblocks = ncoarse // CB

    loads = [
        pltpu.make_async_copy(source, target, local_sem.at[k])
        for k, (source, target) in enumerate(
            (
                (cw_h, cw), (coarse_h, coarse), (k1_h, k1), (interp_h, interp),
                (fine_h, fine), (k2_h, k2), (c2_h, cot2), (c1_h, cot1),
            )
        )
    ]
    for load in loads:
        load.start()

    barrier = pltpu.get_barrier_semaphore()

    def greet(row, col):
        pl.semaphore_signal(barrier, inc=1, device_id=(row, col), device_id_type=MESH)

    for step in range(1, nc):
        greet(r, lax.rem(c + step, nc))
    for step in range(1, nr):
        greet(lax.rem(r + step, nr), c)

    live_total = live[0, 0]
    owner = [lax.shift_right_logical(ids[0, k], jnp.int32(nblocks.bit_length() - 1)) for k in range(listed)]
    local = [ids[0, k] - owner[k] * nblocks for k in range(listed)]
    place = []
    for k in range(listed):
        rank = jnp.int32(0)
        for j in range(k):
            rank = rank + jnp.where(owner[j] == owner[k], 1, 0)
        place.append(jnp.where(k < live_total, owner[k] * CAP + rank, -1))
    row_at = iota((places, 128), 0)
    row_place = lax.shift_right_logical(row_at, 3)
    row_sub = row_at - row_place * CB
    wanted = jnp.full((places, 128), -1, jnp.int32)
    for k in range(listed):
        wanted = jnp.where(row_place == place[k], local[k] * CB + row_sub, wanted)
    ask[...] = wanted.astype(F32).reshape(ask.shape)
    list_at = iota((listed * CB, 128), 0)
    list_slot = lax.shift_right_logical(list_at, 3)
    list_sub = list_at - list_slot * CB
    target = jnp.full((listed * CB, 128), -1, jnp.int32)
    for k in range(listed):
        found = jnp.where(place[k] >= 0, place[k] * CB, -CB)
        target = jnp.where(list_slot == k, found + list_sub, target)
    lanes = iota((listed * CB, 128), 1)
    for j in range(places // 128):
        perm[:, j * 128 : j * 128 + 128] = jnp.where(target == lanes + j * 128, 1.0, 0.0).astype(BF)

    loads[0].wait()
    loads[1].wait()
    cwp[...] = jnp.zeros_like(cwp)
    cwp[0 : cw.shape[0], :] = cw[...].astype(F32)
    coarse_t[...] = jnp.zeros_like(coarse_t)
    weight = cwp[...].astype(BF)

    def project(k, carry):
        at = pl.ds(pl.multiple_of(k * 512, 512), 512)
        coarse_t[0 : coarse.shape[0], :] = coarse[:, at].astype(F32)
        part = coarse_t[...].T.astype(BF)
        table[at, 0:128] = dot(part, weight).astype(BF)
        table[at, 128:256] = part
        return carry

    lax.fori_loop(0, ncoarse // 512, project, 0)
    loads[2].wait()
    pair_weights(k1, w1, False)

    loads[5].wait()
    pair_weights(k1, v1, True)
    pair_weights(k2, w2, False)
    pair_weights(k2, v2, True)
    loads[3].wait()

    def turn(pair, carry):
        at = pl.ds(pl.multiple_of(pair * width1, width1), width1)
        for side in range(2):
            flip[side, :, at] = interp[pair, side].astype(F32).T.astype(BF)
        return carry

    lax.fori_loop(0, pairs1, turn, 0)
    shift[...] = jnp.zeros_like(shift)


    pl.semaphore_wait(barrier, nr - 1 + nc - 1)

    row = lambda k, source, dest: Push(here, 0, nr, source, dest, row_send.at[k], row_recv.at[k])
    col = lambda k, source, dest: Push(here, 1, nc, source, dest, col_send.at[k], col_recv.at[k])
    halo = lambda k, *bufs: Halo(here, counts, *bufs, halo_send.at[k], halo_recv.at[k])
    masks = (
        jnp.where(r > 0, 1.0, 0.0),
        jnp.where(r < nr - 1, 1.0, 0.0),
        jnp.where(c > 0, 1.0, 0.0),
        jnp.where(c < nc - 1, 1.0, 0.0),
    )

    push_ask = row(0, lambda peer: ask.at[peer], asked)
    push_ask.start()
    asked[r] = ask[r]

    push_ask.wait_recv()
    every = asked[...].reshape(places, 128)
    lane_f = iota((places, 128), 1).astype(F32)

    def heat(k, carry):
        base = (k * 128).astype(F32)
        hot[k] = jnp.where(every == lane_f + base, 1.0, 0.0).astype(BF)
        return carry

    lax.fori_loop(0, ncoarse // 128, heat, 0)
    gathered_rows = jnp.zeros((places, 256), F32)

    def gather(k, carry):
        pieces = [hot[k * 4 + j] for j in range(4)]
        return carry + dot(
            jnp.concatenate(pieces, axis=1), table[pl.ds(pl.multiple_of(k * 512, 512), 512), :]
        )

    gathered_rows = lax.fori_loop(0, ncoarse // 512, gather, gathered_rows)
    reply[...] = gathered_rows.astype(BF).reshape(reply.shape)
    push_reply = row(1, lambda peer: reply.at[peer], arrived)
    push_reply.start()
    arrived[r] = reply[r]
    askrow[...] = every.T[0:8, :]
    push_row = col(0, lambda peer: askrow, askedrow)
    push_row.start()
    askedrow[c] = askrow[...]

    push_reply.wait_recv()
    both = dot(perm[...], arrived[...].reshape(places, 256)).astype(BF)
    proj[...] = both[:, 0:128]
    patch[...] = both[:, 128:256]
    loads[4].wait()

    for half in range(2):
        at = pl.ds(half * (width1 - 16), 16)
        value = dot(interp[:, :, at, :].reshape(pairs1 * 32, 128), proj[...])
        pool[...] = value + fine[:, :, at, :].reshape(pairs1 * 32, 128).astype(F32)
        cols1[half] = pool[pl.ds(15 * half, 2 * pairs1, stride=16), :].astype(BF)
        at = (half * (pairs1 - 1), half)
        rows1[half] = (dot(interp[at], proj[...]) + fine[at].astype(F32)).astype(BF)
    halo1 = halo(0, rows1, cols1, hrow1, hcol1, hcor1)
    halo1.start()

    def condition(k, carry):
        for j in range(4):
            pair = k * 4 + j
            value = dot(interp[pair].reshape(2 * width1, 128), proj[...])
            value = value + fine[pair].reshape(2 * width1, 128).astype(F32)
            for side in range(2):
                line = value[side * width1 : (side + 1) * width1]
                put_row(field1, pair + side, 1 - side, line, shift.at[2 * j + side])
        return carry

    lax.fori_loop(0, pairs1 // 4, condition, 0)
    halo1.wait_recv()
    set_halo(field1, hrow1, hcol1, hcor1, hcolf, masks, shift.at[0])

    middle = width1 - 32
    inner = middle // 2

    def level_one(pair, count, cols):
        lane_rows = [field1[pl.ds(pair + j, count), cols, :].reshape(-1, 768) for j in range(2)]
        y, grade = activate(dot(jnp.concatenate(lane_rows, axis=1), w1[...]))
        cells = y.shape[0]
        slope[pl.ds(pair, count), cols, :] = grade.reshape(count, cells // count, 256)
        pool[0:cells] = y[:, 0:128] + y[:, 128:256]
        total = pool[pl.ds(0, cells // 2, stride=2), :] + pool[pl.ds(1, cells // 2, stride=2), :]
        return total * 0.25

    for half in range(2):
        total = level_one(0, pairs1, pl.ds(half * (width1 - 16), 16))
        pool[0 : pairs1 * 8] = total
        cols2[half] = pool[pl.ds(7 * half, pairs1, stride=8), :].astype(BF)
        stage[1 : pairs1 + 1, 8 + half * (width2 - 8) : 16 + half * (width2 - 8), :] = total.reshape(
            pairs1, 8, 128
        )
    for half in range(2):
        at = half * (pairs1 - 1)
        stage[at + 1, 16 : 16 + inner, :] = level_one(at, 1, pl.ds(16, middle))
        rows2[half] = stage[at + 1, 8 : 8 + width2, :].astype(BF)
    halo2 = halo(1, rows2, cols2, hrow2, hcol2, hcor2)
    halo2.start()
    step1 = (pairs1 - 2) // 3

    def level_one_inner(k, carry):
        pair = 1 + k * step1
        total = level_one(pair, step1, pl.ds(16, middle))
        stage[pl.ds(pair + 1, step1), 16 : 16 + inner, :] = total.reshape(step1, inner, 128)
        return carry

    lax.fori_loop(0, 3, level_one_inner, 0)
    half = pl.ds(0, 2 * pairs2)
    loads[6].wait()
    halo2.wait_recv()
    north, south, west, east = masks
    for k, up in ((0, north), (1, south)):
        at = k * (pairs1 + 1)
        stage[at, 8 : 8 + width2, :] = hrow2[k].astype(F32) * up
        stage[at, 7:8, :] = hcor2[2 * k].astype(F32)[15:16] * (up * west)
        stage[at, 8 + width2 : 9 + width2, :] = hcor2[2 * k + 1].astype(F32)[0:1] * (up * east)
    hcolf[0, half] = hcol2[0].astype(F32) * west
    hcolf[1, half] = hcol2[1].astype(F32) * east

    def edge_cells(k, carry):
        stage[k + 1, 7:8, :] = hcolf[0, pl.ds(k, 1), :]
        stage[k + 1, 8 + width2 : 9 + width2, :] = hcolf[1, pl.ds(k, 1), :]
        return carry

    lax.fori_loop(0, pairs1, edge_cells, 0)

    def lay_out(pair, carry):
        for side in range(2):
            for j in range(3):
                lane = side * 384 + j * 128
                line = stage[2 * pair + side, 7 + j : 7 + j + width2, :]
                field2[pair, :, lane : lane + 128] = line.astype(BF)
        return carry

    lax.fori_loop(0, pairs2 + 1, lay_out, 0)

    def level_two(k, carry):
        pair = k * 8
        z = dot(jnp.concatenate(windows(field2, pair, 8), axis=1), w2[...])
        y, grade = activate(z)
        for side in range(2):
            lane = slice(side * 128, side * 128 + 128)
            skip[pl.ds(pair, 8), side] = y[:, lane].astype(BF).reshape(8, width2, 128)
            value = cot2[pl.ds(pair, 8), side].astype(F32) * grade[:, lane].reshape(8, width2, 128)
            for j in range(8):
                at = pl.ds(2 * (pair + j) + side, 1)
                colf[0, at, :] = value[j, 0:1]
                colf[1, at, :] = value[j, width2 - 1 : width2]
                put_row(delta2, pair + j + side, 1 - side, value[j], shift.at[j])
        return carry

    lax.fori_loop(0, pairs2 // 8, level_two, 0)
    skip_out = pltpu.make_async_copy(skip, skip_h, local_sem.at[8])
    skip_out.start()
    take_edges(delta2, rows3, cols3, colf.at[:, half])
    halo3 = halo(2, rows3, cols3, hrow3, hcol3, hcor3)
    halo3.start()

    def tap_grad(field, delta, acc, step):
        count = step // field.shape[1]

        def body(k, carry):
            outer = jnp.concatenate(centres(delta, k * count, count), axis=1)
            for i, window in enumerate(windows(field, k * count, count)):
                acc[i] += lax.dot_general(outer, window, CONTRACT0, preferred_element_type=F32)
            return carry

        acc[...] = jnp.zeros_like(acc)
        lax.fori_loop(0, (field.shape[0] - 1) // count, body, 0)

    push_row.wait_recv()

    def spot(k, carry):
        at = pl.ds(pl.multiple_of(k * 256, 256), 256)
        number = iota((256, places), 0).astype(F32) + (k * 256).astype(F32)
        for j in range(nc):
            match = number == askedrow[j, 0:1, :]
            spread[j, at, :] = jnp.where(match, 1.0, 0.0).astype(BF)
        return carry

    lax.fori_loop(0, ncoarse // 256, spot, 0)

    tap_grad(field2, delta2, acc2, 1024)
    tap_sums(acc2, p2)

    class Total:
        def __init__(self, k, parts, held, middle, full):
            self.parts, self.held, self.middle, self.full = parts, held, middle, full
            self.size = parts.shape[0] // nr
            block = lambda peer: parts.at[pl.ds(peer * self.size, self.size)]
            self.first = row(k, block, held)
            self.second = col(k - 1, lambda peer: middle.at[c], middle)
            self.third = row(k + 1, lambda peer: full.at[r], full)

        def scatter(self):
            self.first.start()
            self.held[r] = self.parts[pl.ds(r * self.size, self.size)]

        def exchange(self):
            self.first.wait_recv()
            total = self.held[0].astype(F32)
            for k in range(1, nr):
                total = total + self.held[k].astype(F32)
            self.middle[c] = total.astype(self.middle.dtype)
            self.second.start()

        def gather(self):
            self.second.wait_recv()
            total = self.middle[0].astype(F32)
            for k in range(1, nc):
                total = total + self.middle[k].astype(F32)
            self.full[r] = total.astype(self.full.dtype)
            self.third.start()

        def finish(self):
            self.third.wait_recv()

        def wait_send(self):
            self.first.wait_send()
            self.second.wait_send()
            self.third.wait_send()

    sum2 = Total(2, p2, p2in, p2mid, p2all)
    sum1 = Total(4, p1, p1in, p1mid, p1all)
    sumq = Total(6, q, qin, qmid, qall)
    sum2.scatter()

    halo3.wait_recv()
    set_halo(delta2, hrow3, hcol3, hcor3, hcolf.at[:, half], masks, shift.at[0])

    def back_two(k, carry):
        z = dot(jnp.concatenate(windows(delta2, k * 8, 8), axis=1), v2[...]) * 0.25
        back[pl.ds(k * 8, 8)] = z.reshape(8, width2, 256)
        return carry

    lax.fori_loop(0, pairs2 // 8, back_two, 0)
    loads[7].wait()

    def delta_one(k, carry):
        for j in range(2):
            pair = k * 2 + j
            line = back[k, :, j * 128 : j * 128 + 128]
            base = j * width1
            pool[pl.ds(base, width2, stride=2), :] = line
            pool[pl.ds(base + 1, width2, stride=2), :] = line
            wide = pool[base : base + width1]
            for side in range(2):
                grade = slope[pair, :, side * 128 : side * 128 + 128]
                value = (cot1[pair, side].astype(F32) + wide) * grade
                at = pl.ds(2 * pair + side, 1)
                colf[0, at, :] = value[0:1]
                colf[1, at, :] = value[width1 - 1 : width1]
                put_row(delta1, pair + side, 1 - side, value, shift.at[2 * j + side])
        return carry

    lax.fori_loop(0, pairs1 // 2, delta_one, 0)
    take_edges(delta1, rows4, cols4, colf)
    halo4 = halo(3, rows4, cols4, hrow4, hcol4, hcor4)
    halo4.start()
    sum2.exchange()
    tap_grad(field1, delta1, acc1, 2048)
    tap_sums(acc1, p1)
    sum1.scatter()
    sum2.gather()
    halo4.wait_recv()
    set_halo(delta1, hrow4, hcol4, hcor4, hcolf, masks, shift.at[0])

    def input_grad(k, carry):
        z = dot(jnp.concatenate(windows(delta1, k * 16, 16), axis=1), v1[...]).astype(BF)
        for side in range(2):
            gin[pl.ds(k * 16, 16), side] = z[:, side * 128 : side * 128 + 128].reshape(16, width1, 128)
        return carry

    lax.fori_loop(0, pairs1 // 16, input_grad, 0)

    def list_grad(k, carry):
        at = pl.ds(pl.multiple_of(k * 8 * width1, 8 * width1), 8 * width1)
        for side in range(2):
            part = gin[pl.ds(k * 8, 8), side].reshape(8 * width1, 128)
            carry = carry + dot(flip[side, :, at], part)
        return carry

    gpacc = lax.fori_loop(0, pairs1 // 8, list_grad, jnp.zeros((128, 128), F32))
    gin_out = pltpu.make_async_copy(gin, gin_h, local_sem.at[9])
    gin_out.start()

    gproj = gpacc.astype(BF)
    q[...] = lax.dot_general(patch[...], gproj, CONTRACT0, preferred_element_type=F32).reshape(q.shape)
    sumq.scatter()
    gpatch = lax.dot_general(gproj, weight, CONTRACT1, preferred_element_type=F32).astype(BF)
    moved = lax.dot_general(perm[...], gpatch, CONTRACT0, preferred_element_type=F32)
    placed[...] = moved.astype(BF).reshape(placed.shape)
    push_back = Back(
        here, counts, placed, gathered, back_send, back_recv, core_send, core_recv
    )
    push_back.start()
    gathered[c, r] = placed[r]
    sum1.exchange()
    sum2.finish()
    p2_out = pltpu.make_async_copy(p2all, p2_h, local_sem.at[10])
    p2_out.start()
    sumq.exchange()
    push_back.forward()
    sum1.gather()
    started = []

    def scatter(slots):
        if not slots:
            return
        parts = jnp.concatenate([gathered[slot].reshape(places, 128) for slot in slots], axis=0)
        first = not started
        started.append(slots)

        def body(k, carry):
            at = pl.ds(pl.multiple_of(k * 1024, 1024), 1024)
            value = dot(jnp.concatenate([spread[slot, at, :] for slot in slots], axis=1), parts)
            gcoarse[at, :] = value if first else gcoarse[at, :] + value
            return carry

        lax.fori_loop(0, ncoarse // 1024, body, 0)

    scatter(push_back.slots(push_back.core))
    sumq.gather()
    push_back.wait_across()
    scatter(push_back.slots(1 - push_back.core))
    gcoarse_out = pltpu.make_async_copy(gcoarse, gcoarse_h, local_sem.at[11])
    gcoarse_out.start()
    sum1.finish()
    p1_out = pltpu.make_async_copy(p1all, p1_h, local_sem.at[12])
    p1_out.start()
    sumq.finish()
    gcond_out = pltpu.make_async_copy(qall, gcond_h, local_sem.at[13])
    gcond_out.start()

    for sent in (
        push_ask, push_reply, push_row, halo1, halo2, halo3, halo4, sum2, sum1, push_back,
        sumq,
    ):
        sent.wait_send()
    for out in (skip_out, gin_out, p2_out, gcoarse_out, p1_out, gcond_out):
        out.wait()


def finish_kernel(skip_k, gin_k, p1_k, p2_k, gcond_k, gcoarse_k, *refs):
    skip_h, gin_h, g1_h, g2_h, gcond_h, gcoarse_h = refs[:6]
    skip, gin, p1, p2, qs, held, g1, g2, gcond, gcoarse, sem = refs[6:]
    quarter = gin.shape[0] // 4
    parts = [pl.ds(k * quarter, quarter) for k in range(4)]
    loads = [
        pltpu.make_async_copy(source, target, sem.at[k])
        for k, (source, target) in enumerate(
            (
                (gcoarse_k, held), (skip_k, skip), (p2_k, p2), (p1_k, p1), (gcond_k, qs),
                *((gin_k.at[part], gin.at[part]) for part in parts),
            )
        )
    ]
    for load in loads:
        load.start()
    outs = []

    def store(source, target):
        copy = pltpu.make_async_copy(source, target, sem.at[16 + len(outs)])
        copy.start()
        outs.append(copy)

    loads[0].wait()
    for k in range(held.shape[0] // 128):
        at = slice(k * 128, k * 128 + 128)
        gcoarse[:, at] = held[at, :].T[0 : gcoarse.shape[0], :]
    store(gcoarse, gcoarse_h)
    loads[1].wait()
    store(skip, skip_h)
    for load, part in zip(loads[5:], parts):
        load.wait()
        store(gin.at[part], gin_h.at[part])
    loads[2].wait()
    g2[...] = p2[0 : g2.shape[0]].astype(F32)
    store(g2, g2_h)
    loads[3].wait()
    g1[...] = p1[0 : g1.shape[0]].astype(F32)
    store(g1, g1_h)
    loads[4].wait()
    gcond[...] = qs[0 : gcond.shape[0], :]
    store(gcond, gcond_h)
    for out in outs:
        out.wait()


def per_device(counts, fine, interp, ids, live, coarse, cw, conv_one, conv_two, cot_one, cot_two):
    nr, nc = counts
    height, width, channels = fine.shape
    pairs1, pairs2, width2 = height // 2, height // 4, width // 2
    cch, ncoarse = coarse.shape[1], coarse.shape[0]
    listed = ids.shape[-1]
    places = nr * SLOT
    blocks = -(-72 // nr) * nr
    any_space = pl.BlockSpec(memory_space=pl.ANY)
    smem = pl.BlockSpec(memory_space=pltpu.SMEM)
    vm = pltpu.VMEM
    chunk = blocks // nr

    def halo_bufs(rows, cols):
        return [
            vm((2, cols, 128), BF), vm((2, rows, 128), BF),
            vm((2, cols, 128), BF), vm((2, rows, 128), BF), vm((4, 16, 128), BF),
        ]

    def sum_bufs():
        return [
            vm((blocks, 16, 128), BF), vm((nr, chunk, 16, 128), BF), vm((nc, chunk, 16, 128), BF),
            vm((nr, chunk, 16, 128), BF),
        ]

    scratch = [
        vm((pairs1, 2, width, 128), BF), vm((pairs1, 2, width, 128), BF), vm((cch, ncoarse), BF),
        vm(cw.shape, BF), vm((9, 128, 128), BF), vm((9, 128, 128), BF),
        vm((pairs1, 2, width, 128), BF), vm((pairs2, 2, width2, 128), BF),
        vm((pairs2, 2, width2, 128), BF), vm((pairs1, 2, width, 128), BF),
        vm((ncoarse, 128), F32),
        vm((pairs1 + 1, width, 768), BF), vm((pairs2 + 1, width2, 768), BF),
        vm((pairs1 + 1, width, 768), BF), vm((pairs2 + 1, width2, 768), BF),
        vm((pairs1, width, 256), F32), vm((pairs2, width2, 256), F32), vm((2, 128, pairs1 * width), BF),
        vm((1536, 256), BF), vm((1536, 256), BF), vm((1536, 256), BF), vm((1536, 256), BF),
        vm((128, 128), F32), vm((128, 512), F32), vm((ncoarse, 256), BF),
        vm((ncoarse // 128, places, 128), BF), vm((nc, ncoarse, places), BF),
        vm((listed * CB, places), BF), vm((listed * CB, 128), BF), vm((listed * CB, 128), BF),
        vm((2, 256, 768), F32), vm((2, 256, 768), F32),
        vm((8, width + 16, 128), F32), vm((8 * width, 128), F32), vm((pairs1 + 2, width2 + 16, 128), F32),
        vm((2, height, 128), F32), vm((2, height, 128), F32),
        vm((nr, SLOT, 128), F32), vm((nr, SLOT, 128), F32), vm((8, places), F32), vm((nc, 8, places), F32),
        vm((nr, SLOT, 256), BF), vm((nr, SLOT, 256), BF),
        vm((nr, SLOT, 128), BF), vm((nc, nr, SLOT, 128), BF),
        *halo_bufs(height, width), *halo_bufs(height // 2, width2),
        *halo_bufs(height // 2, width2), *halo_bufs(height, width),
        *sum_bufs(), *sum_bufs(),
        vm((nr, 128 // nr, 128), F32), vm((nr, 1, 128 // nr, 128), F32), vm((nc, 1, 128 // nr, 128), F32),
        vm((nr, 1, 128 // nr, 128), F32),
        pltpu.SemaphoreType.DMA((16,)),
        pltpu.SemaphoreType.DMA((8,)), pltpu.SemaphoreType.DMA((8,)),
        pltpu.SemaphoreType.DMA((7,)), pltpu.SemaphoreType.DMA((7,)),
        pltpu.SemaphoreType.DMA((4, 8)), pltpu.SemaphoreType.DMA((4, 8)),
        *[pltpu.SemaphoreType.DMA((nc // 2,))] * 4,
    ]
    shape = jax.ShapeDtypeStruct
    results = pl.pallas_call(
        functools.partial(kernel, counts),
        out_shape=(
            shape((pairs2, 2, width2, 128), BF),
            shape((pairs1, 2, width, 128), BF),
            shape((nr, chunk, 16, 128), BF),
            shape((nr, chunk, 16, 128), BF),
            shape((nr, 1, 128 // nr, 128), F32),
            shape((ncoarse, 128), F32),
        ),
        in_specs=[smem, smem] + [any_space] * 8,
        out_specs=(any_space,) * 6,
        scratch_shapes=scratch,
        compiler_params=pltpu.CompilerParams(
            collective_id=0, has_side_effects=True, vmem_limit_bytes=63 * 2**20
        ),
        cost_estimate=pl.CostEstimate(
            flops=10 * 10**9, bytes_accessed=13 * 10**6, transcendentals=2 * 10**6
        ),
    )(
        ids.reshape(1, listed),
        live.reshape(1, 1),
        fine.reshape(pairs1, 2, width, channels),
        interp.reshape(pairs1, 2, width, interp.shape[2]),
        coarse.T,
        cw,
        conv_one.reshape(9, 128, 128),
        conv_two.reshape(9, 128, 128),
        cot_one.reshape(pairs1, 2, width, channels),
        cot_two.reshape(pairs2, 2, width2, channels),
    )
    skip, gin, g1, g2, gcond, gcoarse = pl.pallas_call(
        finish_kernel,
        out_shape=(
            shape((pairs2, 2, width2, 128), BF),
            shape((pairs1, 2, width, 128), BF),
            shape((72, 16, 128), F32),
            shape((72, 16, 128), F32),
            shape((cch, 128), F32),
            shape((cch, ncoarse), F32),
        ),
        in_specs=[any_space] * 6,
        out_specs=(any_space,) * 6,
        scratch_shapes=[
            vm((pairs2, 2, width2, 128), BF), vm((pairs1, 2, width, 128), BF),
            vm((blocks, 16, 128), BF), vm((blocks, 16, 128), BF), vm((128, 128), F32), vm((ncoarse, 128), F32),
            vm((72, 16, 128), F32), vm((72, 16, 128), F32), vm((cch, 128), F32), vm((cch, ncoarse), F32),
            pltpu.SemaphoreType.DMA((32,)),
        ],
        compiler_params=pltpu.CompilerParams(vmem_limit_bytes=63 * 2**20),
        cost_estimate=pl.CostEstimate(flops=0, bytes_accessed=12 * 10**6, transcendentals=0),
    )(
        results[0],
        results[1],
        results[2].reshape(blocks, 16, 128),
        results[3].reshape(blocks, 16, 128),
        results[4].reshape(128, 128),
        results[5],
    )
    return (
        skip.reshape(height // 2, width2, 128),
        gin.reshape(height, width, 128),
        g1.reshape(3, 3, 128, 128),
        g2.reshape(3, 3, 128, 128),
        gcond,
        gcoarse.T,
    )


def solution(mesh):
    counts = (mesh.shape["row"], mesh.shape["col"])
    tiles = P("row", "col", None)
    return jax.shard_map(
        functools.partial(per_device, counts),
        mesh=mesh,
        in_specs=(tiles, tiles, tiles, P("row", "col"), P("row", None), P(), P(), P(), tiles, tiles),
        out_specs=(tiles, tiles, P(), P(), P(), P("row", None)),
        check_vma=False,
    )
```

```python
import functools

import jax
import jax.numpy as jnp
from jax import lax
from jax.experimental import pallas as pl
from jax.experimental.pallas import tpu as pltpu
from jax.sharding import PartitionSpec as P

MESH = pl.DeviceIdType.MESH
BF = jnp.bfloat16
F32 = jnp.float32
CB = 8
CAP = 2
SLOT = CAP * CB
CONTRACT0 = (((0,), (0,)), ((), ()))
CONTRACT1 = (((1,), (1,)), ((), ()))


def dot(left, right):
    return jnp.dot(left, right, preferred_element_type=F32)


def iota(shape, dim):
    return lax.broadcasted_iota(jnp.int32, shape, dim)


class Push:
    def __init__(self, coords, axis, count, source, target, send, recv):
        self.coords, self.axis, self.count = coords, axis, count
        self.source, self.target, self.send, self.recv = source, target, send, recv
        self.me = coords[axis]

    def device(self, index):
        return (index, self.coords[1]) if self.axis == 0 else (self.coords[0], index)

    def copy(self, step):
        peer = lax.rem(self.me + step, self.count)
        return pltpu.make_async_remote_copy(
            src_ref=self.source(peer),
            dst_ref=self.target.at[self.me],
            send_sem=self.send,
            recv_sem=self.recv,
            device_id=self.device(peer),
            device_id_type=MESH,
        )

    def all(self):
        blocks = self.target.at[pl.ds(0, self.count - 1)]
        return pltpu.make_async_remote_copy(
            src_ref=blocks,
            dst_ref=blocks,
            send_sem=self.send,
            recv_sem=self.recv,
            device_id=self.device(lax.rem(self.me + 1, self.count)),
            device_id_type=MESH,
        )

    def each(self, act):
        def body(step, carry):
            act(step)
            return carry

        lax.fori_loop(1, self.count, body, 0)

    def start(self):
        self.each(lambda step: self.copy(step).start())

    def wait_recv(self):
        self.all().wait_recv()

    def wait_send(self):
        self.all().wait_send()


class Back:
    def __init__(self, coords, counts, placed, gathered, send, recv, core_send, core_recv):
        self.row, self.c = coords
        self.rows, self.chips = counts[0], counts[1] // 2
        self.placed, self.gathered = placed, gathered
        self.send, self.recv, self.core_send, self.core_recv = send, recv, core_send, core_recv
        self.core = lax.rem(self.c, 2)
        self.chip = lax.div(self.c, 2)

    def slot(self, step, core):
        return lax.rem(self.chip + self.chips - step, self.chips) * 2 + core

    def along(self, step, place):
        row = lax.rem(self.row + place, self.rows)
        col = lax.rem(self.chip + step, self.chips) * 2 + self.core
        return pltpu.make_async_remote_copy(
            src_ref=self.placed.at[row],
            dst_ref=self.gathered.at[self.c, self.row],
            send_sem=self.send.at[step],
            recv_sem=self.recv.at[step],
            device_id=(row, col),
            device_id_type=MESH,
        )

    def all(self, step):
        blocks = self.placed.at[pl.ds(0, self.rows - 1 if step == 0 else self.rows)]
        return pltpu.make_async_remote_copy(
            src_ref=blocks,
            dst_ref=blocks,
            send_sem=self.send.at[step],
            recv_sem=self.recv.at[step],
            device_id=(lax.rem(self.row + 1, self.rows), self.c),
            device_id_type=MESH,
        )

    def across(self, step):
        at = self.slot(step, self.core)
        return pltpu.make_async_remote_copy(
            src_ref=self.gathered.at[at],
            dst_ref=self.gathered.at[at],
            send_sem=self.core_send.at[step],
            recv_sem=self.core_recv.at[step],
            device_id=(self.row, self.chip * 2 + 1 - self.core),
            device_id_type=MESH,
        )

    def each(self, step, act):
        def body(place, carry):
            act(place)
            return carry

        lax.fori_loop(1 if step == 0 else 0, self.rows, body, 0)

    def start(self):
        for step in reversed(range(self.chips)):
            self.each(step, lambda place: self.along(step, place).start())

    def forward(self):
        for step in range(self.chips):
            self.all(step).wait_recv()
            self.across(step).start()

    def slots(self, core):
        return [self.slot(step, core) for step in range(self.chips)]

    def wait_across(self):
        for step in range(self.chips):
            self.across(step).wait_recv()

    def wait_send(self):
        for step in range(self.chips):
            self.all(step).wait_send()
            self.across(step).wait_send()


class Halo:
    def __init__(self, coords, counts, rows, cols, hrow, hcol, hcor, send, recv):
        (r, c), (nr, nc) = coords, counts
        north, south = lax.rem(r + nr - 1, nr), lax.rem(r + 1, nr)
        west, east = lax.rem(c + nc - 1, nc), lax.rem(c + 1, nc)
        width = rows.shape[1]
        low, high = pl.ds(0, 16), pl.ds(width - 16, 16)
        plan = (
            (rows.at[0], hrow.at[1], (north, c)),
            (rows.at[1], hrow.at[0], (south, c)),
            (cols.at[0], hcol.at[1], (r, west)),
            (cols.at[1], hcol.at[0], (r, east)),
            (rows.at[0, low], hcor.at[3], (north, west)),
            (rows.at[0, high], hcor.at[2], (north, east)),
            (rows.at[1, low], hcor.at[1], (south, west)),
            (rows.at[1, high], hcor.at[0], (south, east)),
        )
        def copy(source, target, k, device):
            return pltpu.make_async_remote_copy(
                src_ref=source,
                dst_ref=target,
                send_sem=send.at[k],
                recv_sem=recv.at[k],
                device_id=device,
                device_id_type=MESH,
            )

        order = (4, 5, 6, 7, 0, 1, 2, 3)
        self.copies = [copy(*plan[k][:2], (0, 1, 2, 2)[k // 2], plan[k][2]) for k in order]
        self.waits = [copy(part, part, k, (north, c)) for k, part in enumerate((hrow, hcol, hcor))]

    def start(self):
        for copy in self.copies:
            copy.start()

    def wait_recv(self):
        for copy in self.waits:
            copy.wait_recv()

    def wait_send(self):
        for copy in self.waits:
            copy.wait_send()


def put_row(field, pair, side, value, scratch):
    width = value.shape[0]
    base = side * 384
    scratch[8 : 8 + width] = value
    field[pair, :, base : base + 128] = scratch[7 : 7 + width].astype(BF)
    field[pair, :, base + 128 : base + 256] = value.astype(BF)
    field[pair, :, base + 256 : base + 384] = scratch[9 : 9 + width].astype(BF)


def set_halo(field, hrow, hcol, hcor, hcolf, masks, scratch):
    north, south, west, east = masks
    pairs, width = field.shape[0] - 1, field.shape[1]
    for pair, side, k, up in ((0, 0, 0, north), (pairs, 1, 1, south)):
        scratch[7:8] = hcor[2 * k].astype(F32)[15:16] * (up * west)
        scratch[8 + width : 9 + width] = hcor[2 * k + 1].astype(F32)[0:1] * (up * east)
        put_row(field, pair, side, hrow[k].astype(F32) * up, scratch)
    hcolf[0] = hcol[0].astype(F32) * west
    hcolf[1] = hcol[1].astype(F32) * east
    place = iota((16, 128), 0)

    def body(pair, carry):
        for half, spot, sub, lane in ((0, 0, 0, 0), (1, width - 16, 15, 256)):
            for side in (1, 0):
                at = (
                    pair + 1 - side,
                    pl.ds(spot, 16),
                    pl.ds(side * 384 + lane, 128),
                )
                cell = hcolf[half, pl.ds(2 * pair + 1 - side, 1), :]
                field[at] = jnp.where(place == sub, cell, field[at].astype(F32)).astype(BF)
        return carry

    lax.fori_loop(0, pairs, body, 0)


def take_edges(field, rows, cols, colf):
    pairs = field.shape[0] - 1
    rows[0] = field[0, :, 512:640]
    rows[1] = field[pairs, :, 128:256]
    cols[0] = colf[0].astype(BF)
    cols[1] = colf[1].astype(BF)


def windows(field, at, count):
    width = field.shape[1]
    low = field[pl.ds(at, count)].reshape(count * width, 768)
    high = field[pl.ds(at + 1, count)].reshape(count * width, 768)
    return low, high


def centres(field, at, count):
    width = field.shape[1]
    even = field[pl.ds(at, count), :, 512:640].reshape(count * width, 128)
    odd = field[pl.ds(at + 1, count), :, 128:256].reshape(count * width, 128)
    return even, odd


def pair_weights(kernel, out, flipped):
    out[...] = jnp.zeros_like(out)
    for a in range(3):
        for b in range(3):
            if flipped:
                block = kernel[(2 - a) * 3 + 2 - b].astype(F32).T.astype(BF)
            else:
                block = kernel[a * 3 + b]
            for half in range(2):
                base = (a + half) * 384 + b * 128
                out[base : base + 128, half * 128 : half * 128 + 128] = block


def tap_sums(acc, out):
    for a in range(3):
        for b in range(3):
            total = None
            for half in range(2):
                i = a + half
                lane = (i % 2) * 384 + b * 128
                part = acc[i // 2, half * 128 : half * 128 + 128, lane : lane + 128]
                total = part if total is None else total + part
            t = a * 3 + b
            out[t * 8 : t * 8 + 8] = total.T.astype(BF).reshape(8, 16, 128)


def activate(z):
    sig = 0.5 + 0.5 * jnp.tanh(0.5 * z)
    y = z * sig
    return y, sig + y * (1.0 - sig)


def kernel(counts, *refs):
    nr, nc = counts
    (ids, live, fine_h, interp_h, coarse_h, cw_h, k1_h, k2_h, c1_h, c2_h) = refs[:10]
    (skip_h, gin_h, p1_h, p2_h, gcond_h, gcoarse_h) = refs[10:16]
    (
        fine, interp, coarse, cw, k1, k2, cot1, cot2,
        skip, gin, gcoarse,
        field1, field2, delta1, delta2, slope, back, flip,
        w1, w2, v1, v2, cwp, coarse_t, table, spread, perm, proj, patch,
        acc1, acc2, shift, pool, stage, colf, hcolf,
        ask, asked, askrow, askedrow, reply, arrived, placed, gathered,
        rows1, cols1, hrow1, hcol1, hcor1,
        rows2, cols2, hrow2, hcol2, hcor2,
        rows3, cols3, hrow3, hcol3, hcor3,
        rows4, cols4, hrow4, hcol4, hcor4,
        p1, p1in, p1mid, p1all, p2, p2in, p2mid, p2all,
        q, qin, qmid, qall,
        local_sem, row_send, row_recv, col_send, col_recv, halo_send, halo_recv, back_send, back_recv, core_send, core_recv,
    ) = refs[16:]
    r, c = lax.axis_index("row"), lax.axis_index("col")
    here = (r, c)
    pairs1, width1 = fine.shape[0], fine.shape[2]
    pairs2, width2 = pairs1 // 2, width1 // 2
    listed = ids.shape[1]
    places = nr * SLOT
    ncoarse = coarse.shape[1]
    nblocks = ncoarse // CB

    loads = [
        pltpu.make_async_copy(source, target, local_sem.at[k])
        for k, (source, target) in enumerate(
            (
                (cw_h, cw), (coarse_h, coarse), (k1_h, k1), (interp_h, interp),
                (fine_h, fine), (k2_h, k2), (c2_h, cot2), (c1_h, cot1),
            )
        )
    ]
    for load in loads:
        load.start()

    barrier = pltpu.get_barrier_semaphore()

    def greet(row, col):
        pl.semaphore_signal(barrier, inc=1, device_id=(row, col), device_id_type=MESH)

    for step in range(1, nc):
        greet(r, lax.rem(c + step, nc))
    for step in range(1, nr):
        greet(lax.rem(r + step, nr), c)

    live_total = live[0, 0]
    owner = [lax.shift_right_logical(ids[0, k], jnp.int32(nblocks.bit_length() - 1)) for k in range(listed)]
    local = [ids[0, k] - owner[k] * nblocks for k in range(listed)]
    place = []
    for k in range(listed):
        rank = jnp.int32(0)
        for j in range(k):
            rank = rank + jnp.where(owner[j] == owner[k], 1, 0)
        place.append(jnp.where(k < live_total, owner[k] * CAP + rank, -1))
    row_at = iota((places, 128), 0)
    row_place = lax.shift_right_logical(row_at, 3)
    row_sub = row_at - row_place * CB
    wanted = jnp.full((places, 128), -1, jnp.int32)
    for k in range(listed):
        wanted = jnp.where(row_place == place[k], local[k] * CB + row_sub, wanted)
    ask[...] = wanted.astype(F32).reshape(ask.shape)
    list_at = iota((listed * CB, 128), 0)
    list_slot = lax.shift_right_logical(list_at, 3)
    list_sub = list_at - list_slot * CB
    target = jnp.full((listed * CB, 128), -1, jnp.int32)
    for k in range(listed):
        found = jnp.where(place[k] >= 0, place[k] * CB, -CB)
        target = jnp.where(list_slot == k, found + list_sub, target)
    lanes = iota((listed * CB, 128), 1)
    for j in range(places // 128):
        perm[:, j * 128 : j * 128 + 128] = jnp.where(target == lanes + j * 128, 1.0, 0.0).astype(BF)

    loads[0].wait()
    loads[1].wait()
    cwp[...] = jnp.zeros_like(cwp)
    cwp[0 : cw.shape[0], :] = cw[...].astype(F32)
    coarse_t[...] = jnp.zeros_like(coarse_t)
    weight = cwp[...].astype(BF)

    def project(k, carry):
        at = pl.ds(pl.multiple_of(k * 512, 512), 512)
        coarse_t[0 : coarse.shape[0], :] = coarse[:, at].astype(F32)
        part = coarse_t[...].T.astype(BF)
        table[at, 0:128] = dot(part, weight).astype(BF)
        table[at, 128:256] = part
        return carry

    lax.fori_loop(0, ncoarse // 512, project, 0)
    loads[2].wait()
    pair_weights(k1, w1, False)

    loads[5].wait()
    pair_weights(k1, v1, True)
    pair_weights(k2, w2, False)
    pair_weights(k2, v2, True)
    loads[3].wait()

    def turn(pair, carry):
        at = pl.ds(pl.multiple_of(pair * width1, width1), width1)
        for side in range(2):
            flip[side, :, at] = interp[pair, side].astype(F32).T.astype(BF)
        return carry

    lax.fori_loop(0, pairs1, turn, 0)
    shift[...] = jnp.zeros_like(shift)


    pl.semaphore_wait(barrier, nr - 1 + nc - 1)

    row = lambda k, source, dest: Push(here, 0, nr, source, dest, row_send.at[k], row_recv.at[k])
    col = lambda k, source, dest: Push(here, 1, nc, source, dest, col_send.at[k], col_recv.at[k])
    halo = lambda k, *bufs: Halo(here, counts, *bufs, halo_send.at[k], halo_recv.at[k])
    masks = (
        jnp.where(r > 0, 1.0, 0.0),
        jnp.where(r < nr - 1, 1.0, 0.0),
        jnp.where(c > 0, 1.0, 0.0),
        jnp.where(c < nc - 1, 1.0, 0.0),
    )

    push_ask = row(0, lambda peer: ask.at[peer], asked)
    push_ask.start()
    asked[r] = ask[r]

    push_ask.wait_recv()
    every = asked[...].reshape(places, 128)
    lane_f = iota((places, 128), 1).astype(F32)

    def gather(k, carry):
        base = (k * 512).astype(F32)
        pieces = [jnp.where(every == lane_f + (base + j * 128.0), 1.0, 0.0).astype(BF) for j in range(4)]
        return carry + dot(
            jnp.concatenate(pieces, axis=1), table[pl.ds(pl.multiple_of(k * 512, 512), 512), :]
        )

    gathered_rows = lax.fori_loop(0, ncoarse // 512, gather, jnp.zeros((places, 256), F32))
    reply[...] = gathered_rows.astype(BF).reshape(reply.shape)
    push_reply = row(1, lambda peer: reply.at[peer], arrived)
    push_reply.start()
    arrived[r] = reply[r]
    askrow[...] = every.T[0:8, :]
    push_row = col(0, lambda peer: askrow, askedrow)
    push_row.start()
    askedrow[c] = askrow[...]

    push_reply.wait_recv()
    both = dot(perm[...], arrived[...].reshape(places, 256)).astype(BF)
    proj[...] = both[:, 0:128]
    patch[...] = both[:, 128:256]
    loads[4].wait()

    for half in range(2):
        at = pl.ds(half * (width1 - 16), 16)
        value = dot(interp[:, :, at, :].reshape(pairs1 * 32, 128), proj[...])
        pool[...] = value + fine[:, :, at, :].reshape(pairs1 * 32, 128).astype(F32)
        cols1[half] = pool[pl.ds(15 * half, 2 * pairs1, stride=16), :].astype(BF)
        at = (half * (pairs1 - 1), half)
        rows1[half] = (dot(interp[at], proj[...]) + fine[at].astype(F32)).astype(BF)
    halo1 = halo(0, rows1, cols1, hrow1, hcol1, hcor1)
    halo1.start()

    def condition(k, carry):
        for j in range(4):
            pair = k * 4 + j
            value = dot(interp[pair].reshape(2 * width1, 128), proj[...])
            value = value + fine[pair].reshape(2 * width1, 128).astype(F32)
            for side in range(2):
                line = value[side * width1 : (side + 1) * width1]
                put_row(field1, pair + side, 1 - side, line, shift.at[2 * j + side])
        return carry

    lax.fori_loop(0, pairs1 // 4, condition, 0)
    halo1.wait_recv()
    set_halo(field1, hrow1, hcol1, hcor1, hcolf, masks, shift.at[0])

    middle = width1 - 32
    inner = middle // 2

    def level_one(pair, count, cols):
        lane_rows = [field1[pl.ds(pair + j, count), cols, :].reshape(-1, 768) for j in range(2)]
        y, grade = activate(dot(jnp.concatenate(lane_rows, axis=1), w1[...]))
        cells = y.shape[0]
        slope[pl.ds(pair, count), cols, :] = grade.reshape(count, cells // count, 256)
        pool[0:cells] = y[:, 0:128] + y[:, 128:256]
        total = pool[pl.ds(0, cells // 2, stride=2), :] + pool[pl.ds(1, cells // 2, stride=2), :]
        return total * 0.25

    for half in range(2):
        total = level_one(0, pairs1, pl.ds(half * (width1 - 16), 16))
        pool[0 : pairs1 * 8] = total
        cols2[half] = pool[pl.ds(7 * half, pairs1, stride=8), :].astype(BF)
        stage[1 : pairs1 + 1, 8 + half * (width2 - 8) : 16 + half * (width2 - 8), :] = total.reshape(
            pairs1, 8, 128
        )
    for half in range(2):
        at = half * (pairs1 - 1)
        stage[at + 1, 16 : 16 + inner, :] = level_one(at, 1, pl.ds(16, middle))
        rows2[half] = stage[at + 1, 8 : 8 + width2, :].astype(BF)
    halo2 = halo(1, rows2, cols2, hrow2, hcol2, hcor2)
    halo2.start()
    step1 = (pairs1 - 2) // 3

    def level_one_inner(k, carry):
        pair = 1 + k * step1
        total = level_one(pair, step1, pl.ds(16, middle))
        stage[pl.ds(pair + 1, step1), 16 : 16 + inner, :] = total.reshape(step1, inner, 128)
        return carry

    lax.fori_loop(0, 3, level_one_inner, 0)
    half = pl.ds(0, 2 * pairs2)
    loads[6].wait()
    halo2.wait_recv()
    north, south, west, east = masks
    for k, up in ((0, north), (1, south)):
        at = k * (pairs1 + 1)
        stage[at, 8 : 8 + width2, :] = hrow2[k].astype(F32) * up
        stage[at, 7:8, :] = hcor2[2 * k].astype(F32)[15:16] * (up * west)
        stage[at, 8 + width2 : 9 + width2, :] = hcor2[2 * k + 1].astype(F32)[0:1] * (up * east)
    hcolf[0, half] = hcol2[0].astype(F32) * west
    hcolf[1, half] = hcol2[1].astype(F32) * east

    def edge_cells(k, carry):
        stage[k + 1, 7:8, :] = hcolf[0, pl.ds(k, 1), :]
        stage[k + 1, 8 + width2 : 9 + width2, :] = hcolf[1, pl.ds(k, 1), :]
        return carry

    lax.fori_loop(0, pairs1, edge_cells, 0)

    def lay_out(pair, carry):
        for side in range(2):
            for j in range(3):
                lane = side * 384 + j * 128
                line = stage[2 * pair + side, 7 + j : 7 + j + width2, :]
                field2[pair, :, lane : lane + 128] = line.astype(BF)
        return carry

    lax.fori_loop(0, pairs2 + 1, lay_out, 0)

    def level_two(k, carry):
        pair = k * 8
        z = dot(jnp.concatenate(windows(field2, pair, 8), axis=1), w2[...])
        y, grade = activate(z)
        for side in range(2):
            lane = slice(side * 128, side * 128 + 128)
            skip[pl.ds(pair, 8), side] = y[:, lane].astype(BF).reshape(8, width2, 128)
            value = cot2[pl.ds(pair, 8), side].astype(F32) * grade[:, lane].reshape(8, width2, 128)
            for j in range(8):
                at = pl.ds(2 * (pair + j) + side, 1)
                colf[0, at, :] = value[j, 0:1]
                colf[1, at, :] = value[j, width2 - 1 : width2]
                put_row(delta2, pair + j + side, 1 - side, value[j], shift.at[j])
        return carry

    lax.fori_loop(0, pairs2 // 8, level_two, 0)
    skip_out = pltpu.make_async_copy(skip, skip_h, local_sem.at[8])
    skip_out.start()
    take_edges(delta2, rows3, cols3, colf.at[:, half])
    halo3 = halo(2, rows3, cols3, hrow3, hcol3, hcor3)
    halo3.start()

    def tap_grad(field, delta, acc, step):
        count = step // field.shape[1]

        def body(k, carry):
            outer = jnp.concatenate(centres(delta, k * count, count), axis=1)
            for i, window in enumerate(windows(field, k * count, count)):
                acc[i] += lax.dot_general(outer, window, CONTRACT0, preferred_element_type=F32)
            return carry

        acc[...] = jnp.zeros_like(acc)
        lax.fori_loop(0, (field.shape[0] - 1) // count, body, 0)

    push_row.wait_recv()

    def spot(k, carry):
        at = pl.ds(pl.multiple_of(k * 256, 256), 256)
        number = iota((256, places), 0).astype(F32) + (k * 256).astype(F32)
        for j in range(nc):
            match = number == askedrow[j, 0:1, :]
            spread[j, at, :] = jnp.where(match, 1.0, 0.0).astype(BF)
        return carry

    lax.fori_loop(0, ncoarse // 256, spot, 0)

    tap_grad(field2, delta2, acc2, 1024)
    tap_sums(acc2, p2)

    class Total:
        def __init__(self, outer, inner, numbers, parts, held, middle, full):
            (push, self.me, self.count), (cross, self.other, self.others) = outer, inner
            self.parts, self.held, self.middle, self.full = parts, held, middle, full
            self.size = parts.shape[0] // self.count
            block = lambda peer: parts.at[pl.ds(peer * self.size, self.size)]
            self.first = push(numbers[0], block, held)
            self.second = cross(numbers[1], lambda peer: middle.at[self.other], middle)
            self.third = push(numbers[2], lambda peer: full.at[self.me], full)

        def scatter(self):
            self.first.start()
            self.held[self.me] = self.parts[pl.ds(self.me * self.size, self.size)]

        def exchange(self):
            self.first.wait_recv()
            total = self.held[0].astype(F32)
            for k in range(1, self.count):
                total = total + self.held[k].astype(F32)
            self.middle[self.other] = total.astype(self.middle.dtype)
            self.second.start()

        def gather(self):
            self.second.wait_recv()
            total = self.middle[0].astype(F32)
            for k in range(1, self.others):
                total = total + self.middle[k].astype(F32)
            self.full[self.me] = total.astype(self.full.dtype)
            self.third.start()

        def finish(self):
            self.third.wait_recv()

        def wait_send(self):
            self.first.wait_send()
            self.second.wait_send()
            self.third.wait_send()

    over_row, over_col = (row, r, nr), (col, c, nc)
    sum2 = Total(over_row, over_col, (2, 1, 3), p2, p2in, p2mid, p2all)
    sum1 = Total(over_row, over_col, (4, 3, 5), p1, p1in, p1mid, p1all)
    sumq = Total(over_col, over_row, (5, 6, 6), q, qin, qmid, qall)
    sum2.scatter()

    halo3.wait_recv()
    set_halo(delta2, hrow3, hcol3, hcor3, hcolf.at[:, half], masks, shift.at[0])

    def back_two(k, carry):
        z = dot(jnp.concatenate(windows(delta2, k * 8, 8), axis=1), v2[...]) * 0.25
        back[pl.ds(k * 8, 8)] = z.reshape(8, width2, 256)
        return carry

    lax.fori_loop(0, pairs2 // 8, back_two, 0)
    loads[7].wait()

    def delta_one(k, carry):
        for j in range(2):
            pair = k * 2 + j
            line = back[k, :, j * 128 : j * 128 + 128]
            base = j * width1
            pool[pl.ds(base, width2, stride=2), :] = line
            pool[pl.ds(base + 1, width2, stride=2), :] = line
            wide = pool[base : base + width1]
            for side in range(2):
                grade = slope[pair, :, side * 128 : side * 128 + 128]
                value = (cot1[pair, side].astype(F32) + wide) * grade
                at = pl.ds(2 * pair + side, 1)
                colf[0, at, :] = value[0:1]
                colf[1, at, :] = value[width1 - 1 : width1]
                put_row(delta1, pair + side, 1 - side, value, shift.at[2 * j + side])
        return carry

    lax.fori_loop(0, pairs1 // 2, delta_one, 0)
    take_edges(delta1, rows4, cols4, colf)
    halo4 = halo(3, rows4, cols4, hrow4, hcol4, hcor4)
    halo4.start()
    sum2.exchange()
    tap_grad(field1, delta1, acc1, 2048)
    tap_sums(acc1, p1)
    sum1.scatter()
    sum2.gather()
    halo4.wait_recv()
    set_halo(delta1, hrow4, hcol4, hcor4, hcolf, masks, shift.at[0])

    def input_grad(k, carry):
        z = dot(jnp.concatenate(windows(delta1, k * 16, 16), axis=1), v1[...]).astype(BF)
        for side in range(2):
            gin[pl.ds(k * 16, 16), side] = z[:, side * 128 : side * 128 + 128].reshape(16, width1, 128)
        return carry

    lax.fori_loop(0, pairs1 // 16, input_grad, 0)

    def list_grad(k, carry):
        at = pl.ds(pl.multiple_of(k * 8 * width1, 8 * width1), 8 * width1)
        for side in range(2):
            part = gin[pl.ds(k * 8, 8), side].reshape(8 * width1, 128)
            carry = carry + dot(flip[side, :, at], part)
        return carry

    gpacc = lax.fori_loop(0, pairs1 // 8, list_grad, jnp.zeros((128, 128), F32))
    gin_out = pltpu.make_async_copy(gin, gin_h, local_sem.at[9])
    gin_out.start()

    gproj = gpacc.astype(BF)
    q[...] = lax.dot_general(patch[...], gproj, CONTRACT0, preferred_element_type=F32).reshape(q.shape)
    sumq.scatter()
    gpatch = lax.dot_general(gproj, weight, CONTRACT1, preferred_element_type=F32).astype(BF)
    moved = lax.dot_general(perm[...], gpatch, CONTRACT0, preferred_element_type=F32)
    placed[...] = moved.astype(BF).reshape(placed.shape)
    push_back = Back(
        here, counts, placed, gathered, back_send, back_recv, core_send, core_recv
    )
    push_back.start()
    gathered[c, r] = placed[r]
    sum1.exchange()
    sum2.finish()
    p2_out = pltpu.make_async_copy(p2all, p2_h, local_sem.at[10])
    p2_out.start()
    sumq.exchange()
    push_back.forward()
    sum1.gather()
    started = []

    def scatter(slots):
        if not slots:
            return
        parts = jnp.concatenate([gathered[slot].reshape(places, 128) for slot in slots], axis=0)
        first = not started
        started.append(slots)

        def body(k, carry):
            at = pl.ds(pl.multiple_of(k * 1024, 1024), 1024)
            value = dot(jnp.concatenate([spread[slot, at, :] for slot in slots], axis=1), parts)
            gcoarse[at, :] = value if first else gcoarse[at, :] + value
            return carry

        lax.fori_loop(0, ncoarse // 1024, body, 0)

    scatter(push_back.slots(push_back.core))
    sumq.gather()
    push_back.wait_across()
    scatter(push_back.slots(1 - push_back.core))
    gcoarse_out = pltpu.make_async_copy(gcoarse, gcoarse_h, local_sem.at[11])
    gcoarse_out.start()
    sum1.finish()
    p1_out = pltpu.make_async_copy(p1all, p1_h, local_sem.at[12])
    p1_out.start()
    sumq.finish()
    gcond_out = pltpu.make_async_copy(qall, gcond_h, local_sem.at[13])
    gcond_out.start()

    for sent in (
        push_ask, push_reply, push_row, halo1, halo2, halo3, halo4, sum2, sum1, push_back,
        sumq,
    ):
        sent.wait_send()
    for out in (skip_out, gin_out, p2_out, gcoarse_out, p1_out, gcond_out):
        out.wait()


def finish_kernel(skip_k, gin_k, p1_k, p2_k, gcond_k, gcoarse_k, *refs):
    skip_h, gin_h, g1_h, g2_h, gcond_h, gcoarse_h = refs[:6]
    skip, gin, p1, p2, qs, held, g1, g2, gcond, gcoarse, sem = refs[6:]
    quarter = gin.shape[0] // 4
    parts = [pl.ds(k * quarter, quarter) for k in range(4)]
    loads = [
        pltpu.make_async_copy(source, target, sem.at[k])
        for k, (source, target) in enumerate(
            (
                (gcoarse_k, held), *((gin_k.at[part], gin.at[part]) for part in parts),
                (skip_k, skip), (p2_k, p2), (p1_k, p1), (gcond_k, qs),
            )
        )
    ]
    for load in loads:
        load.start()
    outs = []

    def store(source, target):
        copy = pltpu.make_async_copy(source, target, sem.at[16 + len(outs)])
        copy.start()
        outs.append(copy)

    loads[0].wait()
    pieces = held.shape[0] // 4
    for j, part in enumerate(parts):
        loads[1 + j].wait()
        store(gin.at[part], gin_h.at[part])
        for k in range(pieces // 128):
            at = slice(j * pieces + k * 128, j * pieces + k * 128 + 128)
            gcoarse[:, at] = held[at, :].T[0 : gcoarse.shape[0], :]
    store(gcoarse, gcoarse_h)
    loads[5].wait()
    store(skip, skip_h)
    loads[6].wait()
    g2[...] = p2[0 : g2.shape[0]].astype(F32)
    store(g2, g2_h)
    loads[7].wait()
    g1[...] = p1[0 : g1.shape[0]].astype(F32)
    store(g1, g1_h)
    loads[8].wait()
    gcond[...] = qs[0 : gcond.shape[0], :]
    store(gcond, gcond_h)
    for out in outs:
        out.wait()


def per_device(counts, fine, interp, ids, live, coarse, cw, conv_one, conv_two, cot_one, cot_two):
    nr, nc = counts
    height, width, channels = fine.shape
    pairs1, pairs2, width2 = height // 2, height // 4, width // 2
    cch, ncoarse = coarse.shape[1], coarse.shape[0]
    listed = ids.shape[-1]
    places = nr * SLOT
    blocks = -(-72 // nr) * nr
    any_space = pl.BlockSpec(memory_space=pl.ANY)
    smem = pl.BlockSpec(memory_space=pltpu.SMEM)
    vm = pltpu.VMEM
    chunk = blocks // nr

    def halo_bufs(rows, cols):
        return [
            vm((2, cols, 128), BF), vm((2, rows, 128), BF),
            vm((2, cols, 128), BF), vm((2, rows, 128), BF), vm((4, 16, 128), BF),
        ]

    def sum_bufs():
        return [
            vm((blocks, 16, 128), BF), vm((nr, chunk, 16, 128), BF), vm((nc, chunk, 16, 128), BF),
            vm((nr, chunk, 16, 128), BF),
        ]

    scratch = [
        vm((pairs1, 2, width, 128), BF), vm((pairs1, 2, width, 128), BF), vm((cch, ncoarse), BF),
        vm(cw.shape, BF), vm((9, 128, 128), BF), vm((9, 128, 128), BF),
        vm((pairs1, 2, width, 128), BF), vm((pairs2, 2, width2, 128), BF),
        vm((pairs2, 2, width2, 128), BF), vm((pairs1, 2, width, 128), BF),
        vm((ncoarse, 128), F32),
        vm((pairs1 + 1, width, 768), BF), vm((pairs2 + 1, width2, 768), BF),
        vm((pairs1 + 1, width, 768), BF), vm((pairs2 + 1, width2, 768), BF),
        vm((pairs1, width, 256), F32), vm((pairs2, width2, 256), F32), vm((2, 128, pairs1 * width), BF),
        vm((1536, 256), BF), vm((1536, 256), BF), vm((1536, 256), BF), vm((1536, 256), BF),
        vm((128, 128), F32), vm((128, 512), F32), vm((ncoarse, 256), BF),
        vm((nc, ncoarse, places), BF),
        vm((listed * CB, places), BF), vm((listed * CB, 128), BF), vm((listed * CB, 128), BF),
        vm((2, 256, 768), F32), vm((2, 256, 768), F32),
        vm((8, width + 16, 128), F32), vm((8 * width, 128), F32), vm((pairs1 + 2, width2 + 16, 128), F32),
        vm((2, height, 128), F32), vm((2, height, 128), F32),
        vm((nr, SLOT, 128), F32), vm((nr, SLOT, 128), F32), vm((8, places), F32), vm((nc, 8, places), F32),
        vm((nr, SLOT, 256), BF), vm((nr, SLOT, 256), BF),
        vm((nr, SLOT, 128), BF), vm((nc, nr, SLOT, 128), BF),
        *halo_bufs(height, width), *halo_bufs(height // 2, width2),
        *halo_bufs(height // 2, width2), *halo_bufs(height, width),
        *sum_bufs(), *sum_bufs(),
        vm((nc, 128 // nc, 128), F32), vm((nc, 1, 128 // nc, 128), F32), vm((nr, 1, 128 // nc, 128), F32),
        vm((nc, 1, 128 // nc, 128), F32),
        pltpu.SemaphoreType.DMA((16,)),
        pltpu.SemaphoreType.DMA((8,)), pltpu.SemaphoreType.DMA((8,)),
        pltpu.SemaphoreType.DMA((7,)), pltpu.SemaphoreType.DMA((7,)),
        pltpu.SemaphoreType.DMA((4, 3)), pltpu.SemaphoreType.DMA((4, 3)),
        *[pltpu.SemaphoreType.DMA((nc // 2,))] * 4,
    ]
    shape = jax.ShapeDtypeStruct
    results = pl.pallas_call(
        functools.partial(kernel, counts),
        out_shape=(
            shape((pairs2, 2, width2, 128), BF),
            shape((pairs1, 2, width, 128), BF),
            shape((nr, chunk, 16, 128), BF),
            shape((nr, chunk, 16, 128), BF),
            shape((nc, 1, 128 // nc, 128), F32),
            shape((ncoarse, 128), F32),
        ),
        in_specs=[smem, smem] + [any_space] * 8,
        out_specs=(any_space,) * 6,
        scratch_shapes=scratch,
        compiler_params=pltpu.CompilerParams(
            collective_id=0, has_side_effects=True, vmem_limit_bytes=63 * 2**20
        ),
        cost_estimate=pl.CostEstimate(
            flops=10 * 10**9, bytes_accessed=13 * 10**6, transcendentals=2 * 10**6
        ),
    )(
        ids.reshape(1, listed),
        live.reshape(1, 1),
        fine.reshape(pairs1, 2, width, channels),
        interp.reshape(pairs1, 2, width, interp.shape[2]),
        coarse.T,
        cw,
        conv_one.reshape(9, 128, 128),
        conv_two.reshape(9, 128, 128),
        cot_one.reshape(pairs1, 2, width, channels),
        cot_two.reshape(pairs2, 2, width2, channels),
    )
    skip, gin, g1, g2, gcond, gcoarse = pl.pallas_call(
        finish_kernel,
        out_shape=(
            shape((pairs2, 2, width2, 128), BF),
            shape((pairs1, 2, width, 128), BF),
            shape((72, 16, 128), F32),
            shape((72, 16, 128), F32),
            shape((cch, 128), F32),
            shape((cch, ncoarse), F32),
        ),
        in_specs=[any_space] * 6,
        out_specs=(any_space,) * 6,
        scratch_shapes=[
            vm((pairs2, 2, width2, 128), BF), vm((pairs1, 2, width, 128), BF),
            vm((blocks, 16, 128), BF), vm((blocks, 16, 128), BF), vm((128, 128), F32), vm((ncoarse, 128), F32),
            vm((72, 16, 128), F32), vm((72, 16, 128), F32), vm((cch, 128), F32), vm((cch, ncoarse), F32),
            pltpu.SemaphoreType.DMA((32,)),
        ],
        compiler_params=pltpu.CompilerParams(vmem_limit_bytes=63 * 2**20),
        cost_estimate=pl.CostEstimate(flops=0, bytes_accessed=12 * 10**6, transcendentals=0),
    )(
        results[0],
        results[1],
        results[2].reshape(blocks, 16, 128),
        results[3].reshape(blocks, 16, 128),
        results[4].reshape(128, 128),
        results[5],
    )
    return (
        skip.reshape(height // 2, width2, 128),
        gin.reshape(height, width, 128),
        g1.reshape(3, 3, 128, 128),
        g2.reshape(3, 3, 128, 128),
        gcond,
        gcoarse.T,
    )


def solution(mesh):
    counts = (mesh.shape["row"], mesh.shape["col"])
    tiles = P("row", "col", None)
    return jax.shard_map(
        functools.partial(per_device, counts),
        mesh=mesh,
        in_specs=(tiles, tiles, tiles, P("row", "col"), P("row", None), P(), P(), P(), tiles, tiles),
        out_specs=(tiles, tiles, P(), P(), P(), P("row", None)),
        check_vma=False,
    )
```

```python
import functools

import jax
import jax.numpy as jnp
from jax import lax
from jax.experimental import pallas as pl
from jax.experimental.pallas import tpu as pltpu
from jax.sharding import PartitionSpec as P

MESH = pl.DeviceIdType.MESH
BF = jnp.bfloat16
F32 = jnp.float32
CB = 8
CAP = 2
SLOT = CAP * CB
CONTRACT0 = (((0,), (0,)), ((), ()))
CONTRACT1 = (((1,), (1,)), ((), ()))


def dot(left, right):
    return jnp.dot(left, right, preferred_element_type=F32)


def iota(shape, dim):
    return lax.broadcasted_iota(jnp.int32, shape, dim)


class Push:
    def __init__(self, coords, axis, count, source, target, send, recv):
        self.coords, self.axis, self.count = coords, axis, count
        self.source, self.target, self.send, self.recv = source, target, send, recv
        self.me = coords[axis]

    def device(self, index):
        return (index, self.coords[1]) if self.axis == 0 else (self.coords[0], index)

    def copy(self, step):
        peer = lax.rem(self.me + step, self.count)
        return pltpu.make_async_remote_copy(
            src_ref=self.source(peer),
            dst_ref=self.target.at[self.me],
            send_sem=self.send,
            recv_sem=self.recv,
            device_id=self.device(peer),
            device_id_type=MESH,
        )

    def all(self):
        blocks = self.target.at[pl.ds(0, self.count - 1)]
        return pltpu.make_async_remote_copy(
            src_ref=blocks,
            dst_ref=blocks,
            send_sem=self.send,
            recv_sem=self.recv,
            device_id=self.device(lax.rem(self.me + 1, self.count)),
            device_id_type=MESH,
        )

    def each(self, act):
        def body(step, carry):
            act(step)
            return carry

        lax.fori_loop(1, self.count, body, 0)

    def start(self):
        self.each(lambda step: self.copy(step).start())

    def wait_recv(self):
        self.all().wait_recv()

    def wait_send(self):
        self.all().wait_send()


class Back:
    def __init__(self, coords, counts, placed, gathered, send, recv, core_send, core_recv):
        self.row, self.c = coords
        self.rows, self.chips = counts[0], counts[1] // 2
        self.placed, self.gathered = placed, gathered
        self.send, self.recv, self.core_send, self.core_recv = send, recv, core_send, core_recv
        self.core = lax.rem(self.c, 2)
        self.chip = lax.div(self.c, 2)

    def slot(self, step, core):
        return lax.rem(self.chip + self.chips - step, self.chips) * 2 + core

    def along(self, step, place):
        row = lax.rem(self.row + place, self.rows)
        col = lax.rem(self.chip + step, self.chips) * 2 + self.core
        return pltpu.make_async_remote_copy(
            src_ref=self.placed.at[row],
            dst_ref=self.gathered.at[self.c, self.row],
            send_sem=self.send.at[step],
            recv_sem=self.recv.at[step],
            device_id=(row, col),
            device_id_type=MESH,
        )

    def all(self, step):
        blocks = self.placed.at[pl.ds(0, self.rows - 1 if step == 0 else self.rows)]
        return pltpu.make_async_remote_copy(
            src_ref=blocks,
            dst_ref=blocks,
            send_sem=self.send.at[step],
            recv_sem=self.recv.at[step],
            device_id=(lax.rem(self.row + 1, self.rows), self.c),
            device_id_type=MESH,
        )

    def across(self, step):
        at = self.slot(step, self.core)
        return pltpu.make_async_remote_copy(
            src_ref=self.gathered.at[at],
            dst_ref=self.gathered.at[at],
            send_sem=self.core_send.at[step],
            recv_sem=self.core_recv.at[step],
            device_id=(self.row, self.chip * 2 + 1 - self.core),
            device_id_type=MESH,
        )

    def each(self, step, act):
        def body(place, carry):
            act(place)
            return carry

        lax.fori_loop(1 if step == 0 else 0, self.rows, body, 0)

    def start(self):
        for step in reversed(range(self.chips)):
            self.each(step, lambda place: self.along(step, place).start())

    def forward(self):
        for step in range(self.chips):
            self.all(step).wait_recv()
            self.across(step).start()

    def slots(self, core):
        return [self.slot(step, core) for step in range(self.chips)]

    def wait_across(self):
        for step in range(self.chips):
            self.across(step).wait_recv()

    def wait_send(self):
        for step in range(self.chips):
            self.all(step).wait_send()
            self.across(step).wait_send()


class Halo:
    def __init__(self, coords, counts, rows, cols, hrow, hcol, hcor, send, recv):
        (r, c), (nr, nc) = coords, counts
        north, south = lax.rem(r + nr - 1, nr), lax.rem(r + 1, nr)
        west, east = lax.rem(c + nc - 1, nc), lax.rem(c + 1, nc)
        width = rows.shape[1]
        low, high = pl.ds(0, 16), pl.ds(width - 16, 16)
        plan = (
            (rows.at[0], hrow.at[1], (north, c)),
            (rows.at[1], hrow.at[0], (south, c)),
            (cols.at[0], hcol.at[1], (r, west)),
            (cols.at[1], hcol.at[0], (r, east)),
            (rows.at[0, low], hcor.at[3], (north, west)),
            (rows.at[0, high], hcor.at[2], (north, east)),
            (rows.at[1, low], hcor.at[1], (south, west)),
            (rows.at[1, high], hcor.at[0], (south, east)),
        )
        def copy(source, target, k, device):
            return pltpu.make_async_remote_copy(
                src_ref=source,
                dst_ref=target,
                send_sem=send.at[k],
                recv_sem=recv.at[k],
                device_id=device,
                device_id_type=MESH,
            )

        order = (4, 5, 6, 7, 0, 1, 2, 3)
        self.copies = [copy(*plan[k][:2], (0, 1, 2, 2)[k // 2], plan[k][2]) for k in order]
        self.waits = [copy(part, part, k, (north, c)) for k, part in enumerate((hrow, hcol, hcor))]

    def start(self):
        for copy in self.copies:
            copy.start()

    def wait_recv(self):
        for copy in self.waits:
            copy.wait_recv()

    def wait_send(self):
        for copy in self.waits:
            copy.wait_send()


def put_row(field, pair, side, value, scratch):
    width = value.shape[0]
    base = side * 384
    scratch[8 : 8 + width] = value
    field[pair, :, base : base + 128] = scratch[7 : 7 + width].astype(BF)
    field[pair, :, base + 128 : base + 256] = value.astype(BF)
    field[pair, :, base + 256 : base + 384] = scratch[9 : 9 + width].astype(BF)


def set_halo(field, hrow, hcol, hcor, hcolf, masks, scratch):
    north, south, west, east = masks
    pairs, width = field.shape[0] - 1, field.shape[1]
    for pair, side, k, up in ((0, 0, 0, north), (pairs, 1, 1, south)):
        scratch[7:8] = hcor[2 * k].astype(F32)[15:16] * (up * west)
        scratch[8 + width : 9 + width] = hcor[2 * k + 1].astype(F32)[0:1] * (up * east)
        put_row(field, pair, side, hrow[k].astype(F32) * up, scratch)
    hcolf[0] = hcol[0].astype(F32) * west
    hcolf[1] = hcol[1].astype(F32) * east
    place = iota((16, 128), 0)

    def body(pair, carry):
        for half, spot, sub, lane in ((0, 0, 0, 0), (1, width - 16, 15, 256)):
            for side in (1, 0):
                at = (
                    pair + 1 - side,
                    pl.ds(spot, 16),
                    pl.ds(side * 384 + lane, 128),
                )
                cell = hcolf[half, pl.ds(2 * pair + 1 - side, 1), :]
                field[at] = jnp.where(place == sub, cell, field[at].astype(F32)).astype(BF)
        return carry

    lax.fori_loop(0, pairs, body, 0)


def take_edges(field, rows, cols, colf):
    pairs = field.shape[0] - 1
    rows[0] = field[0, :, 512:640]
    rows[1] = field[pairs, :, 128:256]
    cols[0] = colf[0].astype(BF)
    cols[1] = colf[1].astype(BF)


def windows(field, at, count):
    width = field.shape[1]
    low = field[pl.ds(at, count)].reshape(count * width, 768)
    high = field[pl.ds(at + 1, count)].reshape(count * width, 768)
    return low, high


def centres(field, at, count):
    width = field.shape[1]
    even = field[pl.ds(at, count), :, 512:640].reshape(count * width, 128)
    odd = field[pl.ds(at + 1, count), :, 128:256].reshape(count * width, 128)
    return even, odd


def pair_weights(kernel, out, flipped):
    out[...] = jnp.zeros_like(out)
    for a in range(3):
        for b in range(3):
            if flipped:
                block = kernel[(2 - a) * 3 + 2 - b].astype(F32).T.astype(BF)
            else:
                block = kernel[a * 3 + b]
            for half in range(2):
                base = (a + half) * 384 + b * 128
                out[base : base + 128, half * 128 : half * 128 + 128] = block


def tap_sums(acc, out):
    for a in range(3):
        for b in range(3):
            total = None
            for half in range(2):
                i = a + half
                lane = (i % 2) * 384 + b * 128
                part = acc[i // 2, half * 128 : half * 128 + 128, lane : lane + 128]
                total = part if total is None else total + part
            t = a * 3 + b
            out[t * 8 : t * 8 + 8] = total.T.astype(BF).reshape(8, 16, 128)


def activate(z):
    sig = 0.5 + 0.5 * jnp.tanh(0.5 * z)
    y = z * sig
    return y, sig + y * (1.0 - sig)


def kernel(counts, *refs):
    nr, nc = counts
    (ids, live, fine_h, interp_h, coarse_h, cw_h, k1_h, k2_h, c1_h, c2_h) = refs[:10]
    (skip_h, gin_h, p1_h, p2_h, gcond_h, gcoarse_h) = refs[10:16]
    (
        fine, interp, coarse, cw, k1, k2, cot1, cot2,
        skip, gin, gcoarse,
        field1, field2, delta1, delta2, slope, back, flip,
        w1, w2, v1, v2, cwp, coarse_t, table, spread, perm, proj, patch,
        acc1, acc2, shift, pool, stage, colf, hcolf,
        ask, asked, askrow, askedrow, reply, arrived, placed, gathered,
        rows1, cols1, hrow1, hcol1, hcor1,
        rows2, cols2, hrow2, hcol2, hcor2,
        rows3, cols3, hrow3, hcol3, hcor3,
        rows4, cols4, hrow4, hcol4, hcor4,
        p1, p1in, p1mid, p1all, p2, p2in, p2mid, p2all,
        q, qin, qmid, qall,
        local_sem, row_send, row_recv, col_send, col_recv, halo_send, halo_recv, back_send, back_recv, core_send, core_recv,
    ) = refs[16:]
    r, c = lax.axis_index("row"), lax.axis_index("col")
    here = (r, c)
    pairs1, width1 = fine.shape[0], fine.shape[2]
    pairs2, width2 = pairs1 // 2, width1 // 2
    listed = ids.shape[1]
    places = nr * SLOT
    ncoarse = coarse.shape[1]
    nblocks = ncoarse // CB

    loads = [
        pltpu.make_async_copy(source, target, local_sem.at[k])
        for k, (source, target) in enumerate(
            (
                (cw_h, cw), (coarse_h, coarse), (k1_h, k1), (interp_h, interp),
                (fine_h, fine), (k2_h, k2), (c2_h, cot2), (c1_h, cot1),
            )
        )
    ]
    for load in loads:
        load.start()

    barrier = pltpu.get_barrier_semaphore()

    def greet(row, col):
        pl.semaphore_signal(barrier, inc=1, device_id=(row, col), device_id_type=MESH)

    for step in range(1, nc):
        greet(r, lax.rem(c + step, nc))
    for step in range(1, nr):
        greet(lax.rem(r + step, nr), c)

    live_total = live[0, 0]
    owner = [lax.shift_right_logical(ids[0, k], jnp.int32(nblocks.bit_length() - 1)) for k in range(listed)]
    local = [ids[0, k] - owner[k] * nblocks for k in range(listed)]
    place = []
    for k in range(listed):
        rank = jnp.int32(0)
        for j in range(k):
            rank = rank + jnp.where(owner[j] == owner[k], 1, 0)
        place.append(jnp.where(k < live_total, owner[k] * CAP + rank, -1))
    row_at = iota((places, 128), 0)
    row_place = lax.shift_right_logical(row_at, 3)
    row_sub = row_at - row_place * CB
    wanted = jnp.full((places, 128), -1, jnp.int32)
    for k in range(listed):
        wanted = jnp.where(row_place == place[k], local[k] * CB + row_sub, wanted)
    ask[...] = wanted.astype(F32).reshape(ask.shape)
    list_at = iota((listed * CB, 128), 0)
    list_slot = lax.shift_right_logical(list_at, 3)
    list_sub = list_at - list_slot * CB
    target = jnp.full((listed * CB, 128), -1, jnp.int32)
    for k in range(listed):
        found = jnp.where(place[k] >= 0, place[k] * CB, -CB)
        target = jnp.where(list_slot == k, found + list_sub, target)
    lanes = iota((listed * CB, 128), 1)
    for j in range(places // 128):
        perm[:, j * 128 : j * 128 + 128] = jnp.where(target == lanes + j * 128, 1.0, 0.0).astype(BF)

    pl.semaphore_wait(barrier, nr - 1 + nc - 1)

    row = lambda k, source, dest: Push(here, 0, nr, source, dest, row_send.at[k], row_recv.at[k])
    col = lambda k, source, dest: Push(here, 1, nc, source, dest, col_send.at[k], col_recv.at[k])
    halo = lambda k, *bufs: Halo(here, counts, *bufs, halo_send.at[k], halo_recv.at[k])
    masks = (
        jnp.where(r > 0, 1.0, 0.0),
        jnp.where(r < nr - 1, 1.0, 0.0),
        jnp.where(c > 0, 1.0, 0.0),
        jnp.where(c < nc - 1, 1.0, 0.0),
    )

    push_ask = row(0, lambda peer: ask.at[peer], asked)
    push_ask.start()
    asked[r] = ask[r]

    loads[0].wait()
    loads[1].wait()
    cwp[...] = jnp.zeros_like(cwp)
    cwp[0 : cw.shape[0], :] = cw[...].astype(F32)
    coarse_t[...] = jnp.zeros_like(coarse_t)
    weight = cwp[...].astype(BF)

    def project(k, carry):
        at = pl.ds(pl.multiple_of(k * 512, 512), 512)
        coarse_t[0 : coarse.shape[0], :] = coarse[:, at].astype(F32)
        part = coarse_t[...].T.astype(BF)
        table[at, 0:128] = dot(part, weight).astype(BF)
        table[at, 128:256] = part
        return carry

    lax.fori_loop(0, ncoarse // 512, project, 0)
    loads[2].wait()
    pair_weights(k1, w1, False)

    loads[5].wait()
    pair_weights(k1, v1, True)
    pair_weights(k2, w2, False)
    pair_weights(k2, v2, True)
    shift[...] = jnp.zeros_like(shift)

    push_ask.wait_recv()
    every = asked[...].reshape(places, 128)
    lane_f = iota((places, 128), 1).astype(F32)

    def gather(k, carry):
        base = (k * 512).astype(F32)
        pieces = [jnp.where(every == lane_f + (base + j * 128.0), 1.0, 0.0).astype(BF) for j in range(4)]
        return carry + dot(
            jnp.concatenate(pieces, axis=1), table[pl.ds(pl.multiple_of(k * 512, 512), 512), :]
        )

    gathered_rows = lax.fori_loop(0, ncoarse // 512, gather, jnp.zeros((places, 256), F32))
    reply[...] = gathered_rows.astype(BF).reshape(reply.shape)
    push_reply = row(1, lambda peer: reply.at[peer], arrived)
    push_reply.start()
    arrived[r] = reply[r]
    askrow[...] = every.T[0:8, :]
    push_row = col(0, lambda peer: askrow, askedrow)
    push_row.start()
    askedrow[c] = askrow[...]

    loads[3].wait()

    def turn(pair, carry):
        at = pl.ds(pl.multiple_of(pair * width1, width1), width1)
        for side in range(2):
            flip[side, :, at] = interp[pair, side].astype(F32).T.astype(BF)
        return carry

    lax.fori_loop(0, pairs1, turn, 0)

    push_reply.wait_recv()
    both = dot(perm[...], arrived[...].reshape(places, 256)).astype(BF)
    proj[...] = both[:, 0:128]
    patch[...] = both[:, 128:256]
    loads[4].wait()

    for half in range(2):
        at = pl.ds(half * (width1 - 16), 16)
        value = dot(interp[:, :, at, :].reshape(pairs1 * 32, 128), proj[...])
        pool[...] = value + fine[:, :, at, :].reshape(pairs1 * 32, 128).astype(F32)
        cols1[half] = pool[pl.ds(15 * half, 2 * pairs1, stride=16), :].astype(BF)
        at = (half * (pairs1 - 1), half)
        rows1[half] = (dot(interp[at], proj[...]) + fine[at].astype(F32)).astype(BF)
    halo1 = halo(0, rows1, cols1, hrow1, hcol1, hcor1)
    halo1.start()

    def condition(k, carry):
        for j in range(4):
            pair = k * 4 + j
            value = dot(interp[pair].reshape(2 * width1, 128), proj[...])
            value = value + fine[pair].reshape(2 * width1, 128).astype(F32)
            for side in range(2):
                line = value[side * width1 : (side + 1) * width1]
                put_row(field1, pair + side, 1 - side, line, shift.at[2 * j + side])
        return carry

    lax.fori_loop(0, pairs1 // 4, condition, 0)
    halo1.wait_recv()
    set_halo(field1, hrow1, hcol1, hcor1, hcolf, masks, shift.at[0])

    middle = width1 - 32
    inner = middle // 2

    def level_one(pair, count, cols):
        lane_rows = [field1[pl.ds(pair + j, count), cols, :].reshape(-1, 768) for j in range(2)]
        y, grade = activate(dot(jnp.concatenate(lane_rows, axis=1), w1[...]))
        cells = y.shape[0]
        slope[pl.ds(pair, count), cols, :] = grade.reshape(count, cells // count, 256)
        pool[0:cells] = y[:, 0:128] + y[:, 128:256]
        total = pool[pl.ds(0, cells // 2, stride=2), :] + pool[pl.ds(1, cells // 2, stride=2), :]
        return total * 0.25

    for half in range(2):
        total = level_one(0, pairs1, pl.ds(half * (width1 - 16), 16))
        pool[0 : pairs1 * 8] = total
        cols2[half] = pool[pl.ds(7 * half, pairs1, stride=8), :].astype(BF)
        stage[1 : pairs1 + 1, 8 + half * (width2 - 8) : 16 + half * (width2 - 8), :] = total.reshape(
            pairs1, 8, 128
        )
    for half in range(2):
        at = half * (pairs1 - 1)
        stage[at + 1, 16 : 16 + inner, :] = level_one(at, 1, pl.ds(16, middle))
        rows2[half] = stage[at + 1, 8 : 8 + width2, :].astype(BF)
    halo2 = halo(1, rows2, cols2, hrow2, hcol2, hcor2)
    halo2.start()
    step1 = (pairs1 - 2) // 3

    def level_one_inner(k, carry):
        pair = 1 + k * step1
        total = level_one(pair, step1, pl.ds(16, middle))
        stage[pl.ds(pair + 1, step1), 16 : 16 + inner, :] = total.reshape(step1, inner, 128)
        return carry

    lax.fori_loop(0, 3, level_one_inner, 0)
    half = pl.ds(0, 2 * pairs2)
    loads[6].wait()
    halo2.wait_recv()
    north, south, west, east = masks
    for k, up in ((0, north), (1, south)):
        at = k * (pairs1 + 1)
        stage[at, 8 : 8 + width2, :] = hrow2[k].astype(F32) * up
        stage[at, 7:8, :] = hcor2[2 * k].astype(F32)[15:16] * (up * west)
        stage[at, 8 + width2 : 9 + width2, :] = hcor2[2 * k + 1].astype(F32)[0:1] * (up * east)
    hcolf[0, half] = hcol2[0].astype(F32) * west
    hcolf[1, half] = hcol2[1].astype(F32) * east

    def edge_cells(k, carry):
        stage[k + 1, 7:8, :] = hcolf[0, pl.ds(k, 1), :]
        stage[k + 1, 8 + width2 : 9 + width2, :] = hcolf[1, pl.ds(k, 1), :]
        return carry

    lax.fori_loop(0, pairs1, edge_cells, 0)

    def lay_out(pair, carry):
        for side in range(2):
            for j in range(3):
                lane = side * 384 + j * 128
                line = stage[2 * pair + side, 7 + j : 7 + j + width2, :]
                field2[pair, :, lane : lane + 128] = line.astype(BF)
        return carry

    lax.fori_loop(0, pairs2 + 1, lay_out, 0)

    def level_two(k, carry):
        pair = k * 8
        z = dot(jnp.concatenate(windows(field2, pair, 8), axis=1), w2[...])
        y, grade = activate(z)
        for side in range(2):
            lane = slice(side * 128, side * 128 + 128)
            skip[pl.ds(pair, 8), side] = y[:, lane].astype(BF).reshape(8, width2, 128)
            value = cot2[pl.ds(pair, 8), side].astype(F32) * grade[:, lane].reshape(8, width2, 128)
            for j in range(8):
                at = pl.ds(2 * (pair + j) + side, 1)
                colf[0, at, :] = value[j, 0:1]
                colf[1, at, :] = value[j, width2 - 1 : width2]
                put_row(delta2, pair + j + side, 1 - side, value[j], shift.at[j])
        return carry

    lax.fori_loop(0, pairs2 // 8, level_two, 0)
    skip_out = pltpu.make_async_copy(skip, skip_h, local_sem.at[8])
    skip_out.start()
    take_edges(delta2, rows3, cols3, colf.at[:, half])
    halo3 = halo(2, rows3, cols3, hrow3, hcol3, hcor3)
    halo3.start()

    def tap_grad(field, delta, acc, step):
        count = step // field.shape[1]

        def body(k, carry):
            outer = jnp.concatenate(centres(delta, k * count, count), axis=1)
            for i, window in enumerate(windows(field, k * count, count)):
                acc[i] += lax.dot_general(outer, window, CONTRACT0, preferred_element_type=F32)
            return carry

        acc[...] = jnp.zeros_like(acc)
        lax.fori_loop(0, (field.shape[0] - 1) // count, body, 0)

    push_row.wait_recv()

    def spot(k, carry):
        at = pl.ds(pl.multiple_of(k * 256, 256), 256)
        number = iota((256, places), 0).astype(F32) + (k * 256).astype(F32)
        for j in range(nc):
            match = number == askedrow[j, 0:1, :]
            spread[j, at, :] = jnp.where(match, 1.0, 0.0).astype(BF)
        return carry

    lax.fori_loop(0, ncoarse // 256, spot, 0)

    tap_grad(field2, delta2, acc2, 1024)
    tap_sums(acc2, p2)

    class Total:
        def __init__(self, outer, inner, numbers, parts, held, middle, full):
            (push, self.me, self.count), (cross, self.other, self.others) = outer, inner
            self.parts, self.held, self.middle, self.full = parts, held, middle, full
            self.size = parts.shape[0] // self.count
            block = lambda peer: parts.at[pl.ds(peer * self.size, self.size)]
            self.first = push(numbers[0], block, held)
            self.second = cross(numbers[1], lambda peer: middle.at[self.other], middle)
            self.third = push(numbers[2], lambda peer: full.at[self.me], full)

        def scatter(self):
            self.first.start()
            self.held[self.me] = self.parts[pl.ds(self.me * self.size, self.size)]

        def exchange(self):
            self.first.wait_recv()
            total = self.held[0].astype(F32)
            for k in range(1, self.count):
                total = total + self.held[k].astype(F32)
            self.middle[self.other] = total.astype(self.middle.dtype)
            self.second.start()

        def gather(self):
            self.second.wait_recv()
            total = self.middle[0].astype(F32)
            for k in range(1, self.others):
                total = total + self.middle[k].astype(F32)
            self.full[self.me] = total.astype(self.full.dtype)
            self.third.start()

        def finish(self):
            self.third.wait_recv()

        def wait_send(self):
            self.first.wait_send()
            self.second.wait_send()
            self.third.wait_send()

    over_row, over_col = (row, r, nr), (col, c, nc)
    sum2 = Total(over_row, over_col, (2, 1, 3), p2, p2in, p2mid, p2all)
    sum1 = Total(over_row, over_col, (4, 3, 5), p1, p1in, p1mid, p1all)
    sumq = Total(over_col, over_row, (5, 6, 6), q, qin, qmid, qall)
    sum2.scatter()

    halo3.wait_recv()
    set_halo(delta2, hrow3, hcol3, hcor3, hcolf.at[:, half], masks, shift.at[0])

    def back_two(k, carry):
        z = dot(jnp.concatenate(windows(delta2, k * 8, 8), axis=1), v2[...]) * 0.25
        back[pl.ds(k * 8, 8)] = z.reshape(8, width2, 256)
        return carry

    lax.fori_loop(0, pairs2 // 8, back_two, 0)
    loads[7].wait()

    def delta_one(k, carry):
        for j in range(2):
            pair = k * 2 + j
            line = back[k, :, j * 128 : j * 128 + 128]
            base = j * width1
            pool[pl.ds(base, width2, stride=2), :] = line
            pool[pl.ds(base + 1, width2, stride=2), :] = line
            wide = pool[base : base + width1]
            for side in range(2):
                grade = slope[pair, :, side * 128 : side * 128 + 128]
                value = (cot1[pair, side].astype(F32) + wide) * grade
                at = pl.ds(2 * pair + side, 1)
                colf[0, at, :] = value[0:1]
                colf[1, at, :] = value[width1 - 1 : width1]
                put_row(delta1, pair + side, 1 - side, value, shift.at[2 * j + side])
        return carry

    lax.fori_loop(0, pairs1 // 2, delta_one, 0)
    take_edges(delta1, rows4, cols4, colf)
    halo4 = halo(3, rows4, cols4, hrow4, hcol4, hcor4)
    halo4.start()
    sum2.exchange()
    tap_grad(field1, delta1, acc1, 2048)
    tap_sums(acc1, p1)
    sum1.scatter()
    sum2.gather()
    halo4.wait_recv()
    set_halo(delta1, hrow4, hcol4, hcor4, hcolf, masks, shift.at[0])

    def input_grad(k, carry):
        z = dot(jnp.concatenate(windows(delta1, k * 16, 16), axis=1), v1[...]).astype(BF)
        for side in range(2):
            gin[pl.ds(k * 16, 16), side] = z[:, side * 128 : side * 128 + 128].reshape(16, width1, 128)
        return carry

    lax.fori_loop(0, pairs1 // 16, input_grad, 0)

    def list_grad(k, carry):
        at = pl.ds(pl.multiple_of(k * 8 * width1, 8 * width1), 8 * width1)
        for side in range(2):
            part = gin[pl.ds(k * 8, 8), side].reshape(8 * width1, 128)
            carry = carry + dot(flip[side, :, at], part)
        return carry

    gpacc = lax.fori_loop(0, pairs1 // 8, list_grad, jnp.zeros((128, 128), F32))
    gin_out = pltpu.make_async_copy(gin, gin_h, local_sem.at[9])
    gin_out.start()

    gproj = gpacc.astype(BF)
    q[...] = lax.dot_general(patch[...], gproj, CONTRACT0, preferred_element_type=F32).reshape(q.shape)
    sumq.scatter()
    gpatch = lax.dot_general(gproj, weight, CONTRACT1, preferred_element_type=F32).astype(BF)
    moved = lax.dot_general(perm[...], gpatch, CONTRACT0, preferred_element_type=F32)
    placed[...] = moved.astype(BF).reshape(placed.shape)
    push_back = Back(
        here, counts, placed, gathered, back_send, back_recv, core_send, core_recv
    )
    push_back.start()
    gathered[c, r] = placed[r]
    sum1.exchange()
    sum2.finish()
    p2_out = pltpu.make_async_copy(p2all, p2_h, local_sem.at[10])
    p2_out.start()
    sumq.exchange()
    push_back.forward()
    sum1.gather()
    started = []

    def scatter(slots):
        if not slots:
            return
        parts = jnp.concatenate([gathered[slot].reshape(places, 128) for slot in slots], axis=0)
        first = not started
        started.append(slots)

        def body(k, carry):
            at = pl.ds(pl.multiple_of(k * 1024, 1024), 1024)
            value = dot(jnp.concatenate([spread[slot, at, :] for slot in slots], axis=1), parts)
            gcoarse[at, :] = value if first else gcoarse[at, :] + value
            return carry

        lax.fori_loop(0, ncoarse // 1024, body, 0)

    scatter(push_back.slots(push_back.core))
    sumq.gather()
    push_back.wait_across()
    scatter(push_back.slots(1 - push_back.core))
    gcoarse_out = pltpu.make_async_copy(gcoarse, gcoarse_h, local_sem.at[11])
    gcoarse_out.start()
    sum1.finish()
    p1_out = pltpu.make_async_copy(p1all, p1_h, local_sem.at[12])
    p1_out.start()
    sumq.finish()
    gcond_out = pltpu.make_async_copy(qall, gcond_h, local_sem.at[13])
    gcond_out.start()

    for sent in (
        push_ask, push_reply, push_row, halo1, halo2, halo3, halo4, sum2, sum1, push_back,
        sumq,
    ):
        sent.wait_send()
    for out in (skip_out, gin_out, p2_out, gcoarse_out, p1_out, gcond_out):
        out.wait()


def finish_kernel(skip_k, gin_k, p1_k, p2_k, gcond_k, gcoarse_k, *refs):
    skip_h, gin_h, g1_h, g2_h, gcond_h, gcoarse_h = refs[:6]
    skip, gin, p1, p2, qs, held, g1, g2, gcond, gcoarse, sem = refs[6:]
    quarter = gin.shape[0] // 4
    parts = [pl.ds(k * quarter, quarter) for k in range(4)]
    loads = [
        pltpu.make_async_copy(source, target, sem.at[k])
        for k, (source, target) in enumerate(
            (
                (gcoarse_k, held), *((gin_k.at[part], gin.at[part]) for part in parts),
                (skip_k, skip), (p2_k, p2), (p1_k, p1), (gcond_k, qs),
            )
        )
    ]
    for load in loads:
        load.start()
    outs = []

    def store(source, target):
        copy = pltpu.make_async_copy(source, target, sem.at[16 + len(outs)])
        copy.start()
        outs.append(copy)

    loads[0].wait()
    pieces = held.shape[0] // 4
    for j, part in enumerate(parts):
        loads[1 + j].wait()
        store(gin.at[part], gin_h.at[part])
        for k in range(pieces // 128):
            at = slice(j * pieces + k * 128, j * pieces + k * 128 + 128)
            gcoarse[:, at] = held[at, :].T[0 : gcoarse.shape[0], :]
    store(gcoarse, gcoarse_h)
    loads[5].wait()
    store(skip, skip_h)
    loads[6].wait()
    g2[...] = p2[0 : g2.shape[0]].astype(F32)
    store(g2, g2_h)
    loads[7].wait()
    g1[...] = p1[0 : g1.shape[0]].astype(F32)
    store(g1, g1_h)
    loads[8].wait()
    gcond[...] = qs[0 : gcond.shape[0], :]
    store(gcond, gcond_h)
    for out in outs:
        out.wait()


def per_device(counts, fine, interp, ids, live, coarse, cw, conv_one, conv_two, cot_one, cot_two):
    nr, nc = counts
    height, width, channels = fine.shape
    pairs1, pairs2, width2 = height // 2, height // 4, width // 2
    cch, ncoarse = coarse.shape[1], coarse.shape[0]
    listed = ids.shape[-1]
    places = nr * SLOT
    blocks = -(-72 // nr) * nr
    any_space = pl.BlockSpec(memory_space=pl.ANY)
    smem = pl.BlockSpec(memory_space=pltpu.SMEM)
    vm = pltpu.VMEM
    chunk = blocks // nr

    def halo_bufs(rows, cols):
        return [
            vm((2, cols, 128), BF), vm((2, rows, 128), BF),
            vm((2, cols, 128), BF), vm((2, rows, 128), BF), vm((4, 16, 128), BF),
        ]

    def sum_bufs():
        return [
            vm((blocks, 16, 128), BF), vm((nr, chunk, 16, 128), BF), vm((nc, chunk, 16, 128), BF),
            vm((nr, chunk, 16, 128), BF),
        ]

    scratch = [
        vm((pairs1, 2, width, 128), BF), vm((pairs1, 2, width, 128), BF), vm((cch, ncoarse), BF),
        vm(cw.shape, BF), vm((9, 128, 128), BF), vm((9, 128, 128), BF),
        vm((pairs1, 2, width, 128), BF), vm((pairs2, 2, width2, 128), BF),
        vm((pairs2, 2, width2, 128), BF), vm((pairs1, 2, width, 128), BF),
        vm((ncoarse, 128), F32),
        vm((pairs1 + 1, width, 768), BF), vm((pairs2 + 1, width2, 768), BF),
        vm((pairs1 + 1, width, 768), BF), vm((pairs2 + 1, width2, 768), BF),
        vm((pairs1, width, 256), F32), vm((pairs2, width2, 256), F32), vm((2, 128, pairs1 * width), BF),
        vm((1536, 256), BF), vm((1536, 256), BF), vm((1536, 256), BF), vm((1536, 256), BF),
        vm((128, 128), F32), vm((128, 512), F32), vm((ncoarse, 256), BF),
        vm((nc, ncoarse, places), BF),
        vm((listed * CB, places), BF), vm((listed * CB, 128), BF), vm((listed * CB, 128), BF),
        vm((2, 256, 768), F32), vm((2, 256, 768), F32),
        vm((8, width + 16, 128), F32), vm((8 * width, 128), F32), vm((pairs1 + 2, width2 + 16, 128), F32),
        vm((2, height, 128), F32), vm((2, height, 128), F32),
        vm((nr, SLOT, 128), F32), vm((nr, SLOT, 128), F32), vm((8, places), F32), vm((nc, 8, places), F32),
        vm((nr, SLOT, 256), BF), vm((nr, SLOT, 256), BF),
        vm((nr, SLOT, 128), BF), vm((nc, nr, SLOT, 128), BF),
        *halo_bufs(height, width), *halo_bufs(height // 2, width2),
        *halo_bufs(height // 2, width2), *halo_bufs(height, width),
        *sum_bufs(), *sum_bufs(),
        vm((nc, 128 // nc, 128), F32), vm((nc, 1, 128 // nc, 128), F32), vm((nr, 1, 128 // nc, 128), F32),
        vm((nc, 1, 128 // nc, 128), F32),
        pltpu.SemaphoreType.DMA((16,)),
        pltpu.SemaphoreType.DMA((8,)), pltpu.SemaphoreType.DMA((8,)),
        pltpu.SemaphoreType.DMA((7,)), pltpu.SemaphoreType.DMA((7,)),
        pltpu.SemaphoreType.DMA((4, 3)), pltpu.SemaphoreType.DMA((4, 3)),
        *[pltpu.SemaphoreType.DMA((nc // 2,))] * 4,
    ]
    shape = jax.ShapeDtypeStruct
    results = pl.pallas_call(
        functools.partial(kernel, counts),
        out_shape=(
            shape((pairs2, 2, width2, 128), BF),
            shape((pairs1, 2, width, 128), BF),
            shape((nr, chunk, 16, 128), BF),
            shape((nr, chunk, 16, 128), BF),
            shape((nc, 1, 128 // nc, 128), F32),
            shape((ncoarse, 128), F32),
        ),
        in_specs=[smem, smem] + [any_space] * 8,
        out_specs=(any_space,) * 6,
        scratch_shapes=scratch,
        compiler_params=pltpu.CompilerParams(
            collective_id=0, has_side_effects=True, vmem_limit_bytes=63 * 2**20
        ),
        cost_estimate=pl.CostEstimate(
            flops=10 * 10**9, bytes_accessed=13 * 10**6, transcendentals=2 * 10**6
        ),
    )(
        ids.reshape(1, listed),
        live.reshape(1, 1),
        fine.reshape(pairs1, 2, width, channels),
        interp.reshape(pairs1, 2, width, interp.shape[2]),
        coarse.T,
        cw,
        conv_one.reshape(9, 128, 128),
        conv_two.reshape(9, 128, 128),
        cot_one.reshape(pairs1, 2, width, channels),
        cot_two.reshape(pairs2, 2, width2, channels),
    )
    skip, gin, g1, g2, gcond, gcoarse = pl.pallas_call(
        finish_kernel,
        out_shape=(
            shape((pairs2, 2, width2, 128), BF),
            shape((pairs1, 2, width, 128), BF),
            shape((72, 16, 128), F32),
            shape((72, 16, 128), F32),
            shape((cch, 128), F32),
            shape((cch, ncoarse), F32),
        ),
        in_specs=[any_space] * 6,
        out_specs=(any_space,) * 6,
        scratch_shapes=[
            vm((pairs2, 2, width2, 128), BF), vm((pairs1, 2, width, 128), BF),
            vm((blocks, 16, 128), BF), vm((blocks, 16, 128), BF), vm((128, 128), F32), vm((ncoarse, 128), F32),
            vm((72, 16, 128), F32), vm((72, 16, 128), F32), vm((cch, 128), F32), vm((cch, ncoarse), F32),
            pltpu.SemaphoreType.DMA((32,)),
        ],
        compiler_params=pltpu.CompilerParams(vmem_limit_bytes=63 * 2**20),
        cost_estimate=pl.CostEstimate(flops=0, bytes_accessed=12 * 10**6, transcendentals=0),
    )(
        results[0],
        results[1],
        results[2].reshape(blocks, 16, 128),
        results[3].reshape(blocks, 16, 128),
        results[4].reshape(128, 128),
        results[5],
    )
    return (
        skip.reshape(height // 2, width2, 128),
        gin.reshape(height, width, 128),
        g1.reshape(3, 3, 128, 128),
        g2.reshape(3, 3, 128, 128),
        gcond,
        gcoarse.T,
    )


def solution(mesh):
    counts = (mesh.shape["row"], mesh.shape["col"])
    tiles = P("row", "col", None)
    return jax.shard_map(
        functools.partial(per_device, counts),
        mesh=mesh,
        in_specs=(tiles, tiles, tiles, P("row", "col"), P("row", None), P(), P(), P(), tiles, tiles),
        out_specs=(tiles, tiles, P(), P(), P(), P("row", None)),
        check_vma=False,
    )
```

```python
import functools

import jax
import jax.numpy as jnp
from jax import lax
from jax.experimental import pallas as pl
from jax.experimental.pallas import tpu as pltpu
from jax.sharding import PartitionSpec as P

MESH = pl.DeviceIdType.MESH
BF = jnp.bfloat16
F32 = jnp.float32
CB = 8
CAP = 2
SLOT = CAP * CB
CONTRACT0 = (((0,), (0,)), ((), ()))
CONTRACT1 = (((1,), (1,)), ((), ()))


def dot(left, right):
    return jnp.dot(left, right, preferred_element_type=F32)


def iota(shape, dim):
    return lax.broadcasted_iota(jnp.int32, shape, dim)


class Push:
    def __init__(self, coords, axis, count, source, target, send, recv):
        self.coords, self.axis, self.count = coords, axis, count
        self.source, self.target, self.send, self.recv = source, target, send, recv
        self.me = coords[axis]

    def device(self, index):
        return (index, self.coords[1]) if self.axis == 0 else (self.coords[0], index)

    def copy(self, step):
        peer = lax.rem(self.me + step, self.count)
        return pltpu.make_async_remote_copy(
            src_ref=self.source(peer),
            dst_ref=self.target.at[self.me],
            send_sem=self.send,
            recv_sem=self.recv,
            device_id=self.device(peer),
            device_id_type=MESH,
        )

    def all(self):
        blocks = self.target.at[pl.ds(0, self.count - 1)]
        return pltpu.make_async_remote_copy(
            src_ref=blocks,
            dst_ref=blocks,
            send_sem=self.send,
            recv_sem=self.recv,
            device_id=self.device(lax.rem(self.me + 1, self.count)),
            device_id_type=MESH,
        )

    def each(self, act):
        def body(step, carry):
            act(step)
            return carry

        lax.fori_loop(1, self.count, body, 0)

    def start(self):
        self.each(lambda step: self.copy(step).start())

    def wait_recv(self):
        self.all().wait_recv()

    def wait_send(self):
        self.all().wait_send()


class Back:
    def __init__(self, coords, counts, placed, gathered, send, recv, core_send, core_recv):
        self.row, self.c = coords
        self.rows, self.chips = counts[0], counts[1] // 2
        self.placed, self.gathered = placed, gathered
        self.send, self.recv, self.core_send, self.core_recv = send, recv, core_send, core_recv
        self.core = lax.rem(self.c, 2)
        self.chip = lax.div(self.c, 2)

    def slot(self, step, core):
        return lax.rem(self.chip + self.chips - step, self.chips) * 2 + core

    def along(self, step, place):
        row = lax.rem(self.row + place, self.rows)
        col = lax.rem(self.chip + step, self.chips) * 2 + self.core
        return pltpu.make_async_remote_copy(
            src_ref=self.placed.at[row],
            dst_ref=self.gathered.at[self.c, self.row],
            send_sem=self.send.at[step],
            recv_sem=self.recv.at[step],
            device_id=(row, col),
            device_id_type=MESH,
        )

    def all(self, step):
        blocks = self.placed.at[pl.ds(0, self.rows - 1 if step == 0 else self.rows)]
        return pltpu.make_async_remote_copy(
            src_ref=blocks,
            dst_ref=blocks,
            send_sem=self.send.at[step],
            recv_sem=self.recv.at[step],
            device_id=(lax.rem(self.row + 1, self.rows), self.c),
            device_id_type=MESH,
        )

    def across(self, step):
        at = self.slot(step, self.core)
        return pltpu.make_async_remote_copy(
            src_ref=self.gathered.at[at],
            dst_ref=self.gathered.at[at],
            send_sem=self.core_send.at[step],
            recv_sem=self.core_recv.at[step],
            device_id=(self.row, self.chip * 2 + 1 - self.core),
            device_id_type=MESH,
        )

    def each(self, step, act):
        def body(place, carry):
            act(place)
            return carry

        lax.fori_loop(1 if step == 0 else 0, self.rows, body, 0)

    def start(self):
        for step in reversed(range(self.chips)):
            self.each(step, lambda place: self.along(step, place).start())

    def forward(self):
        for step in range(self.chips):
            self.all(step).wait_recv()
            self.across(step).start()

    def slots(self, core):
        return [self.slot(step, core) for step in range(self.chips)]

    def wait_across(self):
        for step in range(self.chips):
            self.across(step).wait_recv()

    def wait_send(self):
        for step in range(self.chips):
            self.all(step).wait_send()
            self.across(step).wait_send()


class Halo:
    def __init__(self, coords, counts, rows, cols, hrow, hcol, hcor, send, recv):
        (r, c), (nr, nc) = coords, counts
        north, south = lax.rem(r + nr - 1, nr), lax.rem(r + 1, nr)
        west, east = lax.rem(c + nc - 1, nc), lax.rem(c + 1, nc)
        width = rows.shape[1]
        low, high = pl.ds(0, 16), pl.ds(width - 16, 16)
        plan = (
            (rows.at[0], hrow.at[1], (north, c)),
            (rows.at[1], hrow.at[0], (south, c)),
            (cols.at[0], hcol.at[1], (r, west)),
            (cols.at[1], hcol.at[0], (r, east)),
            (rows.at[0, low], hcor.at[3], (north, west)),
            (rows.at[0, high], hcor.at[2], (north, east)),
            (rows.at[1, low], hcor.at[1], (south, west)),
            (rows.at[1, high], hcor.at[0], (south, east)),
        )
        def copy(source, target, k, device):
            return pltpu.make_async_remote_copy(
                src_ref=source,
                dst_ref=target,
                send_sem=send.at[k],
                recv_sem=recv.at[k],
                device_id=device,
                device_id_type=MESH,
            )

        order = (4, 5, 6, 7, 0, 1, 2, 3)
        self.copies = [copy(*plan[k][:2], (0, 1, 2, 2)[k // 2], plan[k][2]) for k in order]
        self.waits = [copy(part, part, k, (north, c)) for k, part in enumerate((hrow, hcol, hcor))]

    def start(self):
        for copy in self.copies:
            copy.start()

    def wait_recv(self):
        for copy in self.waits:
            copy.wait_recv()

    def wait_send(self):
        for copy in self.waits:
            copy.wait_send()


def put_row(field, pair, side, value, scratch):
    width = value.shape[0]
    base = side * 384
    scratch[8 : 8 + width] = value
    field[pair, :, base : base + 128] = scratch[7 : 7 + width].astype(BF)
    field[pair, :, base + 128 : base + 256] = value.astype(BF)
    field[pair, :, base + 256 : base + 384] = scratch[9 : 9 + width].astype(BF)


def set_halo(field, hrow, hcol, hcor, hcolf, masks, scratch):
    north, south, west, east = masks
    pairs, width = field.shape[0] - 1, field.shape[1]
    for pair, side, k, up in ((0, 0, 0, north), (pairs, 1, 1, south)):
        scratch[7:8] = hcor[2 * k].astype(F32)[15:16] * (up * west)
        scratch[8 + width : 9 + width] = hcor[2 * k + 1].astype(F32)[0:1] * (up * east)
        put_row(field, pair, side, hrow[k].astype(F32) * up, scratch)
    hcolf[0] = hcol[0].astype(F32) * west
    hcolf[1] = hcol[1].astype(F32) * east
    place = iota((16, 128), 0)

    def body(pair, carry):
        for half, spot, sub, lane in ((0, 0, 0, 0), (1, width - 16, 15, 256)):
            for side in (1, 0):
                at = (
                    pair + 1 - side,
                    pl.ds(spot, 16),
                    pl.ds(side * 384 + lane, 128),
                )
                cell = hcolf[half, pl.ds(2 * pair + 1 - side, 1), :]
                field[at] = jnp.where(place == sub, cell, field[at].astype(F32)).astype(BF)
        return carry

    lax.fori_loop(0, pairs, body, 0)


def take_edges(field, rows, cols, colf):
    pairs = field.shape[0] - 1
    rows[0] = field[0, :, 512:640]
    rows[1] = field[pairs, :, 128:256]
    cols[0] = colf[0].astype(BF)
    cols[1] = colf[1].astype(BF)


def windows(field, at, count):
    width = field.shape[1]
    low = field[pl.ds(at, count)].reshape(count * width, 768)
    high = field[pl.ds(at + 1, count)].reshape(count * width, 768)
    return low, high


def centres(field, at, count):
    width = field.shape[1]
    even = field[pl.ds(at, count), :, 512:640].reshape(count * width, 128)
    odd = field[pl.ds(at + 1, count), :, 128:256].reshape(count * width, 128)
    return even, odd


def pair_weights(kernel, out, flipped):
    out[...] = jnp.zeros_like(out)
    for a in range(3):
        for b in range(3):
            if flipped:
                block = kernel[(2 - a) * 3 + 2 - b].astype(F32).T.astype(BF)
            else:
                block = kernel[a * 3 + b]
            for half in range(2):
                base = (a + half) * 384 + b * 128
                out[base : base + 128, half * 128 : half * 128 + 128] = block


def tap_sums(acc, out):
    for a in range(3):
        for b in range(3):
            total = None
            for half in range(2):
                i = a + half
                lane = (i % 2) * 384 + b * 128
                part = acc[i // 2, half * 128 : half * 128 + 128, lane : lane + 128]
                total = part if total is None else total + part
            t = a * 3 + b
            out[t * 8 : t * 8 + 8] = total.T.astype(BF).reshape(8, 16, 128)


def activate(z):
    sig = 0.5 + 0.5 * jnp.tanh(0.5 * z)
    y = z * sig
    return y, sig + y * (1.0 - sig)


def kernel(counts, *refs):
    nr, nc = counts
    (ids, live, fine_h, interp_h, coarse_h, cw_h, k1_h, k2_h, c1_h, c2_h) = refs[:10]
    (skip_h, gin_h, p1_h, p2_h, gcond_h, gcoarse_h) = refs[10:16]
    (
        fine, interp, coarse, cw, k1, k2, cot1, cot2,
        skip, gin, gcoarse,
        field1, field2, delta1, delta2, slope, back, flip,
        w1, w2, v1, v2, cwp, coarse_t, table, spread, perm, proj, patch,
        acc1, acc2, shift, pool, stage, colf, hcolf,
        ask, asked, askrow, askedrow, reply, arrived, placed, gathered,
        rows1, cols1, hrow1, hcol1, hcor1,
        rows2, cols2, hrow2, hcol2, hcor2,
        rows3, cols3, hrow3, hcol3, hcor3,
        rows4, cols4, hrow4, hcol4, hcor4,
        p1, p1in, p1mid, p1all, p2, p2in, p2mid, p2all,
        q, qin, qmid, qall,
        local_sem, row_send, row_recv, col_send, col_recv, halo_send, halo_recv, back_send, back_recv, core_send, core_recv,
    ) = refs[16:]
    r, c = lax.axis_index("row"), lax.axis_index("col")
    here = (r, c)
    pairs1, width1 = fine.shape[0], fine.shape[2]
    pairs2, width2 = pairs1 // 2, width1 // 2
    listed = ids.shape[1]
    places = nr * SLOT
    ncoarse = coarse.shape[1]
    nblocks = ncoarse // CB

    barrier = pltpu.get_barrier_semaphore()

    def greet(row, col):
        pl.semaphore_signal(barrier, inc=1, device_id=(row, col), device_id_type=MESH)

    for step in range(1, nc):
        greet(r, lax.rem(c + step, nc))
    for step in range(1, nr):
        greet(lax.rem(r + step, nr), c)

    loads = [
        pltpu.make_async_copy(source, target, local_sem.at[k])
        for k, (source, target) in enumerate(
            (
                (cw_h, cw), (coarse_h, coarse), (k1_h, k1), (interp_h, interp),
                (fine_h, fine), (k2_h, k2), (c2_h, cot2), (c1_h, cot1),
            )
        )
    ]
    for load in loads:
        load.start()

    live_total = live[0, 0]
    owner = [lax.shift_right_logical(ids[0, k], jnp.int32(nblocks.bit_length() - 1)) for k in range(listed)]
    local = [ids[0, k] - owner[k] * nblocks for k in range(listed)]
    place = []
    for k in range(listed):
        rank = jnp.int32(0)
        for j in range(k):
            rank = rank + jnp.where(owner[j] == owner[k], 1, 0)
        place.append(jnp.where(k < live_total, owner[k] * CAP + rank, -1))
    row_at = iota((places, 128), 0)
    row_place = lax.shift_right_logical(row_at, 3)
    row_sub = row_at - row_place * CB
    wanted = jnp.full((places, 128), -1, jnp.int32)
    for k in range(listed):
        wanted = jnp.where(row_place == place[k], local[k] * CB + row_sub, wanted)
    ask[...] = wanted.astype(F32).reshape(ask.shape)
    pl.semaphore_wait(barrier, nr - 1 + nc - 1)

    row = lambda k, source, dest: Push(here, 0, nr, source, dest, row_send.at[k], row_recv.at[k])
    col = lambda k, source, dest: Push(here, 1, nc, source, dest, col_send.at[k], col_recv.at[k])
    halo = lambda k, *bufs: Halo(here, counts, *bufs, halo_send.at[k], halo_recv.at[k])
    masks = (
        jnp.where(r > 0, 1.0, 0.0),
        jnp.where(r < nr - 1, 1.0, 0.0),
        jnp.where(c > 0, 1.0, 0.0),
        jnp.where(c < nc - 1, 1.0, 0.0),
    )

    push_ask = row(0, lambda peer: ask.at[peer], asked)
    push_ask.start()
    asked[r] = ask[r]

    list_at = iota((listed * CB, 128), 0)
    list_slot = lax.shift_right_logical(list_at, 3)
    list_sub = list_at - list_slot * CB
    target = jnp.full((listed * CB, 128), -1, jnp.int32)
    for k in range(listed):
        found = jnp.where(place[k] >= 0, place[k] * CB, -CB)
        target = jnp.where(list_slot == k, found + list_sub, target)
    lanes = iota((listed * CB, 128), 1)
    for j in range(places // 128):
        perm[:, j * 128 : j * 128 + 128] = jnp.where(target == lanes + j * 128, 1.0, 0.0).astype(BF)

    loads[0].wait()
    loads[1].wait()
    cwp[...] = jnp.zeros_like(cwp)
    cwp[0 : cw.shape[0], :] = cw[...].astype(F32)
    coarse_t[...] = jnp.zeros_like(coarse_t)
    weight = cwp[...].astype(BF)

    def project(k, carry):
        at = pl.ds(pl.multiple_of(k * 512, 512), 512)
        coarse_t[0 : coarse.shape[0], :] = coarse[:, at].astype(F32)
        part = coarse_t[...].T.astype(BF)
        table[at, 0:128] = dot(part, weight).astype(BF)
        table[at, 128:256] = part
        return carry

    lax.fori_loop(0, ncoarse // 512, project, 0)
    loads[2].wait()
    pair_weights(k1, w1, False)

    loads[5].wait()
    pair_weights(k1, v1, True)
    pair_weights(k2, w2, False)
    pair_weights(k2, v2, True)
    shift[...] = jnp.zeros_like(shift)

    push_ask.wait_recv()
    every = asked[...].reshape(places, 128)
    lane_f = iota((places, 128), 1).astype(F32)

    def gather(k, carry):
        base = (k * 512).astype(F32)
        pieces = [jnp.where(every == lane_f + (base + j * 128.0), 1.0, 0.0).astype(BF) for j in range(4)]
        return carry + dot(
            jnp.concatenate(pieces, axis=1), table[pl.ds(pl.multiple_of(k * 512, 512), 512), :]
        )

    gathered_rows = lax.fori_loop(0, ncoarse // 512, gather, jnp.zeros((places, 256), F32))
    reply[...] = gathered_rows.astype(BF).reshape(reply.shape)
    push_reply = row(1, lambda peer: reply.at[peer], arrived)
    push_reply.start()
    arrived[r] = reply[r]
    askrow[...] = every.T[0:8, :]
    push_row = col(0, lambda peer: askrow, askedrow)
    push_row.start()
    askedrow[c] = askrow[...]

    loads[3].wait()

    def turn(pair, carry):
        at = pl.ds(pl.multiple_of(pair * width1, width1), width1)
        for side in range(2):
            flip[side, :, at] = interp[pair, side].astype(F32).T.astype(BF)
        return carry

    lax.fori_loop(0, pairs1, turn, 0)

    push_reply.wait_recv()
    both = dot(perm[...], arrived[...].reshape(places, 256)).astype(BF)
    proj[...] = both[:, 0:128]
    patch[...] = both[:, 128:256]
    loads[4].wait()

    for half in range(2):
        at = pl.ds(half * (width1 - 16), 16)
        value = dot(interp[:, :, at, :].reshape(pairs1 * 32, 128), proj[...])
        pool[...] = value + fine[:, :, at, :].reshape(pairs1 * 32, 128).astype(F32)
        cols1[half] = pool[pl.ds(15 * half, 2 * pairs1, stride=16), :].astype(BF)
        at = (half * (pairs1 - 1), half)
        rows1[half] = (dot(interp[at], proj[...]) + fine[at].astype(F32)).astype(BF)
    halo1 = halo(0, rows1, cols1, hrow1, hcol1, hcor1)
    halo1.start()

    def condition(k, carry):
        for j in range(4):
            pair = k * 4 + j
            value = dot(interp[pair].reshape(2 * width1, 128), proj[...])
            value = value + fine[pair].reshape(2 * width1, 128).astype(F32)
            for side in range(2):
                line = value[side * width1 : (side + 1) * width1]
                put_row(field1, pair + side, 1 - side, line, shift.at[2 * j + side])
        return carry

    lax.fori_loop(0, pairs1 // 4, condition, 0)
    halo1.wait_recv()
    set_halo(field1, hrow1, hcol1, hcor1, hcolf, masks, shift.at[0])

    middle = width1 - 32
    inner = middle // 2

    def level_one(pair, count, cols):
        lane_rows = [field1[pl.ds(pair + j, count), cols, :].reshape(-1, 768) for j in range(2)]
        y, grade = activate(dot(jnp.concatenate(lane_rows, axis=1), w1[...]))
        cells = y.shape[0]
        slope[pl.ds(pair, count), cols, :] = grade.reshape(count, cells // count, 256)
        pool[0:cells] = y[:, 0:128] + y[:, 128:256]
        total = pool[pl.ds(0, cells // 2, stride=2), :] + pool[pl.ds(1, cells // 2, stride=2), :]
        return total * 0.25

    for half in range(2):
        total = level_one(0, pairs1, pl.ds(half * (width1 - 16), 16))
        pool[0 : pairs1 * 8] = total
        cols2[half] = pool[pl.ds(7 * half, pairs1, stride=8), :].astype(BF)
        stage[1 : pairs1 + 1, 8 + half * (width2 - 8) : 16 + half * (width2 - 8), :] = total.reshape(
            pairs1, 8, 128
        )
    for half in range(2):
        at = half * (pairs1 - 1)
        stage[at + 1, 16 : 16 + inner, :] = level_one(at, 1, pl.ds(16, middle))
        rows2[half] = stage[at + 1, 8 : 8 + width2, :].astype(BF)
    halo2 = halo(1, rows2, cols2, hrow2, hcol2, hcor2)
    halo2.start()
    step1 = (pairs1 - 2) // 3

    def level_one_inner(k, carry):
        pair = 1 + k * step1
        total = level_one(pair, step1, pl.ds(16, middle))
        stage[pl.ds(pair + 1, step1), 16 : 16 + inner, :] = total.reshape(step1, inner, 128)
        return carry

    lax.fori_loop(0, 3, level_one_inner, 0)
    half = pl.ds(0, 2 * pairs2)
    loads[6].wait()
    halo2.wait_recv()
    north, south, west, east = masks
    for k, up in ((0, north), (1, south)):
        at = k * (pairs1 + 1)
        stage[at, 8 : 8 + width2, :] = hrow2[k].astype(F32) * up
        stage[at, 7:8, :] = hcor2[2 * k].astype(F32)[15:16] * (up * west)
        stage[at, 8 + width2 : 9 + width2, :] = hcor2[2 * k + 1].astype(F32)[0:1] * (up * east)
    hcolf[0, half] = hcol2[0].astype(F32) * west
    hcolf[1, half] = hcol2[1].astype(F32) * east

    def edge_cells(k, carry):
        stage[k + 1, 7:8, :] = hcolf[0, pl.ds(k, 1), :]
        stage[k + 1, 8 + width2 : 9 + width2, :] = hcolf[1, pl.ds(k, 1), :]
        return carry

    lax.fori_loop(0, pairs1, edge_cells, 0)

    def lay_out(pair, carry):
        for side in range(2):
            for j in range(3):
                lane = side * 384 + j * 128
                line = stage[2 * pair + side, 7 + j : 7 + j + width2, :]
                field2[pair, :, lane : lane + 128] = line.astype(BF)
        return carry

    lax.fori_loop(0, pairs2 + 1, lay_out, 0)

    def level_two(k, carry):
        pair = k * 8
        z = dot(jnp.concatenate(windows(field2, pair, 8), axis=1), w2[...])
        y, grade = activate(z)
        for side in range(2):
            lane = slice(side * 128, side * 128 + 128)
            skip[pl.ds(pair, 8), side] = y[:, lane].astype(BF).reshape(8, width2, 128)
            value = cot2[pl.ds(pair, 8), side].astype(F32) * grade[:, lane].reshape(8, width2, 128)
            for j in range(8):
                at = pl.ds(2 * (pair + j) + side, 1)
                colf[0, at, :] = value[j, 0:1]
                colf[1, at, :] = value[j, width2 - 1 : width2]
                put_row(delta2, pair + j + side, 1 - side, value[j], shift.at[j])
        return carry

    lax.fori_loop(0, pairs2 // 8, level_two, 0)
    skip_out = pltpu.make_async_copy(skip, skip_h, local_sem.at[8])
    skip_out.start()
    take_edges(delta2, rows3, cols3, colf.at[:, half])
    halo3 = halo(2, rows3, cols3, hrow3, hcol3, hcor3)
    halo3.start()

    def tap_grad(field, delta, acc, step):
        count = step // field.shape[1]

        def body(k, carry):
            outer = jnp.concatenate(centres(delta, k * count, count), axis=1)
            for i, window in enumerate(windows(field, k * count, count)):
                acc[i] += lax.dot_general(outer, window, CONTRACT0, preferred_element_type=F32)
            return carry

        acc[...] = jnp.zeros_like(acc)
        lax.fori_loop(0, (field.shape[0] - 1) // count, body, 0)

    push_row.wait_recv()

    def spot(k, carry):
        at = pl.ds(pl.multiple_of(k * 256, 256), 256)
        number = iota((256, places), 0).astype(F32) + (k * 256).astype(F32)
        for j in range(nc):
            match = number == askedrow[j, 0:1, :]
            spread[j, at, :] = jnp.where(match, 1.0, 0.0).astype(BF)
        return carry

    lax.fori_loop(0, ncoarse // 256, spot, 0)

    tap_grad(field2, delta2, acc2, 1024)
    tap_sums(acc2, p2)

    class Total:
        def __init__(self, outer, inner, numbers, parts, held, middle, full):
            (push, self.me, self.count), (cross, self.other, self.others) = outer, inner
            self.parts, self.held, self.middle, self.full = parts, held, middle, full
            self.size = parts.shape[0] // self.count
            block = lambda peer: parts.at[pl.ds(peer * self.size, self.size)]
            self.first = push(numbers[0], block, held)
            self.second = cross(numbers[1], lambda peer: middle.at[self.other], middle)
            self.third = push(numbers[2], lambda peer: full.at[self.me], full)

        def scatter(self):
            self.first.start()
            self.held[self.me] = self.parts[pl.ds(self.me * self.size, self.size)]

        def exchange(self):
            self.first.wait_recv()
            total = self.held[0].astype(F32)
            for k in range(1, self.count):
                total = total + self.held[k].astype(F32)
            self.middle[self.other] = total.astype(self.middle.dtype)
            self.second.start()

        def gather(self):
            self.second.wait_recv()
            total = self.middle[0].astype(F32)
            for k in range(1, self.others):
                total = total + self.middle[k].astype(F32)
            self.full[self.me] = total.astype(self.full.dtype)
            self.third.start()

        def finish(self):
            self.third.wait_recv()

        def wait_send(self):
            self.first.wait_send()
            self.second.wait_send()
            self.third.wait_send()

    over_row, over_col = (row, r, nr), (col, c, nc)
    sum2 = Total(over_row, over_col, (2, 1, 3), p2, p2in, p2mid, p2all)
    sum1 = Total(over_row, over_col, (4, 3, 5), p1, p1in, p1mid, p1all)
    sumq = Total(over_col, over_row, (5, 6, 6), q, qin, qmid, qall)
    sum2.scatter()

    halo3.wait_recv()
    set_halo(delta2, hrow3, hcol3, hcor3, hcolf.at[:, half], masks, shift.at[0])

    def back_two(k, carry):
        z = dot(jnp.concatenate(windows(delta2, k * 8, 8), axis=1), v2[...]) * 0.25
        back[pl.ds(k * 8, 8)] = z.reshape(8, width2, 256)
        return carry

    lax.fori_loop(0, pairs2 // 8, back_two, 0)
    loads[7].wait()

    def delta_one(k, carry):
        for j in range(2):
            pair = k * 2 + j
            line = back[k, :, j * 128 : j * 128 + 128]
            base = j * width1
            pool[pl.ds(base, width2, stride=2), :] = line
            pool[pl.ds(base + 1, width2, stride=2), :] = line
            wide = pool[base : base + width1]
            for side in range(2):
                grade = slope[pair, :, side * 128 : side * 128 + 128]
                value = (cot1[pair, side].astype(F32) + wide) * grade
                at = pl.ds(2 * pair + side, 1)
                colf[0, at, :] = value[0:1]
                colf[1, at, :] = value[width1 - 1 : width1]
                put_row(delta1, pair + side, 1 - side, value, shift.at[2 * j + side])
        return carry

    lax.fori_loop(0, pairs1 // 2, delta_one, 0)
    take_edges(delta1, rows4, cols4, colf)
    halo4 = halo(3, rows4, cols4, hrow4, hcol4, hcor4)
    halo4.start()
    sum2.exchange()
    tap_grad(field1, delta1, acc1, 2048)
    tap_sums(acc1, p1)
    sum1.scatter()
    sum2.gather()
    halo4.wait_recv()
    set_halo(delta1, hrow4, hcol4, hcor4, hcolf, masks, shift.at[0])

    def input_grad(k, carry):
        z = dot(jnp.concatenate(windows(delta1, k * 16, 16), axis=1), v1[...]).astype(BF)
        for side in range(2):
            gin[pl.ds(k * 16, 16), side] = z[:, side * 128 : side * 128 + 128].reshape(16, width1, 128)
        return carry

    lax.fori_loop(0, pairs1 // 16, input_grad, 0)

    def list_grad(k, carry):
        at = pl.ds(pl.multiple_of(k * 8 * width1, 8 * width1), 8 * width1)
        for side in range(2):
            part = gin[pl.ds(k * 8, 8), side].reshape(8 * width1, 128)
            carry = carry + dot(flip[side, :, at], part)
        return carry

    gpacc = lax.fori_loop(0, pairs1 // 8, list_grad, jnp.zeros((128, 128), F32))
    gin_out = pltpu.make_async_copy(gin, gin_h, local_sem.at[9])
    gin_out.start()

    gproj = gpacc.astype(BF)
    q[...] = lax.dot_general(patch[...], gproj, CONTRACT0, preferred_element_type=F32).reshape(q.shape)
    sumq.scatter()
    gpatch = lax.dot_general(gproj, weight, CONTRACT1, preferred_element_type=F32).astype(BF)
    moved = lax.dot_general(perm[...], gpatch, CONTRACT0, preferred_element_type=F32)
    placed[...] = moved.astype(BF).reshape(placed.shape)
    push_back = Back(
        here, counts, placed, gathered, back_send, back_recv, core_send, core_recv
    )
    push_back.start()
    gathered[c, r] = placed[r]
    sum1.exchange()
    sum2.finish()
    p2_out = pltpu.make_async_copy(p2all, p2_h, local_sem.at[10])
    p2_out.start()
    sumq.exchange()
    push_back.forward()
    sum1.gather()
    started = []

    def scatter(slots):
        if not slots:
            return
        parts = jnp.concatenate([gathered[slot].reshape(places, 128) for slot in slots], axis=0)
        first = not started
        started.append(slots)

        def body(k, carry):
            at = pl.ds(pl.multiple_of(k * 1024, 1024), 1024)
            value = dot(jnp.concatenate([spread[slot, at, :] for slot in slots], axis=1), parts)
            gcoarse[at, :] = value if first else gcoarse[at, :] + value
            return carry

        lax.fori_loop(0, ncoarse // 1024, body, 0)

    scatter(push_back.slots(push_back.core))
    sumq.gather()
    push_back.wait_across()
    scatter(push_back.slots(1 - push_back.core))
    gcoarse_out = pltpu.make_async_copy(gcoarse, gcoarse_h, local_sem.at[11])
    gcoarse_out.start()
    sum1.finish()
    p1_out = pltpu.make_async_copy(p1all, p1_h, local_sem.at[12])
    p1_out.start()
    sumq.finish()
    gcond_out = pltpu.make_async_copy(qall, gcond_h, local_sem.at[13])
    gcond_out.start()

    for sent in (
        push_ask, push_reply, push_row, halo1, halo2, halo3, halo4, sum2, sum1, push_back,
        sumq,
    ):
        sent.wait_send()
    for out in (skip_out, gin_out, p2_out, gcoarse_out, p1_out, gcond_out):
        out.wait()


def finish_kernel(skip_k, gin_k, p1_k, p2_k, gcond_k, gcoarse_k, *refs):
    skip_h, gin_h, g1_h, g2_h, gcond_h, gcoarse_h = refs[:6]
    skip, gin, p1, p2, qs, held, g1, g2, gcond, gcoarse, sem = refs[6:]
    quarter = gin.shape[0] // 4
    parts = [pl.ds(k * quarter, quarter) for k in range(4)]
    loads = [
        pltpu.make_async_copy(source, target, sem.at[k])
        for k, (source, target) in enumerate(
            (
                (gcoarse_k, held), *((gin_k.at[part], gin.at[part]) for part in parts),
                (skip_k, skip), (p2_k, p2), (p1_k, p1), (gcond_k, qs),
            )
        )
    ]
    for load in loads:
        load.start()
    outs = []

    def store(source, target):
        copy = pltpu.make_async_copy(source, target, sem.at[16 + len(outs)])
        copy.start()
        outs.append(copy)

    loads[0].wait()
    pieces = held.shape[0] // 4
    for j, part in enumerate(parts):
        loads[1 + j].wait()
        store(gin.at[part], gin_h.at[part])
        for k in range(pieces // 128):
            at = slice(j * pieces + k * 128, j * pieces + k * 128 + 128)
            gcoarse[:, at] = held[at, :].T[0 : gcoarse.shape[0], :]
    store(gcoarse, gcoarse_h)
    loads[5].wait()
    store(skip, skip_h)
    loads[6].wait()
    g2[...] = p2[0 : g2.shape[0]].astype(F32)
    store(g2, g2_h)
    loads[7].wait()
    g1[...] = p1[0 : g1.shape[0]].astype(F32)
    store(g1, g1_h)
    loads[8].wait()
    gcond[...] = qs[0 : gcond.shape[0], :]
    store(gcond, gcond_h)
    for out in outs:
        out.wait()


def per_device(counts, fine, interp, ids, live, coarse, cw, conv_one, conv_two, cot_one, cot_two):
    nr, nc = counts
    height, width, channels = fine.shape
    pairs1, pairs2, width2 = height // 2, height // 4, width // 2
    cch, ncoarse = coarse.shape[1], coarse.shape[0]
    listed = ids.shape[-1]
    places = nr * SLOT
    blocks = -(-72 // nr) * nr
    any_space = pl.BlockSpec(memory_space=pl.ANY)
    smem = pl.BlockSpec(memory_space=pltpu.SMEM)
    vm = pltpu.VMEM
    chunk = blocks // nr

    def halo_bufs(rows, cols):
        return [
            vm((2, cols, 128), BF), vm((2, rows, 128), BF),
            vm((2, cols, 128), BF), vm((2, rows, 128), BF), vm((4, 16, 128), BF),
        ]

    def sum_bufs():
        return [
            vm((blocks, 16, 128), BF), vm((nr, chunk, 16, 128), BF), vm((nc, chunk, 16, 128), BF),
            vm((nr, chunk, 16, 128), BF),
        ]

    scratch = [
        vm((pairs1, 2, width, 128), BF), vm((pairs1, 2, width, 128), BF), vm((cch, ncoarse), BF),
        vm(cw.shape, BF), vm((9, 128, 128), BF), vm((9, 128, 128), BF),
        vm((pairs1, 2, width, 128), BF), vm((pairs2, 2, width2, 128), BF),
        vm((pairs2, 2, width2, 128), BF), vm((pairs1, 2, width, 128), BF),
        vm((ncoarse, 128), F32),
        vm((pairs1 + 1, width, 768), BF), vm((pairs2 + 1, width2, 768), BF),
        vm((pairs1 + 1, width, 768), BF), vm((pairs2 + 1, width2, 768), BF),
        vm((pairs1, width, 256), F32), vm((pairs2, width2, 256), F32), vm((2, 128, pairs1 * width), BF),
        vm((1536, 256), BF), vm((1536, 256), BF), vm((1536, 256), BF), vm((1536, 256), BF),
        vm((128, 128), F32), vm((128, 512), F32), vm((ncoarse, 256), BF),
        vm((nc, ncoarse, places), BF),
        vm((listed * CB, places), BF), vm((listed * CB, 128), BF), vm((listed * CB, 128), BF),
        vm((2, 256, 768), F32), vm((2, 256, 768), F32),
        vm((8, width + 16, 128), F32), vm((8 * width, 128), F32), vm((pairs1 + 2, width2 + 16, 128), F32),
        vm((2, height, 128), F32), vm((2, height, 128), F32),
        vm((nr, SLOT, 128), F32), vm((nr, SLOT, 128), F32), vm((8, places), F32), vm((nc, 8, places), F32),
        vm((nr, SLOT, 256), BF), vm((nr, SLOT, 256), BF),
        vm((nr, SLOT, 128), BF), vm((nc, nr, SLOT, 128), BF),
        *halo_bufs(height, width), *halo_bufs(height // 2, width2),
        *halo_bufs(height // 2, width2), *halo_bufs(height, width),
        *sum_bufs(), *sum_bufs(),
        vm((nc, 128 // nc, 128), F32), vm((nc, 1, 128 // nc, 128), F32), vm((nr, 1, 128 // nc, 128), F32),
        vm((nc, 1, 128 // nc, 128), F32),
        pltpu.SemaphoreType.DMA((16,)),
        pltpu.SemaphoreType.DMA((8,)), pltpu.SemaphoreType.DMA((8,)),
        pltpu.SemaphoreType.DMA((7,)), pltpu.SemaphoreType.DMA((7,)),
        pltpu.SemaphoreType.DMA((4, 3)), pltpu.SemaphoreType.DMA((4, 3)),
        *[pltpu.SemaphoreType.DMA((nc // 2,))] * 4,
    ]
    shape = jax.ShapeDtypeStruct
    results = pl.pallas_call(
        functools.partial(kernel, counts),
        out_shape=(
            shape((pairs2, 2, width2, 128), BF),
            shape((pairs1, 2, width, 128), BF),
            shape((nr, chunk, 16, 128), BF),
            shape((nr, chunk, 16, 128), BF),
            shape((nc, 1, 128 // nc, 128), F32),
            shape((ncoarse, 128), F32),
        ),
        in_specs=[smem, smem] + [any_space] * 8,
        out_specs=(any_space,) * 6,
        scratch_shapes=scratch,
        compiler_params=pltpu.CompilerParams(
            collective_id=0, has_side_effects=True, vmem_limit_bytes=63 * 2**20
        ),
        cost_estimate=pl.CostEstimate(
            flops=10 * 10**9, bytes_accessed=13 * 10**6, transcendentals=2 * 10**6
        ),
    )(
        ids.reshape(1, listed),
        live.reshape(1, 1),
        fine.reshape(pairs1, 2, width, channels),
        interp.reshape(pairs1, 2, width, interp.shape[2]),
        coarse.T,
        cw,
        conv_one.reshape(9, 128, 128),
        conv_two.reshape(9, 128, 128),
        cot_one.reshape(pairs1, 2, width, channels),
        cot_two.reshape(pairs2, 2, width2, channels),
    )
    skip, gin, g1, g2, gcond, gcoarse = pl.pallas_call(
        finish_kernel,
        out_shape=(
            shape((pairs2, 2, width2, 128), BF),
            shape((pairs1, 2, width, 128), BF),
            shape((72, 16, 128), F32),
            shape((72, 16, 128), F32),
            shape((cch, 128), F32),
            shape((cch, ncoarse), F32),
        ),
        in_specs=[any_space] * 6,
        out_specs=(any_space,) * 6,
        scratch_shapes=[
            vm((pairs2, 2, width2, 128), BF), vm((pairs1, 2, width, 128), BF),
            vm((blocks, 16, 128), BF), vm((blocks, 16, 128), BF), vm((128, 128), F32), vm((ncoarse, 128), F32),
            vm((72, 16, 128), F32), vm((72, 16, 128), F32), vm((cch, 128), F32), vm((cch, ncoarse), F32),
            pltpu.SemaphoreType.DMA((32,)),
        ],
        compiler_params=pltpu.CompilerParams(vmem_limit_bytes=63 * 2**20),
        cost_estimate=pl.CostEstimate(flops=0, bytes_accessed=12 * 10**6, transcendentals=0),
    )(
        results[0],
        results[1],
        results[2].reshape(blocks, 16, 128),
        results[3].reshape(blocks, 16, 128),
        results[4].reshape(128, 128),
        results[5],
    )
    return (
        skip.reshape(height // 2, width2, 128),
        gin.reshape(height, width, 128),
        g1.reshape(3, 3, 128, 128),
        g2.reshape(3, 3, 128, 128),
        gcond,
        gcoarse.T,
    )


def solution(mesh):
    counts = (mesh.shape["row"], mesh.shape["col"])
    tiles = P("row", "col", None)
    return jax.shard_map(
        functools.partial(per_device, counts),
        mesh=mesh,
        in_specs=(tiles, tiles, tiles, P("row", "col"), P("row", None), P(), P(), P(), tiles, tiles),
        out_specs=(tiles, tiles, P(), P(), P(), P("row", None)),
        check_vma=False,
    )
```
